128 devices in a mesh: lat: 8 (over x_lo, y), lon: 16 (over x_hi, z, core).
Axes of the slice: x: 4 (x_hi: 2, x_lo: 2; x = x_hi * 2 + x_lo), y: 4, z: 4, core: 2. Of those that a mesh axis runs over, the one named last changes fastest.
Arguments:
- grid_rows: bfloat16 [65536, 512], P(('lat', 'lon')), may hold values from -6 to 6
- dest_owner: int32 [65536, 1], P(('lat', 'lon')), may hold values from 0 to 127; in each aligned block of 512 rows (0 to 511, 512 to 1023, ...) at most 8 rows name the same one
- dest_node: int32 [65536], P(('lat', 'lon')), may hold values from 0 to 127
- node_embed: bfloat16 [16384, 512], P(('lat', 'lon')), may hold values from -6 to 6
- neighbours: int32 [128, 16], P(('lat', 'lon')), may hold values from 0 to 127, as said below
- norm_gain: float32 [512], replicated, may hold values from 0.5 to 1.5
- w_qkv: bfloat16 [512, 1536], replicated, may hold values from -4 to 4
- w_out: bfloat16 [512, 512], replicated, may hold values from -0.25 to 0.25
- cotangent: bfloat16 [16384, 512], P(('lat', 'lon')), may hold values from -6 to 6
Outputs:
- mixed: bfloat16 [16384, 512], P(('lat', 'lon'))
- grad_grid: bfloat16 [65536, 512], P(('lat', 'lon'))
- grad_w_qkv: float32 [512, 1536], replicated
- grad_w_out: float32 [512, 512], replicated
- grad_gain: float32 [512], replicated
The draws below stay inside these ranges and needn't reach their ends.
Inputs may be any that keep to these rules, and one draw needn't show every extreme that they name: dest_owner names a partition (lat index times 16 plus lon index); the 512 rows of one tile name one partition at most 8 times. `neighbours`: block g lies on partition g. Entry 0 of row b is b itself; every listed block lies on b's partition or on one whose lat index differs by at most 1 and whose lon index differs by at most 1 cyclically over 16. Entries may repeat.
All inputs are finite; a program needn't handle non-finite values.
Results may differ from the reference program's by a relative error of at most 0.017.
Values may be sent and summed in bfloat16 or wider, within the bound.
A program may use at most 128 MiB of HBM per device.

```python
import math
import jax
import jax.numpy as jnp
import numpy as np
from jax import lax

D = 512
HEADS = 16
HD = 32
BLK = 128
KB = 16
NB_DEV = 1
G_DEV = 512
M_DEV = 128
LAT_PARTS = 8
LON_PARTS = 16
MESH_BLOCKS = 128
MESH = 16384
GRID = 65536
CAP = 8
N_LAT = 8
N_LON = 16


def draw_neighbours(key, part):
    key = jax.random.fold_in(key, 11)
    lat_key, lon_key, block_key = jax.random.split(key, 3)
    blocks = jnp.arange(MESH_BLOCKS, dtype=jnp.int32)
    partition = blocks // NB_DEV
    lat_index = partition // LON_PARTS
    lon_index = partition % LON_PARTS
    lat_step = jax.random.randint(lat_key, (MESH_BLOCKS, KB), -1, 2)
    lon_step = jax.random.randint(lon_key, (MESH_BLOCKS, KB), -1, 2)
    local_block = jax.random.randint(block_key, (MESH_BLOCKS, KB), 0, NB_DEV)
    near_lat = jnp.clip(lat_index[:, None] + lat_step, 0, LAT_PARTS - 1)
    near_lon = (lon_index[:, None] + lon_step + LON_PARTS) % LON_PARTS
    listed = (near_lat * LON_PARTS + near_lon) * NB_DEV + local_block
    listed = listed.at[:, 0].set(blocks)
    return listed.astype(jnp.int32)


def draw_w_qkv(key, part):
    key = jax.random.fold_in(key, 23)
    base = jax.random.normal(key, (D, 3 * D), jnp.float32) * D ** (-0.5)
    return jnp.clip(base, -4.0, 4.0).astype(jnp.bfloat16)


def set_ends(entries, key, low, largest):
    longest = entries.shape.index(max(entries.shape))
    spots = []
    for shift in (0, 1):
        where = [jax.random.randint(jax.random.fold_in(key, axis), (), 0, length) for axis, length in enumerate(entries.shape)]
        where[longest] = (where[longest] + shift) % entries.shape[longest]
        spots.append(tuple(where))
    return entries.at[spots[0]].set(low).at[spots[1]].set(largest)


def block_scale(stream_key, shape, shards, smallest, high):
    def one(axis_at, shards_of):
        steps = jax.random.uniform(jax.random.fold_in(jax.random.fold_in(stream_key, 6), axis_at), (shards_of,), jnp.float32, smallest / len(shards), high / len(shards))
        return jnp.repeat(jnp.exp(steps), shape[axis_at] // shards_of).reshape((-1,) + (1,) * (len(shape) - axis_at - 1))

    level = one(*shards[0])
    for cut in shards[1:]:
        level = level * one(*cut)
    return level


def assign_block(key, own, number, rows, number_of, top, reach, slope):
    ranking = jax.random.permutation(key, number_of)
    packed, common = load_shares(number_of, rows * top, reach, slope, True), load_shares(number_of, rows * top, reach, slope, False)
    places = jnp.arange(number_of)

    def named(tallies, turn):
        used = int((tallies > 0).sum())
        fixed = max(1, used // 4)
        shifted = fixed + (places - fixed + turn * (used - fixed)) % max(1, number_of - fixed)
        return jnp.zeros((number_of,), jnp.int32).at[ranking[jnp.where(places < fixed, places, shifted)]].set(jnp.asarray(tallies, jnp.int32))

    tallies = jnp.where(number % 4 == 0, named(packed, number // 4), named(common, number - number // 4 - 1))
    mixed = jax.random.permutation(jax.random.fold_in(own, 3), number_of)
    donor, sink = mixed[0:number_of // 2 * 2:2], mixed[1:number_of // 2 * 2:2]
    slack = jnp.minimum(tallies[donor] - 1, reach - tallies[sink]) // 2
    slack = jnp.where((donor == ranking[0]) | (sink == ranking[0]) | (tallies[sink] == 0), 0, jnp.maximum(slack, 0))
    shifted = jax.random.randint(jax.random.fold_in(own, 4), (number_of // 2,), 0, 1 << 20) % (slack + 1)
    tallies = tallies.at[donor].add(-shifted).at[sink].add(shifted)
    labels = jnp.searchsorted(jnp.cumsum(tallies), jnp.arange(rows * top), side="right").astype(jnp.int32)
    listing = labels.reshape(top, rows).T
    listing = listing[jax.random.permutation(jax.random.fold_in(own, 1), rows)]
    turn = jax.random.randint(jax.random.fold_in(own, 2), (rows, 1), 0, top)
    return jnp.take_along_axis(listing, (jnp.arange(top)[None, :] + turn) % top, axis=1)


def load_shares(number_of, total, limit, lean, full):
    portions = [(1 << 20) // math.isqrt(grade ** lean) + 1 for grade in range(1, number_of + 1)]
    largest = limit if full else min(limit, max(-(-total // number_of), total * portions[0] // sum(portions)))
    least = 1 if total - largest >= number_of - 1 else 0
    holding, rest = [largest] + [least] * (number_of - 1), total - largest - least * (number_of - 1)
    while rest > 0:
        candidates = [i for i in range(1, number_of) if holding[i] < largest] or [i for i in range(1, number_of) if holding[i] < limit]
        whole, budget = sum([portions[i] for i in candidates]), rest
        for i in candidates:
            extra = min(limit - holding[i], max(1, budget * portions[i] // whole), rest)
            holding[i] = holding[i] + extra
            rest = rest - extra
    return np.array(holding)


def normal_values(key, extent, deviation, most, shards=(), kind=jnp.bfloat16):
    drawn = deviation * jax.random.normal(key, extent, jnp.float32)
    if shards:
        drawn = drawn * block_scale(key, extent, shards, -0.22, 0.18)
    return jnp.clip(drawn, -most, most).astype(kind)


def setup_inputs(seed: int = 0) -> dict:
    arg_keys = jax.random.split(jax.random.key(seed), 10)
    grid_rows = normal_values(arg_keys[0], (GRID, D), 1.0, 6.0, ((0, 128),))
    dest_owner_keys = jax.random.split(jax.random.fold_in(arg_keys[1], 1), GRID // G_DEV)
    dest_owner_turns = jax.random.permutation(jax.random.fold_in(arg_keys[1], 3), GRID // G_DEV)
    dest_owner = jax.vmap(lambda own, number: assign_block(jax.random.fold_in(arg_keys[1], 2), own, number, G_DEV, N_LAT * N_LON, 1, CAP, 2))(dest_owner_keys, dest_owner_turns).reshape((GRID, 1))
    dest_node = set_ends(jax.random.randint(arg_keys[2], (GRID,), 0, M_DEV), jax.random.fold_in(arg_keys[2], 1), 0, M_DEV - 1).astype(jnp.int32)
    node_embed = normal_values(arg_keys[3], (MESH, D), 1.0, 6.0, ((0, 128),))
    neighbours = draw_neighbours(jax.random.fold_in(arg_keys[9], 71), 0)
    norm_gain = jnp.clip(1.0 + 0.1 * jax.random.normal(arg_keys[5], (D,), jnp.float32), 0.5, 1.5)
    w_qkv = draw_w_qkv(jax.random.fold_in(arg_keys[9], 71), 0)
    w_out = normal_values(arg_keys[7], (D, D), D ** -0.5, 0.25)
    cotangent = normal_values(arg_keys[8], (MESH, D), 1.0, 6.0, ((0, 128),))
    return dict(grid_rows=grid_rows, dest_owner=dest_owner, dest_node=dest_node, node_embed=node_embed, neighbours=neighbours, norm_gain=norm_gain, w_qkv=w_qkv, w_out=w_out, cotangent=cotangent)


EPS = 1e-05

def attend_block(query_block, keyval_block):
    keys = keyval_block[:, :D].reshape(-1, HEADS, HD)
    values = keyval_block[:, D:].reshape(-1, HEADS, HD)
    scores = jnp.einsum('qhd,khd->hqk', query_block.astype(jnp.float32), keys.astype(jnp.float32)) * HD ** (-0.5)
    highest = lax.optimization_barrier(jnp.max(scores, -1, keepdims=True))
    weights = jnp.exp(scores - highest)
    probs = weights / lax.optimization_barrier(jnp.sum(weights, -1, keepdims=True))
    probs_low = probs.astype(jnp.bfloat16)
    mixed_heads = jnp.einsum('hqk,khd->qhd', probs_low.astype(jnp.float32), values.astype(jnp.float32))
    attended = mixed_heads.reshape(BLK, D).astype(jnp.bfloat16)
    return (attended, probs, probs_low, keys, values)

def reference(grid_rows, dest_owner, dest_node, node_embed, neighbours, norm_gain, w_qkv, w_out, cotangent):
    target = (dest_owner[:, 0] * M_DEV + dest_node).astype(jnp.int32)
    counts = jax.ops.segment_sum(jnp.ones(target.shape, jnp.float32), target, num_segments=MESH)
    totals = jax.ops.segment_sum(grid_rows.astype(jnp.float32), target, num_segments=MESH)
    divisor = jnp.maximum(counts, 1.0)[:, None]
    latent = node_embed.astype(jnp.float32) + totals / divisor
    mean_value = lax.optimization_barrier(jnp.mean(latent, -1, keepdims=True))
    centered = latent - mean_value
    inverse_std = lax.rsqrt(lax.optimization_barrier(jnp.mean(centered * centered, -1, keepdims=True)) + EPS)
    normalized = centered * inverse_std
    normed = (normalized * norm_gain).astype(jnp.bfloat16)
    qkv = jnp.dot(normed, w_qkv, preferred_element_type=jnp.float32).astype(jnp.bfloat16)
    queries = qkv[:, :D].reshape(MESH_BLOCKS, BLK, HEADS, HD)
    keyvals = qkv[:, D:].reshape(MESH_BLOCKS, BLK, 2 * D)

    def forward_block(carried):
        query_block, listed = carried
        return attend_block(query_block, keyvals[listed].reshape(-1, 2 * D))[0]
    attended = lax.map(forward_block, (queries, neighbours)).reshape(MESH, D)
    projected = jnp.dot(attended, w_out, preferred_element_type=jnp.float32)
    mixed = (latent + projected).astype(jnp.bfloat16)
    grad_w_out = jnp.dot(attended.T, cotangent, preferred_element_type=jnp.float32)
    d_attended = jnp.dot(cotangent, w_out.T, preferred_element_type=jnp.float32).astype(jnp.bfloat16)
    d_blocks = d_attended.reshape(MESH_BLOCKS, BLK, HEADS, HD)
    scale = HD ** (-0.5)

    def backward_block(grads_kv, carried):
        query_block, listed, d_block = carried
        unused, probs, probs_low, keys, values = attend_block(query_block, keyvals[listed].reshape(-1, 2 * D))
        d_probs = jnp.einsum('qhd,khd->hqk', d_block.astype(jnp.float32), values.astype(jnp.float32))
        d_scores = (probs * (d_probs - lax.optimization_barrier(jnp.sum(probs * d_probs, -1, keepdims=True)))).astype(jnp.bfloat16)
        d_query = jnp.einsum('hqk,khd->qhd', d_scores.astype(jnp.float32), keys.astype(jnp.float32)) * scale
        d_keys = jnp.einsum('hqk,qhd->khd', d_scores.astype(jnp.float32), query_block.astype(jnp.float32)) * scale
        d_values = jnp.einsum('hqk,qhd->khd', probs_low.astype(jnp.float32), d_block.astype(jnp.float32))
        both = jnp.concatenate([d_keys.reshape(KB, BLK, D), d_values.reshape(KB, BLK, D)], -1)
        grads_kv = grads_kv.at[listed].add(both)
        return (grads_kv, d_query.reshape(BLK, D))
    grads_kv, d_queries = lax.scan(backward_block, jnp.zeros((MESH_BLOCKS, BLK, 2 * D), jnp.float32), (queries, neighbours, d_blocks))
    d_qkv = jnp.concatenate([d_queries.reshape(MESH, D), grads_kv.reshape(MESH, 2 * D)], 1).astype(jnp.bfloat16)
    grad_w_qkv = jnp.dot(normed.T, d_qkv, preferred_element_type=jnp.float32)
    d_normed = jnp.dot(d_qkv, w_qkv.T, preferred_element_type=jnp.float32)
    grad_gain = lax.optimization_barrier(jnp.sum(d_normed * normalized, 0))
    scaled = d_normed * norm_gain
    d_latent = cotangent.astype(jnp.float32) + inverse_std * (scaled - lax.optimization_barrier(jnp.mean(scaled, -1, keepdims=True)) - normalized * lax.optimization_barrier(jnp.mean(scaled * normalized, -1, keepdims=True)))
    node_grad = (d_latent / divisor).astype(jnp.bfloat16)
    grad_grid = node_grad[target]
    return (mixed, grad_grid, grad_w_qkv, grad_w_out, grad_gain)
```

```python
import functools
import math

import jax
import jax.numpy as jnp
from jax import lax
from jax.experimental import pallas as pl
from jax.experimental.pallas import tpu as pltpu
from jax.sharding import PartitionSpec as P

HEADS = 16
HEAD_SIZE = 32
BLOCK = 128
LANES = 128
LAT = 8
LON = 16
DEVICES = LAT * LON
OWN = 4
CAP = 8
EPS = 1e-05
VMEM_LIMIT = 56 * 1024 * 1024
MESH = pl.DeviceIdType.MESH


def dot_rows(a, b):
    return lax.dot_general(a, b, (((0,), (0,)), ((), ())), preferred_element_type=jnp.float32)


def dot_cols(a, b):
    return lax.dot_general(a, b, (((1,), (1,)), ((), ())), preferred_element_type=jnp.float32)


def here():
    return lax.axis_index("lat"), lax.axis_index("lon")


def greet_all(me):
    barrier = pltpu.get_barrier_semaphore()

    def greet(step, carry):
        other = (me + step) % DEVICES
        pl.semaphore_signal(
            barrier, inc=1, device_id=(other // LON, other % LON), device_id_type=MESH
        )
        return carry

    lax.fori_loop(1, DEVICES, greet, 0)
    return barrier


def await_bytes(ref, sem):
    pltpu.make_async_copy(ref, ref, sem).wait()


def send_to(src, dst, send_sem, recv_sem, lat, lon):
    pltpu.make_async_remote_copy(
        src_ref=src,
        dst_ref=dst,
        send_sem=send_sem,
        recv_sem=recv_sem,
        device_id=(lat, lon),
        device_id_type=MESH,
    ).start()


def tile_rows(index, rows):
    return pl.ds(pl.multiple_of(index * rows, rows), rows)


def iota(shape, dim):
    return lax.broadcasted_iota(jnp.int32, shape, dim)


def route_kernel(
    grid_ref, owner_ref, node_ref, embed_ref, gain_ref,
    halo_ref, latent_ref, divisor_ref, spread_ref, flat_ref,
    send, recv, ids_send, ids_recv,
    send_sem, recv_sem, ids_send_sem, ids_recv_sem, halo_send_sem, halo_recv_sem,
):
    f32, bf16 = jnp.float32, jnp.bfloat16
    lat, lon = here()
    me = lat * LON + lon
    barrier = greet_all(me)
    count, width = grid_ref.shape
    nodes = embed_ref.shape[0]
    half = width // 2
    slots = DEVICES * CAP

    owner = owner_ref[...]
    picked = (owner == iota((count, DEVICES), 1)).astype(f32)
    earlier = (iota((count, count), 0) > iota((count, count), 1)).astype(f32).astype(bf16)
    ranks = jnp.dot(earlier, picked.astype(bf16), preferred_element_type=f32)
    slot = jnp.sum(picked * ranks, axis=1, keepdims=True).astype(jnp.int32)
    flat = jnp.broadcast_to(owner * CAP + slot, (count, LANES))
    flat_ref[...] = flat
    flat_row = flat.astype(f32).T[0:1, :].astype(jnp.int32)
    named = (iota((DEVICES, count), 0) == (flat_row >> 3)).astype(f32)
    named = (named * (node_ref[...] + 1).astype(f32)).astype(bf16)
    at_slot = (slot == iota((count, LANES), 1)).astype(f32).astype(bf16)
    ids_send[:, 0, :] = jnp.dot(named, at_slot, preferred_element_type=f32)

    grid = grid_ref[...]
    for k in range(slots // 128):
        chosen = (iota((128, count), 0) + k * 128 == flat_row).astype(f32).astype(bf16)
        block = jnp.dot(chosen, grid, preferred_element_type=f32).reshape(16, CAP, width)
        block = jnp.concatenate([block[:, :, :half], block[:, :, half:]], axis=1)
        send[k * 256:(k + 1) * 256, :] = block.reshape(256, half).astype(bf16)

    pl.semaphore_wait(barrier, DEVICES - 1)

    def push(step, carry):
        other = (me + step) % DEVICES
        send_to(ids_send.at[other], ids_recv.at[me], ids_send_sem, ids_recv_sem, other // LON, other % LON)
        send_to(
            send.at[tile_rows(other, 2 * CAP)], recv.at[tile_rows(me, 2 * CAP)],
            send_sem, recv_sem, other // LON, other % LON,
        )
        return carry

    lax.fori_loop(1, DEVICES, push, 0)
    pltpu.make_async_copy(ids_send.at[me], ids_recv.at[me], ids_recv_sem).start()
    pltpu.make_async_copy(
        send.at[tile_rows(me, 2 * CAP)], recv.at[tile_rows(me, 2 * CAP)], recv_sem
    ).start()

    await_bytes(ids_recv, ids_recv_sem)
    ids = ids_recv[:, 0, :]
    lanes = 2 * slots
    source = (iota((DEVICES, lanes), 0) == (iota((DEVICES, lanes), 1) >> 4)).astype(f32).astype(bf16)
    codes = jnp.dot(ids.T[:CAP, :].astype(bf16), source, preferred_element_type=f32)
    mine = (iota((CAP, lanes), 1) & 7) == iota((CAP, lanes), 0)
    code = jnp.sum(jnp.where(mine, codes, 0.0), axis=0, keepdims=True).astype(jnp.int32)
    which = (iota((1, lanes), 1) >> 3) & 1
    code = jnp.where(code > 0, code - 1 + nodes * which, -1)
    members = (iota((2 * nodes, lanes), 0) == code).astype(f32)
    counts = jnp.sum(members[:nodes, :], axis=1, keepdims=True)
    divisor = jnp.maximum(counts, 1.0)
    divisor_ref[...] = jnp.broadcast_to(divisor, (nodes, LANES))
    members = members.astype(bf16)

    await_bytes(recv, recv_sem)
    sums = jnp.dot(members, recv[...], preferred_element_type=f32)
    totals = jnp.concatenate([sums[:nodes, :], sums[nodes:, :]], axis=1)
    latent = embed_ref[...].astype(f32) + totals / divisor
    latent_ref[...] = latent
    centered = latent - jnp.mean(latent, axis=1, keepdims=True)
    inverse_std = lax.rsqrt(jnp.mean(centered * centered, axis=1, keepdims=True) + EPS)
    own = pl.ds(OWN * BLOCK, BLOCK)
    halo_ref[own, :] = (centered * inverse_std * gain_ref[...]).astype(bf16)
    for c in range(9):
        if c != OWN:
            send_to(
                halo_ref.at[own], halo_ref.at[pl.ds((8 - c) * BLOCK, BLOCK)],
                halo_send_sem, halo_recv_sem,
                (lat + c // 3 - 1 + LAT) % LAT, (lon + c % 3 - 1 + LON) % LON,
            )

    source = (iota((lanes, DEVICES), 1) == (iota((lanes, DEVICES), 0) >> 4)).astype(f32).astype(bf16)
    codes = jnp.dot(source, ids.astype(bf16), preferred_element_type=f32)
    mine = (iota((lanes, LANES), 0) & 7) == iota((lanes, LANES), 1)
    code = jnp.sum(jnp.where(mine, codes, 0.0), axis=1, keepdims=True).astype(jnp.int32)
    which = (iota((lanes, 1), 0) >> 3) & 1
    code = jnp.where(code > 0, code - 1 + nodes * which, -1)
    spread_ref[...] = (iota((lanes, 2 * nodes), 1) == code).astype(f32).astype(bf16)

    await_bytes(ids_send.at[pl.ds(0, DEVICES - 1)], ids_send_sem)
    await_bytes(send.at[pl.ds(0, (DEVICES - 1) * 2 * CAP)], send_sem)
    await_bytes(halo_ref.at[pl.ds(0, 8 * BLOCK)], halo_recv_sem)
    await_bytes(halo_ref.at[pl.ds(0, 8 * BLOCK)], halo_send_sem)


def route(grid_rows, dest_owner, dest_node, node_embed, norm_gain):
    count, width = grid_rows.shape
    nodes = node_embed.shape[0]
    lanes = 2 * DEVICES * CAP
    bf16, f32 = jnp.bfloat16, jnp.float32
    return pl.pallas_call(
        route_kernel,
        name="route",
        out_shape=(
            jax.ShapeDtypeStruct((9 * nodes, width), bf16),
            jax.ShapeDtypeStruct((nodes, width), f32),
            jax.ShapeDtypeStruct((nodes, LANES), f32),
            jax.ShapeDtypeStruct((lanes, 2 * nodes), bf16),
            jax.ShapeDtypeStruct((count, LANES), jnp.int32),
        ),
        in_specs=[pl.BlockSpec(memory_space=pltpu.VMEM)] * 5,
        out_specs=[pl.BlockSpec(memory_space=pltpu.VMEM)] * 5,
        scratch_shapes=[
            pltpu.VMEM((lanes, width // 2), bf16),
            pltpu.VMEM((lanes, width // 2), bf16),
            pltpu.VMEM((DEVICES, 1, LANES), f32),
            pltpu.VMEM((DEVICES, 1, LANES), f32),
        ] + [pltpu.SemaphoreType.DMA] * 6,
        compiler_params=pltpu.CompilerParams(
            collective_id=0, has_side_effects=True, vmem_limit_bytes=VMEM_LIMIT
        ),
    )(grid_rows, dest_owner, dest_node.reshape(1, count), node_embed, norm_gain.reshape(1, width))


def attend_kernel(
    halo_ref, listed_ref, latent_ref, cot_ref, w_qkv_ref, w_out_ref,
    mixed_ref, grads_ref, node_parts_ref,
    keys, values, q_blocks, d_blocks, scores, weights, d_keyvals, attended_t, d_query_t,
):
    f32, bf16 = jnp.float32, jnp.bfloat16
    width = latent_ref.shape[1]
    group_heads = LANES // HEAD_SIZE
    groups = HEADS // group_heads
    columns = group_heads * BLOCK
    scale = HEAD_SIZE ** (-0.5)
    to_log2 = math.log2(math.e)
    lat, lon = lax.axis_index("lat"), lax.axis_index("lon")

    listed = listed_ref[...]
    lat_step = listed // LON - lat
    lon_step = (listed % LON - lon + LON + 1) % LON - 1
    places = (lat_step + 1) * 3 + lon_step + 1
    rows = lax.broadcasted_iota(jnp.int32, (16, listed.shape[1]), 0)
    times = jnp.sum((places == rows).astype(f32), axis=1, keepdims=True)
    bias = jnp.where(times > 0, jnp.log(jnp.maximum(times, 1.0)) * to_log2, -1e30)

    halo = halo_ref[...]
    own = halo_ref[OWN * BLOCK:(OWN + 1) * BLOCK, :]
    keys[...] = jnp.dot(halo, w_qkv_ref[:, width:2 * width], preferred_element_type=f32).astype(bf16)
    values[...] = jnp.dot(halo, w_qkv_ref[:, 2 * width:], preferred_element_type=f32).astype(bf16)
    queries = jnp.dot(own, w_qkv_ref[:, :width], preferred_element_type=f32).astype(bf16)
    cot = cot_ref[...]
    d_attended = dot_cols(cot, w_out_ref[...]).astype(bf16)
    q_t = queries.astype(f32).T.astype(bf16)
    d_t = d_attended.astype(f32).T.astype(bf16)
    q_blocks[...] = jnp.zeros_like(q_blocks)
    d_blocks[...] = jnp.zeros_like(d_blocks)
    for g in range(groups):
        for h in range(group_heads):
            span = slice(h * HEAD_SIZE, (h + 1) * HEAD_SIZE)
            lanes = slice(h * BLOCK, (h + 1) * BLOCK)
            at = g * LANES + h * HEAD_SIZE
            q_blocks[g, span, lanes] = q_t[at:at + HEAD_SIZE, :]
            d_blocks[g, span, lanes] = d_t[at:at + HEAD_SIZE, :]

    def diagonal(full):
        return jnp.concatenate(
            [
                full[h * HEAD_SIZE:(h + 1) * HEAD_SIZE, h * BLOCK:(h + 1) * BLOCK]
                for h in range(group_heads)
            ],
            axis=0,
        )

    def spread(row):
        return jnp.concatenate(
            [
                jnp.broadcast_to(row[:, h * BLOCK:(h + 1) * BLOCK], (HEAD_SIZE, BLOCK))
                for h in range(group_heads)
            ],
            axis=0,
        )

    def group(g, carry):
        lanes = pl.ds(pl.multiple_of(g * LANES, LANES), LANES)
        q_block, d_block = q_blocks[g], d_blocks[g]
        highest = None
        for c in range(9):
            part = slice(c * BLOCK, (c + 1) * BLOCK)
            s = jnp.dot(keys[part, lanes], q_block, preferred_element_type=f32)
            scores[part, :] = s
            top = jnp.max(s, axis=0, keepdims=True) * (scale * to_log2) + bias[c:c + 1, :]
            highest = top if c == 0 else jnp.maximum(highest, top)
        total = jnp.zeros((1, columns), f32)
        for c in range(9):
            part = slice(c * BLOCK, (c + 1) * BLOCK)
            w = jnp.exp2(scores[part, :] * (scale * to_log2) - (highest - bias[c:c + 1, :]))
            total = total + jnp.sum(w, axis=0, keepdims=True)
            weights[part, :] = w.astype(bf16)
        inverse = 1.0 / total
        out_t = dot_rows(values[:, lanes], weights[...])
        out_group = diagonal(out_t) * spread(inverse)
        attended_t[lanes, :] = out_group.astype(bf16)
        d_group = diagonal(d_block.astype(f32))
        product = out_group * d_group
        delta = jnp.concatenate(
            [
                jnp.sum(product[h * HEAD_SIZE:(h + 1) * HEAD_SIZE, :], axis=0, keepdims=True)
                for h in range(group_heads)
            ],
            axis=1,
        )
        d_scaled = (d_block.astype(f32) * inverse).astype(bf16)
        d_keyvals[:, pl.ds(pl.multiple_of(width + g * LANES, LANES), LANES)] = dot_cols(
            weights[...], d_scaled
        ).astype(bf16)
        for c in range(9):
            part = slice(c * BLOCK, (c + 1) * BLOCK)
            d = jnp.dot(values[part, lanes], d_block, preferred_element_type=f32)
            weights[part, :] = (weights[part, :].astype(f32) * (d - delta)).astype(bf16)
        back = inverse * scale
        q_scaled = (q_block.astype(f32) * back).astype(bf16)
        d_keyvals[:, lanes] = dot_cols(weights[...], q_scaled).astype(bf16)
        d_query_t[lanes, :] = (diagonal(dot_rows(keys[:, lanes], weights[...])) * spread(back)).astype(bf16)
        return carry

    lax.fori_loop(0, groups, group, 0)

    attended = attended_t[...].astype(f32).T.astype(bf16)
    d_query = d_query_t[...].astype(f32).T.astype(bf16)
    mixed_ref[...] = (
        latent_ref[...] + jnp.dot(attended, w_out_ref[...], preferred_element_type=f32)
    ).astype(bf16)
    grads_ref[:width, :] = dot_rows(own, d_query).astype(bf16)
    grads_ref[width:2 * width, :] = dot_rows(halo, d_keyvals[:, :width]).astype(bf16)
    grads_ref[2 * width:3 * width, :] = dot_rows(halo, d_keyvals[:, width:]).astype(bf16)
    grads_ref[3 * width:, :] = jnp.dot(
        attended_t[...], cot, preferred_element_type=f32
    ).astype(bf16)
    node_parts_ref[...] = dot_cols(d_keyvals[...], w_qkv_ref[:, width:]).astype(bf16)
    part = slice(OWN * BLOCK, (OWN + 1) * BLOCK)
    node_parts_ref[part, :] = (
        dot_cols(d_keyvals[part, :], w_qkv_ref[:, width:]) + dot_cols(d_query, w_qkv_ref[:, :width])
    ).astype(bf16)


def attend(halo, listed, latent, cotangent, w_qkv, w_out):
    nodes, width = latent.shape
    columns = LANES // HEAD_SIZE * BLOCK
    groups = width // LANES
    pool = halo.shape[0]
    bf16, f32 = jnp.bfloat16, jnp.float32
    return pl.pallas_call(
        attend_kernel,
        name="attend",
        out_shape=(
            jax.ShapeDtypeStruct((nodes, width), bf16),
            jax.ShapeDtypeStruct((4 * width, width), bf16),
            jax.ShapeDtypeStruct((pool, width), bf16),
        ),
        in_specs=[pl.BlockSpec(memory_space=pltpu.VMEM)] * 6,
        out_specs=[pl.BlockSpec(memory_space=pltpu.VMEM)] * 3,
        scratch_shapes=[
            pltpu.VMEM((pool, width), bf16),
            pltpu.VMEM((pool, width), bf16),
            pltpu.VMEM((groups, LANES, columns), bf16),
            pltpu.VMEM((groups, LANES, columns), bf16),
            pltpu.VMEM((pool, columns), f32),
            pltpu.VMEM((pool, columns), bf16),
            pltpu.VMEM((pool, 2 * width), bf16),
            pltpu.VMEM((width, BLOCK), bf16),
            pltpu.VMEM((width, BLOCK), bf16),
        ],
        compiler_params=pltpu.CompilerParams(vmem_limit_bytes=VMEM_LIMIT),
    )(halo, listed, latent, cotangent, w_qkv, w_out)


ORDERS = ("xyz", "yzx", "zxy", "yxz")


def place_on(axis, lat, lon):
    return {"x": (lon // 8) * 2 + lat // 4, "y": lat % 4, "z": (lon // 2) % 4}[axis]


def moved_to(axis, index, lat, lon):
    if axis == "x":
        return (index % 2) * 4 + lat % 4, (index // 2) * 8 + lon % 8
    if axis == "y":
        return (lat // 4) * 4 + index, lon
    return lat, (lon // 8) * 8 + index * 2 + lon % 2


def exchange_kernel(
    grads_ref, parts_ref, latent_ref, divisor_ref, gain_ref, cot_ref, spread_ref,
    reduced_ref, returned_ref,
    from_core, held_0, from_1, held_1, from_2, held_2, from_3, halo, send,
    sum_send_sem, sum_recv_sem, send_sem, recv_sem, halo_send_sem, halo_recv_sem,
):
    f32, bf16 = jnp.float32, jnp.bfloat16
    lat, lon = here()
    me = lat * LON + lon
    barrier = greet_all(me)
    width = latent_ref.shape[1]
    nodes = latent_ref.shape[0]
    half = width // 2
    mats = len(ORDERS)
    core = lon % 2
    core_rows, rows_1, rows_2 = width // 2, width // 8, width // 32
    cols_3 = width // 4
    twin = (lat, lon - core + (1 - core))
    pl.semaphore_wait(barrier, DEVICES - 1)

    for p in range(mats):
        send_to(
            grads_ref.at[pl.ds(pl.multiple_of(p * width + (1 - core) * core_rows, core_rows), core_rows)],
            from_core.at[p], sum_send_sem.at[p, 0], sum_recv_sem.at[p, 0], *twin,
        )
    for c in range(9):
        if c != OWN:
            n = c - (c > OWN)
            send_to(
                parts_ref.at[pl.ds(c * BLOCK, BLOCK)], halo.at[pl.ds(n * BLOCK, BLOCK)],
                halo_send_sem, halo_recv_sem,
                (lat + c // 3 - 1 + LAT) % LAT, (lon + c % 3 - 1 + LON) % LON,
            )

    places = [[place_on(axis, lat, lon) for axis in order] for order in ORDERS]

    def others(p, level):
        axis, i = ORDERS[p][level], places[p][level]
        for k in range(1, 4):
            t = (i + k) % 4
            yield k - 1, t, moved_to(axis, t, lat, lon)

    def start_1(p):
        await_bytes(from_core.at[p], sum_recv_sem.at[p, 0])
        kept = grads_ref[pl.ds(pl.multiple_of(p * width + core * core_rows, core_rows), core_rows), :]
        held_0[p] = (kept.astype(f32) + from_core[p].astype(f32)).astype(bf16)
        for k, t, other in others(p, 0):
            send_to(
                held_0.at[p, tile_rows(t, rows_1)], from_1.at[p, pl.ds(k * rows_1, rows_1)],
                sum_send_sem.at[p, 1], sum_recv_sem.at[p, 1], *other,
            )

    def start_2(p):
        await_bytes(from_1.at[p], sum_recv_sem.at[p, 1])
        total = held_0[p, tile_rows(places[p][0], rows_1), :].astype(f32)
        for k in range(3):
            total = total + from_1[p, k * rows_1:(k + 1) * rows_1, :].astype(f32)
        held_1[p] = total.astype(bf16)
        for k, t, other in others(p, 1):
            send_to(
                held_1.at[p, tile_rows(t, rows_2)], from_2.at[p, pl.ds(k * rows_2, rows_2)],
                sum_send_sem.at[p, 2], sum_recv_sem.at[p, 2], *other,
            )

    def lanes_of(t):
        return pl.ds(pl.multiple_of(t * cols_3, cols_3), cols_3)

    def start_3(p):
        await_bytes(from_2.at[p], sum_recv_sem.at[p, 2])
        total = held_1[p, tile_rows(places[p][1], rows_2), :].astype(f32)
        for k in range(3):
            total = total + from_2[p, k * rows_2:(k + 1) * rows_2, :].astype(f32)
        held_2[p] = total.astype(bf16)
        for k, t, other in others(p, 2):
            send_to(
                held_2.at[p, :, lanes_of(t)], from_3.at[p, pl.ds(k * rows_2, rows_2)],
                sum_send_sem.at[p, 3], sum_recv_sem.at[p, 3], *other,
            )

    def region(p, level):
        row = p * width + core * core_rows
        if level == 0:
            return reduced_ref.at[pl.ds(pl.multiple_of(row, core_rows), core_rows)]
        row = row + places[p][0] * rows_1
        if level == 1:
            return reduced_ref.at[pl.ds(pl.multiple_of(row, rows_1), rows_1)]
        row = row + places[p][1] * rows_2
        return reduced_ref.at[pl.ds(pl.multiple_of(row, rows_2), rows_2)]

    def start_back_3(p):
        await_bytes(from_3.at[p], sum_recv_sem.at[p, 3])
        total = held_2[p, :, lanes_of(places[p][2])].astype(f32)
        for k in range(3):
            total = total + from_3[p, k * rows_2:(k + 1) * rows_2, :].astype(f32)
        piece = region(p, 2).at[:, lanes_of(places[p][2])]
        piece[...] = total.astype(bf16)
        for k, t, other in others(p, 2):
            send_to(piece, piece, sum_send_sem.at[p, 4], sum_recv_sem.at[p, 4], *other)

    def start_back_2(p):
        await_bytes(from_3.at[p], sum_recv_sem.at[p, 4])
        piece = region(p, 2)
        for k, t, other in others(p, 1):
            send_to(piece, piece, sum_send_sem.at[p, 5], sum_recv_sem.at[p, 5], *other)

    def start_back_1(p):
        await_bytes(from_2.at[p], sum_recv_sem.at[p, 5])
        piece = region(p, 1)
        for k, t, other in others(p, 0):
            send_to(piece, piece, sum_send_sem.at[p, 6], sum_recv_sem.at[p, 6], *other)

    def start_back_core(p):
        await_bytes(from_1.at[p], sum_recv_sem.at[p, 6])
        piece = region(p, 0)
        send_to(piece, piece, sum_send_sem.at[p, 7], sum_recv_sem.at[p, 7], *twin)

    for p in range(mats):
        start_1(p)

    await_bytes(halo, halo_recv_sem)
    d_normed = parts_ref[OWN * BLOCK:(OWN + 1) * BLOCK, :].astype(f32)
    for n in range(8):
        d_normed = d_normed + halo[n * BLOCK:(n + 1) * BLOCK, :].astype(f32)
    latent = latent_ref[...]
    centered = latent - jnp.mean(latent, axis=1, keepdims=True)
    inverse_std = lax.rsqrt(jnp.mean(centered * centered, axis=1, keepdims=True) + EPS)
    normalized = centered * inverse_std
    scaled = d_normed * gain_ref[...]
    d_latent = cot_ref[...].astype(f32) + inverse_std * (
        scaled
        - jnp.mean(scaled, axis=1, keepdims=True)
        - normalized * jnp.mean(scaled * normalized, axis=1, keepdims=True)
    )
    node_grad = (d_latent / divisor_ref[:, 0:1]).astype(bf16)
    stacked = jnp.concatenate([node_grad[:, :half], node_grad[:, half:]], axis=0)
    send[...] = jnp.dot(spread_ref[...], stacked, preferred_element_type=f32).astype(bf16)

    def push(step, carry):
        other = (me + step) % DEVICES
        send_to(
            send.at[tile_rows(other, 2 * CAP)], returned_ref.at[tile_rows(me, 2 * CAP)],
            send_sem, recv_sem, other // LON, other % LON,
        )
        return carry

    lax.fori_loop(1, DEVICES, push, 0)
    pltpu.make_async_copy(
        send.at[tile_rows(me, 2 * CAP)], returned_ref.at[tile_rows(me, 2 * CAP)], recv_sem
    ).start()

    for stage in (start_2, start_3, start_back_3, start_back_2, start_back_1, start_back_core):
        for p in range(mats):
            stage(p)
    for p in range(mats):
        await_bytes(from_core.at[p], sum_recv_sem.at[p, 7])
        sizes = (from_core, from_1, from_2, from_3, from_3, from_2, from_1, from_core)
        for level, like in enumerate(sizes):
            await_bytes(like.at[p], sum_send_sem.at[p, level])
    await_bytes(halo, halo_send_sem)
    await_bytes(returned_ref, recv_sem)
    await_bytes(send.at[pl.ds(0, (DEVICES - 1) * 2 * CAP)], send_sem)


def exchange(grads, node_parts, latent, divisor, norm_gain, cotangent, spread):
    nodes, width = latent.shape
    lanes = 2 * DEVICES * CAP
    mats = len(ORDERS)
    bf16 = jnp.bfloat16
    return pl.pallas_call(
        exchange_kernel,
        name="exchange",
        out_shape=(
            jax.ShapeDtypeStruct((4 * width, width), bf16),
            jax.ShapeDtypeStruct((lanes, width // 2), bf16),
        ),
        in_specs=[pl.BlockSpec(memory_space=pltpu.VMEM)] * 7,
        out_specs=[pl.BlockSpec(memory_space=pltpu.VMEM)] * 2,
        scratch_shapes=[
            pltpu.VMEM((mats, width // 2, width), bf16),
            pltpu.VMEM((mats, width // 2, width), bf16),
            pltpu.VMEM((mats, 3 * width // 8, width), bf16),
            pltpu.VMEM((mats, width // 8, width), bf16),
            pltpu.VMEM((mats, 3 * width // 32, width), bf16),
            pltpu.VMEM((mats, width // 32, width), bf16),
            pltpu.VMEM((mats, 3 * width // 32, width // 4), bf16),
            pltpu.VMEM((8 * nodes, width), bf16),
            pltpu.VMEM((lanes, width // 2), bf16),
            pltpu.SemaphoreType.DMA((mats, 8)),
            pltpu.SemaphoreType.DMA((mats, 8)),
        ] + [pltpu.SemaphoreType.DMA] * 4,
        compiler_params=pltpu.CompilerParams(
            collective_id=1, has_side_effects=True, vmem_limit_bytes=VMEM_LIMIT
        ),
    )(grads, node_parts, latent, divisor, norm_gain.reshape(1, width), cotangent, spread)


def finish_kernel(
    reduced_ref, returned_ref, flat_ref, w_qkv_ref, gain_ref,
    grad_grid_ref, grad_w_qkv_ref, grad_w_out_ref, grad_gain_ref,
):
    f32, bf16 = jnp.float32, jnp.bfloat16
    count, width = grad_grid_ref.shape
    half = width // 2
    slots = DEVICES * CAP
    back = returned_ref[...].astype(f32).reshape(DEVICES, 2 * CAP, half)
    back = jnp.concatenate([back[:, :CAP, :], back[:, CAP:, :]], axis=2)
    back = back.reshape(slots, width).astype(bf16)
    chosen = (iota((count, slots), 1) == flat_ref[:, 0:1]).astype(f32).astype(bf16)
    grad_grid_ref[...] = jnp.dot(chosen, back, preferred_element_type=f32).astype(bf16)
    product = jnp.zeros((width, 1), f32)
    for third in range(3):
        span = slice(third * width, (third + 1) * width)
        grad = reduced_ref[span, :].astype(f32)
        grad_w_qkv_ref[:, span] = grad
        product = product + jnp.sum(grad * w_qkv_ref[:, span].astype(f32), axis=1, keepdims=True)
    grad_w_out_ref[...] = reduced_ref[3 * width:, :].astype(f32)
    row = jnp.broadcast_to(product, (width, LANES)).T[0:1, :]
    grad_gain_ref[...] = row / gain_ref[...]


def finish(reduced, returned, flat, w_qkv, norm_gain):
    width = w_qkv.shape[0]
    count = flat.shape[0]
    f32 = jnp.float32
    return pl.pallas_call(
        finish_kernel,
        name="finish",
        out_shape=(
            jax.ShapeDtypeStruct((count, width), jnp.bfloat16),
            jax.ShapeDtypeStruct((width, 3 * width), f32),
            jax.ShapeDtypeStruct((width, width), f32),
            jax.ShapeDtypeStruct((1, width), f32),
        ),
        in_specs=[pl.BlockSpec(memory_space=pltpu.VMEM)] * 5,
        out_specs=[pl.BlockSpec(memory_space=pltpu.VMEM)] * 4,
        compiler_params=pltpu.CompilerParams(vmem_limit_bytes=VMEM_LIMIT),
    )(reduced, returned, flat, w_qkv, norm_gain.reshape(1, width))


def local(
    grid_rows, dest_owner, dest_node, node_embed, neighbours, norm_gain, w_qkv, w_out, cotangent
):
    halo, latent, divisor, spread, flat = route(
        grid_rows, dest_owner, dest_node, node_embed, norm_gain
    )
    mixed, grads, node_parts = attend(halo, neighbours, latent, cotangent, w_qkv, w_out)
    reduced, returned = exchange(
        grads, node_parts, latent, divisor, norm_gain, cotangent, spread
    )
    grad_grid, grad_w_qkv, grad_w_out, grad_gain = finish(reduced, returned, flat, w_qkv, norm_gain)
    return (mixed, grad_grid, grad_w_qkv, grad_w_out, grad_gain.reshape(norm_gain.shape))


def solution(mesh):
    split = P(("lat", "lon"), None)
    in_specs = (split, split, P(("lat", "lon")), split, split, P(), P(), P(), split)
    out_specs = (split, split, P(), P(), P())
    return jax.shard_map(local, mesh=mesh, in_specs=in_specs, out_specs=out_specs, check_vma=False)
```

```python
import math

import jax
import jax.numpy as jnp
from jax import lax
from jax.experimental import pallas as pl
from jax.experimental.pallas import tpu as pltpu
from jax.sharding import PartitionSpec as P

HEADS = 16
HEAD_SIZE = 32
BLOCK = 128
LANES = 128
LAT = 8
LON = 16
DEVICES = LAT * LON
OWN = 4
CAP = 8
GROUPS = 4
GROUP_HEADS = LANES // HEAD_SIZE
COLUMNS = GROUP_HEADS * BLOCK
SCALE = HEAD_SIZE ** (-0.5)
TO_LOG2 = math.log2(math.e)
EPS = 1e-05
VMEM_LIMIT = 56 * 1024 * 1024
MESH = pl.DeviceIdType.MESH
F32, BF16 = jnp.float32, jnp.bfloat16
ORDERS = (
    ("xyz", "yzx", "zxy", "xzy"),
    ("xyz", "yzx", "zxy", "yxz"),
    ("xyz", "yzx", "zxy", "zyx"),
    ("xyz", "yzx", "zxy", "yzx"),
)
ROWS_CORE, ROWS_1, ROWS_2 = 256, 64, 16


def dot(a, b):
    return jnp.dot(a, b, preferred_element_type=F32)


def dot_rows(a, b):
    return lax.dot_general(a, b, (((0,), (0,)), ((), ())), preferred_element_type=F32)


def dot_cols(a, b):
    return lax.dot_general(a, b, (((1,), (1,)), ((), ())), preferred_element_type=F32)


def iota(shape, dim):
    return lax.broadcasted_iota(jnp.int32, shape, dim)


def one_hot(condition):
    return condition.astype(F32).astype(BF16)


def turned(a):
    return a.astype(F32).T.astype(BF16)


def await_bytes(ref, sem):
    pltpu.make_async_copy(ref, ref, sem).wait()


def send_to(src, dst, send_sem, recv_sem, place):
    pltpu.make_async_remote_copy(
        src_ref=src,
        dst_ref=dst,
        send_sem=send_sem,
        recv_sem=recv_sem,
        device_id=place,
        device_id_type=MESH,
    ).start()


def tile_rows(index, rows):
    return pl.ds(pl.multiple_of(index * rows, rows), rows)


def block_rows(c):
    return pl.ds(c * BLOCK, BLOCK)


def around(lat, lon):
    for c in range(9):
        if c != OWN:
            yield c, ((lat + c // 3 - 1 + LAT) % LAT, (lon + c % 3 - 1 + LON) % LON)


def place_on(axis, lat, lon):
    return {"x": (lon // 8) * 2 + lat // 4, "y": lat % 4, "z": (lon // 2) % 4}[axis]


def moved_to(axis, index, lat, lon):
    if axis == "x":
        return (index % 2) * 4 + lat % 4, (index // 2) * 8 + lon % 8
    if axis == "y":
        return (lat // 4) * 4 + index, lon
    return lat, (lon // 8) * 8 + index * 2 + lon % 2


def diagonal(full):
    return jnp.concatenate(
        [
            full[h * HEAD_SIZE:(h + 1) * HEAD_SIZE, h * BLOCK:(h + 1) * BLOCK]
            for h in range(GROUP_HEADS)
        ],
        axis=0,
    )


def spread_heads(row):
    return jnp.concatenate(
        [
            jnp.broadcast_to(row[:, h * BLOCK:(h + 1) * BLOCK], (HEAD_SIZE, BLOCK))
            for h in range(GROUP_HEADS)
        ],
        axis=0,
    )


def sublayer_kernel(
    grid_ref, owner_ref, node_ref, listed_ref, gain_ref, embed_hbm, w_qkv_hbm, w_out_hbm, cot_hbm,
    mixed_ref, reduced_ref, returned_ref, flat_ref,
    embed_ref, w_qkv_ref, w_out_ref, cot_ref,
    send, recv, ids_send, ids_recv,
    halo, halo_t, latent_ref, spread_ref, keys, values, q_blocks, d_blocks,
    scores, weights, inverses, deltas, d_keyvals, attended_t, d_query_t,
    grads, from_core, held_0, from_1, held_1, from_2, from_3, parts, from_around,
    load_sem, send_sem, recv_sem, ids_send_sem, ids_recv_sem, halo_send_sem, halo_recv_sem,
    sum_send_sem, sum_recv_sem, parts_send_sem, parts_recv_sem, back_send_sem, back_recv_sem,
):
    lat, lon = lax.axis_index("lat"), lax.axis_index("lon")
    me = lat * LON + lon
    barrier = pltpu.get_barrier_semaphore()

    def greet(step, carry):
        other = (me + step) % DEVICES
        pl.semaphore_signal(
            barrier, inc=1, device_id=(other // LON, other % LON), device_id_type=MESH
        )
        return carry

    lax.fori_loop(1, DEVICES, greet, 0)
    loads = [
        pltpu.make_async_copy(src, dst, load_sem.at[i])
        for i, (src, dst) in enumerate(
            ((embed_hbm, embed_ref), (w_qkv_hbm, w_qkv_ref), (w_out_hbm, w_out_ref), (cot_hbm, cot_ref))
        )
    ]
    for load in loads:
        load.start()

    count, width = grid_ref.shape
    nodes = embed_ref.shape[0]
    half = width // 2
    slots = DEVICES * CAP

    owner = owner_ref[...]
    picked = (iota((DEVICES, count), 0) == owner).astype(F32)
    earlier = one_hot(iota((count, count), 0) < iota((count, count), 1))
    slot = jnp.sum(picked * dot(picked.astype(BF16), earlier), axis=0, keepdims=True).astype(jnp.int32)
    flat = owner * CAP + slot
    named = (picked * (node_ref[...] + 1).astype(F32)).astype(BF16)
    ids_send[:, 0, :] = dot_cols(named, one_hot(iota((LANES, count), 0) == slot))
    grid = grid_ref[...]

    pl.semaphore_wait(barrier, DEVICES - 1)
    for step in (0, 1, 7, 2, 6, 3, 5, 4):
        to_lat = (lat + step) % LAT
        chosen = one_hot(iota((LON * CAP, count), 0) + to_lat * (LON * CAP) == flat)
        block = dot(chosen, grid).reshape(LON, CAP, width)
        block = jnp.concatenate([block[:, :, :half], block[:, :, half:]], axis=1)
        send[tile_rows(to_lat, 2 * CAP * LON), :] = block.reshape(2 * CAP * LON, half).astype(BF16)

        def push(j, carry, to_lat=to_lat):
            to_lon = (lon + j) % LON
            other = to_lat * LON + to_lon
            send_to(ids_send.at[other], ids_recv.at[me], ids_send_sem, ids_recv_sem, (to_lat, to_lon))
            send_to(
                send.at[tile_rows(other, 2 * CAP)], recv.at[tile_rows(me, 2 * CAP)],
                send_sem, recv_sem, (to_lat, to_lon),
            )
            return carry

        lax.fori_loop(1 if step == 0 else 0, LON, push, 0)
    pltpu.make_async_copy(ids_send.at[me], ids_recv.at[me], ids_recv_sem).start()
    pltpu.make_async_copy(
        send.at[tile_rows(me, 2 * CAP)], recv.at[tile_rows(me, 2 * CAP)], recv_sem
    ).start()

    for load in loads:
        load.wait()
    cot = cot_ref[...]
    d_t = turned(dot_cols(cot, w_out_ref[...]).astype(BF16))
    q_blocks[...] = jnp.zeros_like(q_blocks)
    d_blocks[...] = jnp.zeros_like(d_blocks)

    def blocks_of(target, full_t):
        for g in range(GROUPS):
            for h in range(GROUP_HEADS):
                at = g * LANES + h * HEAD_SIZE
                target[g, h * HEAD_SIZE:(h + 1) * HEAD_SIZE, h * BLOCK:(h + 1) * BLOCK] = full_t[
                    at:at + HEAD_SIZE, :
                ]

    blocks_of(d_blocks, d_t)
    flat_ref[...] = jnp.broadcast_to(flat.astype(F32), (LANES, count)).T.astype(jnp.int32)
    listed = listed_ref[...]
    lat_step = listed // LON - lat
    lon_step = (listed % LON - lon + LON + 1) % LON - 1
    at_place = (lat_step + 1) * 3 + lon_step + 1 == iota((16, listed.shape[1]), 0)
    times = jnp.sum(at_place.astype(F32), axis=1, keepdims=True)
    bias = jnp.where(times > 0, jnp.log(jnp.maximum(times, 1.0)) * TO_LOG2, -1e30)

    await_bytes(ids_recv, ids_recv_sem)
    ids = ids_recv[:, 0, :]
    lanes = 2 * slots
    codes = dot(turned(ids)[:CAP, :], one_hot(iota((DEVICES, lanes), 0) == (iota((DEVICES, lanes), 1) >> 4)))
    mine = (iota((CAP, lanes), 1) & 7) == iota((CAP, lanes), 0)
    code = jnp.sum(jnp.where(mine, codes, 0.0), axis=0, keepdims=True).astype(jnp.int32)
    code = jnp.where(code > 0, code - 1 + nodes * ((iota((1, lanes), 1) >> 3) & 1), -1)
    members = (iota((2 * nodes, lanes), 0) == code).astype(F32)
    divisor = jnp.maximum(jnp.sum(members[:nodes, :], axis=1, keepdims=True), 1.0)
    members = members.astype(BF16)
    await_bytes(recv, recv_sem)
    sums = dot(members, recv[...])
    totals = jnp.concatenate([sums[:nodes, :], sums[nodes:, :]], axis=1)
    latent = embed_ref[...].astype(F32) + totals / divisor
    latent_ref[...] = latent
    centered = latent - jnp.mean(latent, axis=1, keepdims=True)
    inverse_std = lax.rsqrt(jnp.mean(centered * centered, axis=1, keepdims=True) + EPS)
    halo[block_rows(OWN), :] = (centered * inverse_std * gain_ref[...]).astype(BF16)
    for c, place in around(lat, lon):
        send_to(
            halo.at[block_rows(OWN)], halo.at[block_rows(8 - c)], halo_send_sem, halo_recv_sem, place
        )

    own = halo[block_rows(OWN), :]
    own_t = turned(own)
    blocks_of(q_blocks, turned(dot(own, w_qkv_ref[:, :width]).astype(BF16)))

    def project(rows):
        keys[rows, :] = dot(halo[rows, :], w_qkv_ref[:, width:2 * width]).astype(BF16)
        values[rows, :] = dot(halo[rows, :], w_qkv_ref[:, 2 * width:]).astype(BF16)

    project(slice(OWN * BLOCK, (OWN + 1) * BLOCK))
    codes = dot(one_hot(iota((lanes, DEVICES), 1) == (iota((lanes, DEVICES), 0) >> 4)), ids.astype(BF16))
    mine = (iota((lanes, LANES), 0) & 7) == iota((lanes, LANES), 1)
    code = jnp.sum(jnp.where(mine, codes, 0.0), axis=1, keepdims=True).astype(jnp.int32)
    code = jnp.where(code > 0, code - 1 + nodes * ((iota((lanes, 1), 0) >> 3) & 1), -1)
    spread_ref[...] = one_hot(iota((lanes, 2 * nodes), 1) == code)

    await_bytes(halo.at[pl.ds(0, 8 * BLOCK)], halo_recv_sem)
    project(slice(0, OWN * BLOCK))
    project(slice((OWN + 1) * BLOCK, 9 * BLOCK))
    halo_t[...] = turned(halo[...])

    def forward(g, carry):
        cols = pl.ds(pl.multiple_of(g * LANES, LANES), LANES)
        q_block = q_blocks[g]
        highest = None
        for c in range(9):
            part = slice(c * BLOCK, (c + 1) * BLOCK)
            s = dot(keys[part, cols], q_block)
            scores[part, :] = s
            top = jnp.max(s, axis=0, keepdims=True) * (SCALE * TO_LOG2) + bias[c:c + 1, :]
            highest = top if c == 0 else jnp.maximum(highest, top)
        total = jnp.zeros((1, COLUMNS), F32)
        for c in range(9):
            part = slice(c * BLOCK, (c + 1) * BLOCK)
            w = jnp.exp2(scores[part, :] * (SCALE * TO_LOG2) - (highest - bias[c:c + 1, :]))
            total = total + jnp.sum(w, axis=0, keepdims=True)
            weights[g, part, :] = w.astype(BF16)
        inverse = 1.0 / total
        out_group = diagonal(dot_rows(values[:, cols], weights[g])) * spread_heads(inverse)
        attended_t[cols, :] = out_group.astype(BF16)
        product = out_group * diagonal(d_blocks[g].astype(F32))
        delta = jnp.concatenate(
            [
                jnp.sum(product[h * HEAD_SIZE:(h + 1) * HEAD_SIZE, :], axis=0, keepdims=True)
                for h in range(GROUP_HEADS)
            ],
            axis=1,
        )
        inverses[g] = jnp.broadcast_to(inverse, (8, COLUMNS))
        deltas[g] = jnp.broadcast_to(delta, (8, COLUMNS))
        return carry

    lax.fori_loop(0, GROUPS, forward, 0)
    grad_w_out = dot(attended_t[...], cot).astype(BF16)
    for g in range(GROUPS):
        grads[4 * g + 3] = grad_w_out[:, g * LANES:(g + 1) * LANES]

    core = lon % 2
    twin = (lat, lon - core + (1 - core))
    core_rows = tile_rows(core, ROWS_CORE)
    places = {axis: place_on(axis, lat, lon) for axis in "xyz"}

    def group_units(g):
        return pl.ds(4 * g, 4)

    def others(axis):
        for k in range(1, 4):
            t = (places[axis] + k) % 4
            yield k - 1, t, moved_to(axis, t, lat, lon)

    def sum_core(g):
        send_to(
            grads.at[group_units(g), tile_rows(1 - core, ROWS_CORE)], from_core.at[group_units(g)],
            sum_send_sem.at[g, 0], sum_recv_sem.at[g, 0], twin,
        )

    def sum_1(g):
        await_bytes(from_core.at[group_units(g)], sum_recv_sem.at[g, 0])
        for m, order in enumerate(ORDERS[g]):
            u = 4 * g + m
            held_0[u] = (grads[u, core_rows, :].astype(F32) + from_core[u].astype(F32)).astype(BF16)
            for k, t, place in others(order[0]):
                send_to(
                    held_0.at[u, tile_rows(t, ROWS_1)], from_1.at[u, pl.ds(k * ROWS_1, ROWS_1)],
                    sum_send_sem.at[g, 1], sum_recv_sem.at[g, 1], place,
                )

    def sum_2(g):
        await_bytes(from_1.at[group_units(g)], sum_recv_sem.at[g, 1])
        for m, order in enumerate(ORDERS[g]):
            u = 4 * g + m
            total = held_0[u, tile_rows(places[order[0]], ROWS_1), :].astype(F32)
            for k in range(3):
                total = total + from_1[u, k * ROWS_1:(k + 1) * ROWS_1, :].astype(F32)
            held_1[u] = total.astype(BF16)
            for k, t, place in others(order[1]):
                send_to(
                    held_1.at[u, tile_rows(t, ROWS_2)], from_2.at[u, pl.ds(k * ROWS_2, ROWS_2)],
                    sum_send_sem.at[g, 2], sum_recv_sem.at[g, 2], place,
                )

    def sum_3(g):
        await_bytes(from_2.at[group_units(g)], sum_recv_sem.at[g, 2])
        for m, order in enumerate(ORDERS[g]):
            u = 4 * g + m
            total = held_1[u, tile_rows(places[order[1]], ROWS_2), :].astype(F32)
            for k in range(3):
                total = total + from_2[u, k * ROWS_2:(k + 1) * ROWS_2, :].astype(F32)
            mine = from_3.at[u, tile_rows(places[order[2]], ROWS_2)]
            mine[...] = total.astype(BF16)
            for k, t, place in others(order[2]):
                send_to(mine, mine, sum_send_sem.at[g, 3], sum_recv_sem.at[g, 3], place)

    def region(u, order, level):
        row = core * ROWS_CORE + places[order[0]] * ROWS_1
        if level == 1:
            return reduced_ref.at[u, pl.ds(pl.multiple_of(row, ROWS_1), ROWS_1)]
        row = row + places[order[1]] * ROWS_2
        return reduced_ref.at[u, pl.ds(pl.multiple_of(row, ROWS_2), ROWS_2)]

    def back_2(g):
        await_bytes(from_2.at[group_units(g)], sum_recv_sem.at[g, 3])
        for m, order in enumerate(ORDERS[g]):
            u = 4 * g + m
            total = from_3[u, :ROWS_2, :].astype(F32)
            for k in range(1, 4):
                total = total + from_3[u, k * ROWS_2:(k + 1) * ROWS_2, :].astype(F32)
            piece = region(u, order, 2)
            piece[...] = total.astype(BF16)
            for k, t, place in others(order[1]):
                send_to(piece, piece, sum_send_sem.at[g, 4], sum_recv_sem.at[g, 4], place)

    def back_1(g):
        await_bytes(from_2.at[group_units(g)], sum_recv_sem.at[g, 4])
        for m, order in enumerate(ORDERS[g]):
            piece = region(4 * g + m, order, 1)
            for k, t, place in others(order[0]):
                send_to(piece, piece, sum_send_sem.at[g, 5], sum_recv_sem.at[g, 5], place)

    def back_core(g):
        await_bytes(from_1.at[group_units(g)], sum_recv_sem.at[g, 5])
        piece = reduced_ref.at[group_units(g), core_rows]
        send_to(piece, piece, sum_send_sem.at[g, 6], sum_recv_sem.at[g, 6], twin)

    def sum_end(g):
        units = group_units(g)
        await_bytes(from_core.at[units], sum_recv_sem.at[g, 6])
        for level, like in enumerate((from_core, from_1, from_2, from_2, from_2, from_1, from_core)):
            await_bytes(like.at[units], sum_send_sem.at[g, level])

    stages = (sum_core, sum_1, sum_2, sum_3, back_2, back_1, back_core, sum_end)
    reached = [0] * GROUPS

    def advance(*groups):
        for g in groups:
            if reached[g] < len(stages):
                stages[reached[g]](g)
                reached[g] += 1

    for g in range(GROUPS):
        cols = slice(g * LANES, (g + 1) * LANES)
        q_block, d_block = q_blocks[g].astype(F32), d_blocks[g]
        inverse, delta = inverses[g, 0:1, :], deltas[g, 0:1, :]
        d_scaled = (d_block.astype(F32) * inverse).astype(BF16)
        d_values = dot_cols(weights[g], d_scaled).astype(BF16)
        d_keyvals[:, width + g * LANES:width + (g + 1) * LANES] = d_values
        for c in range(9):
            part = slice(c * BLOCK, (c + 1) * BLOCK)
            d = dot(values[part, cols], d_block)
            weights[g, part, :] = (weights[g, part, :].astype(F32) * (d - delta)).astype(BF16)
        back = inverse * SCALE
        d_keys = dot_cols(weights[g], (q_block * back).astype(BF16)).astype(BF16)
        d_keyvals[:, cols] = d_keys
        d_query = (diagonal(dot_rows(keys[:, cols], weights[g])) * spread_heads(back)).astype(BF16)
        d_query_t[cols, :] = d_query
        grads[4 * g] = dot_cols(own_t, d_query).astype(BF16)
        both = dot(halo_t[...], jnp.concatenate([d_keys, d_values], axis=1)).astype(BF16)
        grads[4 * g + 1] = both[:, :LANES]
        grads[4 * g + 2] = both[:, LANES:]
        advance(*range(g + 1))

    for c, place in around(lat, lon):
        parts[block_rows(c), :] = dot_cols(
            d_keyvals[block_rows(c), :], w_qkv_ref[:, width:]
        ).astype(BF16)
        n = c - 1 if c > OWN else c
        send_to(
            parts.at[block_rows(c)], from_around.at[block_rows(n)],
            parts_send_sem, parts_recv_sem, place,
        )
    advance(0, 1, 2, 3)
    d_normed = dot_cols(d_keyvals[block_rows(OWN), :], w_qkv_ref[:, width:]) + dot_cols(
        turned(d_query_t[...]), w_qkv_ref[:, :width]
    )
    mixed_ref[...] = (latent_ref[...] + dot_rows(attended_t[...], w_out_ref[...])).astype(BF16)
    advance(0, 1, 2, 3)
    latent = latent_ref[...]
    centered = latent - jnp.mean(latent, axis=1, keepdims=True)
    inverse_std = lax.rsqrt(jnp.mean(centered * centered, axis=1, keepdims=True) + EPS)
    normalized = centered * inverse_std
    await_bytes(from_around, parts_recv_sem)
    for n in range(8):
        d_normed = d_normed + from_around[block_rows(n), :].astype(F32)
    scaled = d_normed * gain_ref[...]
    d_latent = cot.astype(F32) + inverse_std * (
        scaled
        - jnp.mean(scaled, axis=1, keepdims=True)
        - normalized * jnp.mean(scaled * normalized, axis=1, keepdims=True)
    )
    node_grad = (d_latent / divisor).astype(BF16)
    stacked = jnp.concatenate([node_grad[:, :half], node_grad[:, half:]], axis=0)

    await_bytes(send.at[pl.ds(0, (DEVICES - 1) * 2 * CAP)], send_sem)
    for step in (0, 1, 7, 2, 6, 3, 5, 4):
        to_lat = (lat + step) % LAT
        rows = tile_rows(to_lat, 2 * CAP * LON)
        send[rows, :] = dot(spread_ref[rows, :], stacked).astype(BF16)

        def push_back(j, carry, to_lat=to_lat):
            to_lon = (lon + j) % LON
            other = to_lat * LON + to_lon
            send_to(
                send.at[tile_rows(other, 2 * CAP)], returned_ref.at[tile_rows(me, 2 * CAP)],
                back_send_sem, back_recv_sem, (to_lat, to_lon),
            )
            return carry

        lax.fori_loop(1 if step == 0 else 0, LON, push_back, 0)
    pltpu.make_async_copy(
        send.at[tile_rows(me, 2 * CAP)], returned_ref.at[tile_rows(me, 2 * CAP)], back_recv_sem
    ).start()
    while min(reached) < len(stages):
        advance(0, 1, 2, 3)
    await_bytes(ids_send.at[pl.ds(0, DEVICES - 1)], ids_send_sem)
    await_bytes(halo.at[pl.ds(0, 8 * BLOCK)], halo_send_sem)
    await_bytes(from_around, parts_send_sem)
    await_bytes(send.at[pl.ds(0, (DEVICES - 1) * 2 * CAP)], back_send_sem)
    await_bytes(returned_ref, back_recv_sem)


def sublayer(grid_rows, owner, node, embed, listed, gain, w_qkv, w_out, cotangent):
    count, width = grid_rows.shape
    nodes = embed.shape[0]
    lanes = 2 * DEVICES * CAP
    pool = 9 * nodes
    units = 4 * GROUPS
    vmem, dma = pltpu.VMEM, pltpu.SemaphoreType.DMA
    return pl.pallas_call(
        sublayer_kernel,
        name="sublayer",
        out_shape=(
            jax.ShapeDtypeStruct((nodes, width), BF16),
            jax.ShapeDtypeStruct((units, width, LANES), BF16),
            jax.ShapeDtypeStruct((lanes, width // 2), BF16),
            jax.ShapeDtypeStruct((count, LANES), jnp.int32),
        ),
        in_specs=[pl.BlockSpec(memory_space=vmem)] * 5 + [pl.BlockSpec(memory_space=pl.ANY)] * 4,
        out_specs=[pl.BlockSpec(memory_space=vmem)] * 4,
        scratch_shapes=[
            vmem((nodes, width), BF16),
            vmem(w_qkv.shape, BF16),
            vmem(w_out.shape, BF16),
            vmem((nodes, width), BF16),
            vmem((lanes, width // 2), BF16),
            vmem((lanes, width // 2), BF16),
            vmem((DEVICES, 1, LANES), F32),
            vmem((DEVICES, 1, LANES), F32),
            vmem((pool, width), BF16),
            vmem((width, pool), BF16),
            vmem((nodes, width), F32),
            vmem((lanes, 2 * nodes), BF16),
            vmem((pool, width), BF16),
            vmem((pool, width), BF16),
            vmem((GROUPS, LANES, COLUMNS), BF16),
            vmem((GROUPS, LANES, COLUMNS), BF16),
            vmem((pool, COLUMNS), F32),
            vmem((GROUPS, pool, COLUMNS), BF16),
            vmem((GROUPS, 8, COLUMNS), F32),
            vmem((GROUPS, 8, COLUMNS), F32),
            vmem((pool, 2 * width), BF16),
            vmem((width, BLOCK), BF16),
            vmem((width, BLOCK), BF16),
            vmem((units, width, LANES), BF16),
            vmem((units, ROWS_CORE, LANES), BF16),
            vmem((units, ROWS_CORE, LANES), BF16),
            vmem((units, 3 * ROWS_1, LANES), BF16),
            vmem((units, ROWS_1, LANES), BF16),
            vmem((units, 3 * ROWS_2, LANES), BF16),
            vmem((units, 4 * ROWS_2, LANES), BF16),
            vmem((pool, width), BF16),
            vmem((8 * nodes, width), BF16),
            dma((4,)),
        ] + [dma] * 6 + [dma((GROUPS, 7))] * 2 + [dma] * 4,
        compiler_params=pltpu.CompilerParams(
            collective_id=0, has_side_effects=True, vmem_limit_bytes=VMEM_LIMIT
        ),
    )(
        grid_rows, owner.reshape(1, count), node.reshape(1, count), listed, gain.reshape(1, width),
        embed, w_qkv, w_out, cotangent,
    )


def finish_kernel(
    reduced_ref, returned_ref, flat_ref, w_qkv_ref, gain_ref, mixed_in_ref,
    mixed_ref, grad_grid_ref, grad_w_qkv_ref, grad_w_out_ref, grad_gain_ref,
):
    count, width = grad_grid_ref.shape
    half = width // 2
    slots = DEVICES * CAP
    mixed_ref[...] = mixed_in_ref[...]
    product = jnp.zeros((width, LANES), F32)
    for g in range(GROUPS):
        for m in range(3):
            cols = slice(m * width + g * LANES, m * width + (g + 1) * LANES)
            grad = reduced_ref[4 * g + m].astype(F32)
            grad_w_qkv_ref[:, cols] = grad
            product = product + grad * w_qkv_ref[:, cols].astype(F32)
        grad_w_out_ref[:, g * LANES:(g + 1) * LANES] = reduced_ref[4 * g + 3].astype(F32)
    grad_gain_ref[...] = jnp.sum(product.T, axis=0, keepdims=True) / gain_ref[...]
    back = returned_ref[...].astype(F32).reshape(DEVICES, 2 * CAP, half)
    back = jnp.concatenate([back[:, :CAP, :], back[:, CAP:, :]], axis=2)
    back = back.reshape(slots, width).astype(BF16)
    chosen = one_hot(iota((count, slots), 1) == flat_ref[:, 0:1])
    grad_grid_ref[...] = dot(chosen, back).astype(BF16)


def finish(reduced, returned, flat, w_qkv, gain, mixed):
    width = w_qkv.shape[0]
    count = flat.shape[0]
    return pl.pallas_call(
        finish_kernel,
        name="finish",
        out_shape=(
            jax.ShapeDtypeStruct(mixed.shape, BF16),
            jax.ShapeDtypeStruct((count, width), BF16),
            jax.ShapeDtypeStruct((width, 3 * width), F32),
            jax.ShapeDtypeStruct((width, width), F32),
            jax.ShapeDtypeStruct((1, width), F32),
        ),
        in_specs=[pl.BlockSpec(memory_space=pltpu.VMEM)] * 6,
        out_specs=[pl.BlockSpec(memory_space=pltpu.VMEM)] * 5,
        compiler_params=pltpu.CompilerParams(vmem_limit_bytes=VMEM_LIMIT),
    )(reduced, returned, flat, w_qkv, gain.reshape(1, width), mixed)


def local(
    grid_rows, dest_owner, dest_node, node_embed, neighbours, norm_gain, w_qkv, w_out, cotangent
):
    mixed, reduced, returned, flat = sublayer(
        grid_rows, dest_owner, dest_node, node_embed, neighbours, norm_gain, w_qkv, w_out, cotangent
    )
    mixed, grad_grid, grad_w_qkv, grad_w_out, grad_gain = finish(
        reduced, returned, flat, w_qkv, norm_gain, mixed
    )
    return (mixed, grad_grid, grad_w_qkv, grad_w_out, grad_gain.reshape(norm_gain.shape))


def solution(mesh):
    split = P(("lat", "lon"), None)
    in_specs = (split, split, P(("lat", "lon")), split, split, P(), P(), P(), split)
    out_specs = (split, split, P(), P(), P())
    return jax.shard_map(local, mesh=mesh, in_specs=in_specs, out_specs=out_specs, check_vma=False)
```

```python
import math

import jax
import jax.numpy as jnp
from jax import lax
from jax.experimental import pallas as pl
from jax.experimental.pallas import tpu as pltpu
from jax.sharding import PartitionSpec as P

HEADS = 16
HEAD_SIZE = 32
BLOCK = 128
LANES = 128
LAT = 8
LON = 16
DEVICES = LAT * LON
OWN = 4
CAP = 8
GROUPS = 4
GROUP_HEADS = LANES // HEAD_SIZE
COLUMNS = GROUP_HEADS * BLOCK
SCALE = HEAD_SIZE ** (-0.5)
TO_LOG2 = math.log2(math.e)
EPS = 1e-05
VMEM_LIMIT = 56 * 1024 * 1024
MESH = pl.DeviceIdType.MESH
F32, BF16 = jnp.float32, jnp.bfloat16
FIRST_AXES = "xyz"
CHIPS = DEVICES // 2
ROWS_CORE, ROWS_1, ROWS_2 = 256, 64, 16


def dot(a, b):
    return jnp.dot(a, b, preferred_element_type=F32)


def dot_rows(a, b):
    return lax.dot_general(a, b, (((0,), (0,)), ((), ())), preferred_element_type=F32)


def dot_cols(a, b):
    return lax.dot_general(a, b, (((1,), (1,)), ((), ())), preferred_element_type=F32)


def iota(shape, dim):
    return lax.broadcasted_iota(jnp.int32, shape, dim)


def one_hot(condition):
    return condition.astype(F32).astype(BF16)


def turned(a):
    return a.astype(F32).T.astype(BF16)


def await_bytes(ref, sem):
    pltpu.make_async_copy(ref, ref, sem).wait()


def send_to(src, dst, send_sem, recv_sem, place):
    pltpu.make_async_remote_copy(
        src_ref=src,
        dst_ref=dst,
        send_sem=send_sem,
        recv_sem=recv_sem,
        device_id=place,
        device_id_type=MESH,
    ).start()


def tile_rows(index, rows):
    return pl.ds(pl.multiple_of(index * rows, rows), rows)


def block_rows(c):
    return pl.ds(c * BLOCK, BLOCK)


def beside(lat, lon):
    for sign in (-1, 1):
        yield sign, (lat, (lon + sign + LON) % LON)


def above(lat, lon):
    for sign in (-1, 1):
        yield sign, ((lat + sign + LAT) % LAT, lon)


def cell(lat_step, lon_step):
    return (lat_step + 1) * 3 + lon_step + 1


def place_on(axis, lat, lon):
    return {"x": (lon // 8) * 2 + lat // 4, "y": lat % 4, "z": (lon // 2) % 4}[axis]


def moved_to(axis, index, lat, lon):
    if axis == "x":
        return (index % 2) * 4 + lat % 4, (index // 2) * 8 + lon % 8
    if axis == "y":
        return (lat // 4) * 4 + index, lon
    return lat, (lon // 8) * 8 + index * 2 + lon % 2


def diagonal(full):
    return jnp.concatenate(
        [
            full[h * HEAD_SIZE:(h + 1) * HEAD_SIZE, h * BLOCK:(h + 1) * BLOCK]
            for h in range(GROUP_HEADS)
        ],
        axis=0,
    )


def spread_heads(row):
    return jnp.concatenate(
        [
            jnp.broadcast_to(row[:, h * BLOCK:(h + 1) * BLOCK], (HEAD_SIZE, BLOCK))
            for h in range(GROUP_HEADS)
        ],
        axis=0,
    )


def sublayer_kernel(
    grid_ref, owner_ref, node_ref, listed_ref, gain_ref, embed_hbm, w_qkv_hbm, w_out_hbm, cot_hbm,
    mixed_ref, reduced_ref, returned_ref, flat_ref,
    embed_ref, w_qkv_ref, w_out_ref, cot_ref,
    send, recv, ids_send, ids_recv,
    halo, halo_t, latent_ref, spread_ref, keys, values, q_blocks, d_blocks,
    scores, weights, inverses, deltas, d_keyvals, attended_t, d_query_t,
    grads, from_core, held_0, from_1, held_1, from_plane, from_chips, parts, from_around,
    load_sem, send_sem, recv_sem, ids_send_sem, ids_recv_sem, halo_send_sem, halo_recv_sem,
    sum_send_sem, sum_recv_sem, parts_send_sem, parts_recv_sem, back_send_sem, back_recv_sem,
):
    lat, lon = lax.axis_index("lat"), lax.axis_index("lon")
    me = lat * LON + lon
    barrier = pltpu.get_barrier_semaphore()

    def greet(step, carry):
        other = (me + step) % DEVICES
        pl.semaphore_signal(
            barrier, inc=1, device_id=(other // LON, other % LON), device_id_type=MESH
        )
        return carry

    lax.fori_loop(1, DEVICES, greet, 0)
    loads = [
        pltpu.make_async_copy(src, dst, load_sem.at[i])
        for i, (src, dst) in enumerate(
            ((embed_hbm, embed_ref), (w_qkv_hbm, w_qkv_ref), (w_out_hbm, w_out_ref), (cot_hbm, cot_ref))
        )
    ]
    for load in loads:
        load.start()

    count, width = grid_ref.shape
    nodes = embed_ref.shape[0]
    half = width // 2
    slots = DEVICES * CAP

    owner = owner_ref[...]
    picked = (iota((DEVICES, count), 0) == owner).astype(F32)
    earlier = one_hot(iota((count, count), 0) < iota((count, count), 1))
    slot = jnp.sum(picked * dot(picked.astype(BF16), earlier), axis=0, keepdims=True).astype(jnp.int32)
    flat = owner * CAP + slot
    named = (picked * (node_ref[...] + 1).astype(F32)).astype(BF16)
    ids_send[:, 0, :] = dot_cols(named, one_hot(iota((LANES, count), 0) == slot))
    grid = grid_ref[...]

    pl.semaphore_wait(barrier, DEVICES - 1)
    for step in (0, 1, 7, 2, 6, 3, 5, 4):
        to_lat = (lat + step) % LAT
        chosen = one_hot(iota((LON * CAP, count), 0) + to_lat * (LON * CAP) == flat)
        block = dot(chosen, grid).reshape(LON, CAP, width)
        block = jnp.concatenate([block[:, :, :half], block[:, :, half:]], axis=1)
        send[tile_rows(to_lat, 2 * CAP * LON), :] = block.reshape(2 * CAP * LON, half).astype(BF16)

        def push(j, carry, to_lat=to_lat):
            to_lon = (lon + j) % LON
            other = to_lat * LON + to_lon
            send_to(ids_send.at[other], ids_recv.at[me], ids_send_sem, ids_recv_sem, (to_lat, to_lon))
            send_to(
                send.at[tile_rows(other, 2 * CAP)], recv.at[tile_rows(me, 2 * CAP)],
                send_sem, recv_sem, (to_lat, to_lon),
            )
            return carry

        lax.fori_loop(1 if step == 0 else 0, LON, push, 0)
    pltpu.make_async_copy(ids_send.at[me], ids_recv.at[me], ids_recv_sem).start()
    pltpu.make_async_copy(
        send.at[tile_rows(me, 2 * CAP)], recv.at[tile_rows(me, 2 * CAP)], recv_sem
    ).start()

    for load in loads:
        load.wait()
    cot = cot_ref[...]
    d_t = turned(dot_cols(cot, w_out_ref[...]).astype(BF16))
    q_blocks[...] = jnp.zeros_like(q_blocks)
    d_blocks[...] = jnp.zeros_like(d_blocks)

    def blocks_of(target, full_t):
        for g in range(GROUPS):
            for h in range(GROUP_HEADS):
                at = g * LANES + h * HEAD_SIZE
                target[g, h * HEAD_SIZE:(h + 1) * HEAD_SIZE, h * BLOCK:(h + 1) * BLOCK] = full_t[
                    at:at + HEAD_SIZE, :
                ]

    blocks_of(d_blocks, d_t)
    flat_ref[...] = jnp.broadcast_to(flat.astype(F32), (LANES, count)).T.astype(jnp.int32)
    listed = listed_ref[...]
    lat_step = listed // LON - lat
    lon_step = (listed % LON - lon + LON + 1) % LON - 1
    at_place = (lat_step + 1) * 3 + lon_step + 1 == iota((16, listed.shape[1]), 0)
    times = jnp.sum(at_place.astype(F32), axis=1, keepdims=True)
    bias = jnp.where(times > 0, jnp.log(jnp.maximum(times, 1.0)) * TO_LOG2, -1e30)

    await_bytes(ids_recv, ids_recv_sem)
    ids = ids_recv[:, 0, :]
    lanes = 2 * slots
    codes = dot(turned(ids)[:CAP, :], one_hot(iota((DEVICES, lanes), 0) == (iota((DEVICES, lanes), 1) >> 4)))
    mine = (iota((CAP, lanes), 1) & 7) == iota((CAP, lanes), 0)
    code = jnp.sum(jnp.where(mine, codes, 0.0), axis=0, keepdims=True).astype(jnp.int32)
    code = jnp.where(code > 0, code - 1 + nodes * ((iota((1, lanes), 1) >> 3) & 1), -1)
    members = (iota((2 * nodes, lanes), 0) == code).astype(F32)
    divisor = jnp.maximum(jnp.sum(members[:nodes, :], axis=1, keepdims=True), 1.0)
    members = members.astype(BF16)
    await_bytes(recv, recv_sem)
    sums = dot(members, recv[...])
    totals = jnp.concatenate([sums[:nodes, :], sums[nodes:, :]], axis=1)
    latent = embed_ref[...].astype(F32) + totals / divisor
    latent_ref[...] = latent
    centered = latent - jnp.mean(latent, axis=1, keepdims=True)
    inverse_std = lax.rsqrt(jnp.mean(centered * centered, axis=1, keepdims=True) + EPS)
    halo[block_rows(OWN), :] = (centered * inverse_std * gain_ref[...]).astype(BF16)
    mine = halo.at[block_rows(OWN)]
    for n, (sign, place) in enumerate(above(lat, lon)):
        send_to(
            mine, halo.at[block_rows(cell(-sign, 0))], halo_send_sem.at[n], halo_recv_sem.at[n], place
        )
    for sign, place in beside(lat, lon):
        send_to(mine, halo.at[block_rows(cell(0, -sign))], halo_send_sem.at[2], halo_recv_sem.at[2], place)

    own = halo[block_rows(OWN), :]
    own_t = turned(own)
    blocks_of(q_blocks, turned(dot(own, w_qkv_ref[:, :width]).astype(BF16)))

    def project(rows):
        keys[rows, :] = dot(halo[rows, :], w_qkv_ref[:, width:2 * width]).astype(BF16)
        values[rows, :] = dot(halo[rows, :], w_qkv_ref[:, 2 * width:]).astype(BF16)

    for n, (step, _) in enumerate(above(lat, lon)):
        block = halo.at[block_rows(cell(-step, 0))]
        await_bytes(block, halo_recv_sem.at[n])
        for sign, place in beside(lat, lon):
            send_to(
                block, halo.at[block_rows(cell(-step, -sign))],
                halo_send_sem.at[2], halo_recv_sem.at[2], place,
            )
    project(slice(OWN * BLOCK, (OWN + 1) * BLOCK))
    codes = dot(one_hot(iota((lanes, DEVICES), 1) == (iota((lanes, DEVICES), 0) >> 4)), ids.astype(BF16))
    mine = (iota((lanes, LANES), 0) & 7) == iota((lanes, LANES), 1)
    code = jnp.sum(jnp.where(mine, codes, 0.0), axis=1, keepdims=True).astype(jnp.int32)
    code = jnp.where(code > 0, code - 1 + nodes * ((iota((lanes, 1), 0) >> 3) & 1), -1)
    spread_ref[...] = one_hot(iota((lanes, 2 * nodes), 1) == code)

    await_bytes(halo.at[pl.ds(0, 6 * BLOCK)], halo_recv_sem.at[2])
    project(slice(0, OWN * BLOCK))
    project(slice((OWN + 1) * BLOCK, 9 * BLOCK))
    halo_t[...] = turned(halo[...])

    def forward(g, carry):
        cols = pl.ds(pl.multiple_of(g * LANES, LANES), LANES)
        q_block = q_blocks[g]
        highest = None
        for c in range(9):
            part = slice(c * BLOCK, (c + 1) * BLOCK)
            s = dot(keys[part, cols], q_block)
            scores[part, :] = s
            top = jnp.max(s, axis=0, keepdims=True) * (SCALE * TO_LOG2) + bias[c:c + 1, :]
            highest = top if c == 0 else jnp.maximum(highest, top)
        total = jnp.zeros((1, COLUMNS), F32)
        for c in range(9):
            part = slice(c * BLOCK, (c + 1) * BLOCK)
            w = jnp.exp2(scores[part, :] * (SCALE * TO_LOG2) - (highest - bias[c:c + 1, :]))
            total = total + jnp.sum(w, axis=0, keepdims=True)
            weights[g, part, :] = w.astype(BF16)
        inverse = 1.0 / total
        out_group = diagonal(dot_rows(values[:, cols], weights[g])) * spread_heads(inverse)
        attended_t[cols, :] = out_group.astype(BF16)
        product = out_group * diagonal(d_blocks[g].astype(F32))
        delta = jnp.concatenate(
            [
                jnp.sum(product[h * HEAD_SIZE:(h + 1) * HEAD_SIZE, :], axis=0, keepdims=True)
                for h in range(GROUP_HEADS)
            ],
            axis=1,
        )
        inverses[g] = jnp.broadcast_to(inverse, (8, COLUMNS))
        deltas[g] = jnp.broadcast_to(delta, (8, COLUMNS))
        return carry

    lax.fori_loop(0, GROUPS, forward, 0)
    grad_w_out = dot(attended_t[...], cot).astype(BF16)
    for g in range(GROUPS):
        grads[4 * g + 3] = grad_w_out[:, g * LANES:(g + 1) * LANES]

    core = lon % 2
    twin = (lat, lon - core + (1 - core))
    core_rows = tile_rows(core, ROWS_CORE)
    places = {axis: place_on(axis, lat, lon) for axis in "xyz"}

    def group_units(g):
        return pl.ds(4 * g, 4)

    def others(axis):
        for k in range(1, 4):
            t = (places[axis] + k) % 4
            yield k - 1, t, moved_to(axis, t, lat, lon)

    def sum_core(g):
        send_to(
            grads.at[group_units(g), tile_rows(1 - core, ROWS_CORE)], from_core.at[group_units(g)],
            sum_send_sem.at[g, 0], sum_recv_sem.at[g, 0], twin,
        )

    def add_core(g):
        units = group_units(g)
        await_bytes(from_core.at[units], sum_recv_sem.at[g, 0])
        held_0[units] = (grads[units, core_rows, :].astype(F32) + from_core[units].astype(F32)).astype(BF16)

    def sum_1(g):
        add_core(g)
        units = group_units(g)
        for k, t, place in others(FIRST_AXES[g]):
            send_to(
                held_0.at[units, tile_rows(t, ROWS_1)], from_1.at[units, pl.ds(k * ROWS_1, ROWS_1)],
                sum_send_sem.at[g, 1], sum_recv_sem.at[g, 1], place,
            )

    def plane_index(g):
        b, c = (axis for axis in "xyz" if axis != FIRST_AXES[g])
        return places[b] * 4 + places[c]

    def plane_place(g, j):
        b, c = (axis for axis in "xyz" if axis != FIRST_AXES[g])
        return moved_to(c, j % 4, *moved_to(b, j // 4, lat, lon))

    def sum_plane(g):
        units = group_units(g)
        await_bytes(from_1.at[units], sum_recv_sem.at[g, 1])
        total = held_0[units, tile_rows(places[FIRST_AXES[g]], ROWS_1), :].astype(F32)
        for k in range(3):
            total = total + from_1[units, pl.ds(k * ROWS_1, ROWS_1), :].astype(F32)
        held_1[units] = total.astype(BF16)
        mine = plane_index(g)

        def push_piece(k, carry):
            j = (mine + k) % 16
            send_to(
                held_1.at[4 * g + j // 4, tile_rows(j % 4, ROWS_2)], from_plane.at[g, mine],
                sum_send_sem.at[g, 2], sum_recv_sem.at[g, 2], plane_place(g, j),
            )
            return carry

        lax.fori_loop(1, 16, push_piece, 0)
        from_plane[g, mine] = held_1[4 * g + mine // 4, tile_rows(mine % 4, ROWS_2), :]

    def back_plane(g):
        await_bytes(from_plane.at[g, pl.ds(0, 15)], sum_recv_sem.at[g, 2])
        mine = plane_index(g)
        row = core * ROWS_CORE + places[FIRST_AXES[g]] * ROWS_1 + (mine % 4) * ROWS_2
        piece = reduced_ref.at[4 * g + mine // 4, pl.ds(pl.multiple_of(row, ROWS_2), ROWS_2)]
        piece[...] = jnp.sum(from_plane[g].astype(F32), axis=0).astype(BF16)

        def push_sum(k, carry):
            send_to(
                piece, piece, sum_send_sem.at[g, 3], sum_recv_sem.at[g, 3],
                plane_place(g, (mine + k) % 16),
            )
            return carry

        lax.fori_loop(1, 16, push_sum, 0)

    def back_1(g):
        await_bytes(from_plane.at[g, pl.ds(0, 15)], sum_recv_sem.at[g, 3])
        row = core * ROWS_CORE + places[FIRST_AXES[g]] * ROWS_1
        piece = reduced_ref.at[group_units(g), pl.ds(pl.multiple_of(row, ROWS_1), ROWS_1)]
        for k, t, place in others(FIRST_AXES[g]):
            send_to(piece, piece, sum_send_sem.at[g, 4], sum_recv_sem.at[g, 4], place)

    def back_core(g):
        await_bytes(from_1.at[group_units(g)], sum_recv_sem.at[g, 4])
        piece = reduced_ref.at[group_units(g), core_rows]
        send_to(piece, piece, sum_send_sem.at[g, 5], sum_recv_sem.at[g, 5], twin)

    chip = places["x"] * 16 + places["y"] * 4 + places["z"]

    def place_of(i):
        x, y, z = i // 16, (i // 4) % 4, i % 4
        return (x % 2) * 4 + y, (x // 2) * 8 + z * 2 + core

    def piece_of(i):
        return i // 16, tile_rows(i % 16, ROWS_2)

    def scatter(g):
        add_core(g)

        def push_piece(k, carry):
            i = (chip + k) % CHIPS
            unit, rows = piece_of(i)
            send_to(
                held_0.at[4 * g + unit, rows], from_chips.at[chip],
                sum_send_sem.at[g, 1], sum_recv_sem.at[g, 1], place_of(i),
            )
            return carry

        lax.fori_loop(1, CHIPS, push_piece, 0)
        unit, rows = piece_of(chip)
        from_chips[chip] = held_0[4 * g + unit, rows, :]

    def gather(g):
        await_bytes(from_chips.at[pl.ds(0, CHIPS - 1)], sum_recv_sem.at[g, 1])
        total = jnp.sum(from_chips[...].astype(F32), axis=0)
        unit, rows = piece_of(chip)
        row = core * ROWS_CORE + (chip % 16) * ROWS_2
        piece = reduced_ref.at[4 * g + unit, pl.ds(pl.multiple_of(row, ROWS_2), ROWS_2)]
        piece[...] = total.astype(BF16)

        def push_sum(k, carry):
            send_to(
                piece, piece, sum_send_sem.at[g, 2], sum_recv_sem.at[g, 2], place_of((chip + k) % CHIPS)
            )
            return carry

        lax.fori_loop(1, CHIPS, push_sum, 0)

    def gather_core(g):
        await_bytes(from_chips.at[pl.ds(0, CHIPS - 1)], sum_recv_sem.at[g, 2])
        piece = reduced_ref.at[group_units(g), core_rows]
        send_to(piece, piece, sum_send_sem.at[g, 5], sum_recv_sem.at[g, 5], twin)

    def sum_end(g):
        units = group_units(g)
        await_bytes(from_core.at[units], sum_recv_sem.at[g, 5])
        await_bytes(from_core.at[units], sum_send_sem.at[g, 0])
        await_bytes(from_core.at[units], sum_send_sem.at[g, 5])
        if g < len(FIRST_AXES):
            await_bytes(from_1.at[units], sum_send_sem.at[g, 1])
            await_bytes(from_plane.at[g, pl.ds(0, 15)], sum_send_sem.at[g, 2])
            await_bytes(from_plane.at[g, pl.ds(0, 15)], sum_send_sem.at[g, 3])
            await_bytes(from_1.at[units], sum_send_sem.at[g, 4])
        else:
            for level in (1, 2):
                await_bytes(from_chips.at[pl.ds(0, CHIPS - 1)], sum_send_sem.at[g, level])

    for g in range(GROUPS):
        cols = slice(g * LANES, (g + 1) * LANES)
        q_block, d_block = q_blocks[g].astype(F32), d_blocks[g]
        inverse, delta = inverses[g, 0:1, :], deltas[g, 0:1, :]
        d_scaled = (d_block.astype(F32) * inverse).astype(BF16)
        d_values = dot_cols(weights[g], d_scaled).astype(BF16)
        d_keyvals[:, width + g * LANES:width + (g + 1) * LANES] = d_values
        if g > 0:
            sum_1(g - 1)
        for c in range(9):
            part = slice(c * BLOCK, (c + 1) * BLOCK)
            d = dot(values[part, cols], d_block)
            weights[g, part, :] = (weights[g, part, :].astype(F32) * (d - delta)).astype(BF16)
        back = inverse * SCALE
        d_keys = dot_cols(weights[g], (q_block * back).astype(BF16)).astype(BF16)
        d_keyvals[:, cols] = d_keys
        d_query = (diagonal(dot_rows(keys[:, cols], weights[g])) * spread_heads(back)).astype(BF16)
        d_query_t[cols, :] = d_query
        grads[4 * g] = dot_cols(own_t, d_query).astype(BF16)
        both = dot(halo_t[...], jnp.concatenate([d_keys, d_values], axis=1)).astype(BF16)
        grads[4 * g + 1] = both[:, :LANES]
        grads[4 * g + 2] = both[:, LANES:]
        sum_core(g)
    sum_plane(0)

    def node_part(c):
        return dot_cols(d_keyvals[block_rows(c), :], w_qkv_ref[:, width:])

    for lat_step in (-1, 1, 0):
        for n, (sign, place) in enumerate(beside(lat, lon)):
            slot_rows = pl.ds((2 * (lat_step % 3) + n) * BLOCK, BLOCK)
            parts[slot_rows, :] = node_part(cell(lat_step, sign)).astype(BF16)
            send_to(
                parts.at[slot_rows], from_around.at[slot_rows],
                parts_send_sem.at[lat_step % 3], parts_recv_sem.at[lat_step % 3], place,
            )
    scatter(3)
    sum_plane(1)
    d_normed = node_part(OWN) + dot_cols(turned(d_query_t[...]), w_qkv_ref[:, :width])
    mixed_ref[...] = (latent_ref[...] + dot_rows(attended_t[...], w_out_ref[...])).astype(BF16)
    latent = latent_ref[...]
    centered = latent - jnp.mean(latent, axis=1, keepdims=True)
    inverse_std = lax.rsqrt(jnp.mean(centered * centered, axis=1, keepdims=True) + EPS)
    normalized = centered * inverse_std
    sum_plane(2)
    for n, (sign, place) in enumerate(above(lat, lon)):
        at = sign % 3
        part = node_part(cell(sign, 0))
        arrived = from_around.at[pl.ds(2 * at * BLOCK, 2 * BLOCK)]
        await_bytes(arrived, parts_recv_sem.at[at])
        part = part + arrived[:BLOCK, :].astype(F32) + arrived[BLOCK:, :].astype(F32)
        slot_rows = pl.ds((6 + n) * BLOCK, BLOCK)
        parts[slot_rows, :] = part.astype(BF16)
        send_to(
            parts.at[slot_rows], from_around.at[slot_rows], parts_send_sem.at[3], parts_recv_sem.at[3], place
        )
    for g in range(3):
        back_plane(g)
    gather(3)
    await_bytes(from_around.at[pl.ds(0, 2 * BLOCK)], parts_recv_sem.at[0])
    await_bytes(from_around.at[pl.ds(6 * BLOCK, 2 * BLOCK)], parts_recv_sem.at[3])
    for n in (0, 1, 6, 7):
        d_normed = d_normed + from_around[block_rows(n), :].astype(F32)
    scaled = d_normed * gain_ref[...]
    d_latent = cot.astype(F32) + inverse_std * (
        scaled
        - jnp.mean(scaled, axis=1, keepdims=True)
        - normalized * jnp.mean(scaled * normalized, axis=1, keepdims=True)
    )
    node_grad = (d_latent / divisor).astype(BF16)
    stacked = jnp.concatenate([node_grad[:, :half], node_grad[:, half:]], axis=0)

    await_bytes(send.at[pl.ds(0, (DEVICES - 1) * 2 * CAP)], send_sem)
    for turn, step in enumerate((0, 1, 7, 2, 6, 3, 5, 4)):
        if turn == 2:
            for g in range(3):
                back_1(g)
        to_lat = (lat + step) % LAT
        rows = tile_rows(to_lat, 2 * CAP * LON)
        send[rows, :] = dot(spread_ref[rows, :], stacked).astype(BF16)

        def push_back(j, carry, to_lat=to_lat):
            to_lon = (lon + j) % LON
            other = to_lat * LON + to_lon
            send_to(
                send.at[tile_rows(other, 2 * CAP)], returned_ref.at[tile_rows(me, 2 * CAP)],
                back_send_sem, back_recv_sem, (to_lat, to_lon),
            )
            return carry

        lax.fori_loop(1 if step == 0 else 0, LON, push_back, 0)
    pltpu.make_async_copy(
        send.at[tile_rows(me, 2 * CAP)], returned_ref.at[tile_rows(me, 2 * CAP)], back_recv_sem
    ).start()
    gather_core(3)
    for g in range(3):
        back_core(g)
    for g in range(GROUPS):
        sum_end(g)
    await_bytes(ids_send.at[pl.ds(0, DEVICES - 1)], ids_send_sem)
    for n, blocks in enumerate((1, 1, 6)):
        await_bytes(halo.at[pl.ds(0, blocks * BLOCK)], halo_send_sem.at[n])
    for n in range(4):
        await_bytes(parts.at[pl.ds(0, 2 * BLOCK)], parts_send_sem.at[n])
    await_bytes(send.at[pl.ds(0, (DEVICES - 1) * 2 * CAP)], back_send_sem)
    await_bytes(returned_ref, back_recv_sem)


def sublayer(grid_rows, owner, node, embed, listed, gain, w_qkv, w_out, cotangent):
    count, width = grid_rows.shape
    nodes = embed.shape[0]
    lanes = 2 * DEVICES * CAP
    pool = 9 * nodes
    units, early = 4 * GROUPS, 4 * len(FIRST_AXES)
    vmem, dma = pltpu.VMEM, pltpu.SemaphoreType.DMA
    return pl.pallas_call(
        sublayer_kernel,
        name="sublayer",
        out_shape=(
            jax.ShapeDtypeStruct((nodes, width), BF16),
            jax.ShapeDtypeStruct((units, width, LANES), BF16),
            jax.ShapeDtypeStruct((lanes, width // 2), BF16),
            jax.ShapeDtypeStruct((count, LANES), jnp.int32),
        ),
        in_specs=[pl.BlockSpec(memory_space=vmem)] * 5 + [pl.BlockSpec(memory_space=pl.ANY)] * 4,
        out_specs=[pl.BlockSpec(memory_space=vmem)] * 4,
        scratch_shapes=[
            vmem((nodes, width), BF16),
            vmem(w_qkv.shape, BF16),
            vmem(w_out.shape, BF16),
            vmem((nodes, width), BF16),
            vmem((lanes, width // 2), BF16),
            vmem((lanes, width // 2), BF16),
            vmem((DEVICES, 1, LANES), F32),
            vmem((DEVICES, 1, LANES), F32),
            vmem((pool, width), BF16),
            vmem((width, pool), BF16),
            vmem((nodes, width), F32),
            vmem((lanes, 2 * nodes), BF16),
            vmem((pool, width), BF16),
            vmem((pool, width), BF16),
            vmem((GROUPS, LANES, COLUMNS), BF16),
            vmem((GROUPS, LANES, COLUMNS), BF16),
            vmem((pool, COLUMNS), F32),
            vmem((GROUPS, pool, COLUMNS), BF16),
            vmem((GROUPS, 8, COLUMNS), F32),
            vmem((GROUPS, 8, COLUMNS), F32),
            vmem((pool, 2 * width), BF16),
            vmem((width, BLOCK), BF16),
            vmem((width, BLOCK), BF16),
            vmem((units, width, LANES), BF16),
            vmem((units, ROWS_CORE, LANES), BF16),
            vmem((units, ROWS_CORE, LANES), BF16),
            vmem((early, 3 * ROWS_1, LANES), BF16),
            vmem((early, ROWS_1, LANES), BF16),
            vmem((len(FIRST_AXES), 16, ROWS_2, LANES), BF16),
            vmem((CHIPS, ROWS_2, LANES), BF16),
            vmem((8 * nodes, width), BF16),
            vmem((8 * nodes, width), BF16),
            dma((4,)),
        ] + [dma] * 4 + [dma((3,))] * 2 + [dma((GROUPS, 6))] * 2 + [dma((4,))] * 2 + [dma] * 2,
        compiler_params=pltpu.CompilerParams(
            collective_id=0, has_side_effects=True, vmem_limit_bytes=VMEM_LIMIT
        ),
    )(
        grid_rows, owner.reshape(1, count), node.reshape(1, count), listed, gain.reshape(1, width),
        embed, w_qkv, w_out, cotangent,
    )


def finish_kernel(
    reduced_ref, returned_ref, flat_ref, w_qkv_ref, gain_ref, mixed_in_ref,
    mixed_ref, grad_grid_ref, grad_w_qkv_ref, grad_w_out_ref, grad_gain_ref,
):
    count, width = grad_grid_ref.shape
    half = width // 2
    slots = DEVICES * CAP
    mixed_ref[...] = mixed_in_ref[...]
    product = jnp.zeros((width, LANES), F32)
    for g in range(GROUPS):
        for m in range(3):
            cols = slice(m * width + g * LANES, m * width + (g + 1) * LANES)
            grad = reduced_ref[4 * g + m].astype(F32)
            grad_w_qkv_ref[:, cols] = grad
            product = product + grad * w_qkv_ref[:, cols].astype(F32)
        grad_w_out_ref[:, g * LANES:(g + 1) * LANES] = reduced_ref[4 * g + 3].astype(F32)
    grad_gain_ref[...] = jnp.sum(product.T, axis=0, keepdims=True) / gain_ref[...]
    back = returned_ref[...].astype(F32).reshape(DEVICES, 2 * CAP, half)
    back = jnp.concatenate([back[:, :CAP, :], back[:, CAP:, :]], axis=2)
    back = back.reshape(slots, width).astype(BF16)
    chosen = one_hot(iota((count, slots), 1) == flat_ref[:, 0:1])
    grad_grid_ref[...] = dot(chosen, back).astype(BF16)


def finish(reduced, returned, flat, w_qkv, gain, mixed):
    width = w_qkv.shape[0]
    count = flat.shape[0]
    return pl.pallas_call(
        finish_kernel,
        name="finish",
        out_shape=(
            jax.ShapeDtypeStruct(mixed.shape, BF16),
            jax.ShapeDtypeStruct((count, width), BF16),
            jax.ShapeDtypeStruct((width, 3 * width), F32),
            jax.ShapeDtypeStruct((width, width), F32),
            jax.ShapeDtypeStruct((1, width), F32),
        ),
        in_specs=[pl.BlockSpec(memory_space=pltpu.VMEM)] * 6,
        out_specs=[pl.BlockSpec(memory_space=pltpu.VMEM)] * 5,
        compiler_params=pltpu.CompilerParams(vmem_limit_bytes=VMEM_LIMIT),
    )(reduced, returned, flat, w_qkv, gain.reshape(1, width), mixed)


def local(
    grid_rows, dest_owner, dest_node, node_embed, neighbours, norm_gain, w_qkv, w_out, cotangent
):
    mixed, reduced, returned, flat = sublayer(
        grid_rows, dest_owner, dest_node, node_embed, neighbours, norm_gain, w_qkv, w_out, cotangent
    )
    mixed, grad_grid, grad_w_qkv, grad_w_out, grad_gain = finish(
        reduced, returned, flat, w_qkv, norm_gain, mixed
    )
    return (mixed, grad_grid, grad_w_qkv, grad_w_out, grad_gain.reshape(norm_gain.shape))


def solution(mesh):
    split = P(("lat", "lon"), None)
    in_specs = (split, split, P(("lat", "lon")), split, split, P(), P(), P(), split)
    out_specs = (split, split, P(), P(), P())
    return jax.shard_map(local, mesh=mesh, in_specs=in_specs, out_specs=out_specs, check_vma=False)
```

```python
import math

import jax
import jax.numpy as jnp
from jax import lax
from jax.experimental import pallas as pl
from jax.experimental.pallas import tpu as pltpu
from jax.sharding import PartitionSpec as P

HEADS = 16
HEAD_SIZE = 32
BLOCK = 128
LANES = 128
LAT = 8
LON = 16
DEVICES = LAT * LON
OWN = 4
CAP = 8
GROUPS = 4
GROUP_HEADS = LANES // HEAD_SIZE
COLUMNS = GROUP_HEADS * BLOCK
SCALE = HEAD_SIZE ** (-0.5)
TO_LOG2 = math.log2(math.e)
EPS = 1e-05
VMEM_LIMIT = 56 * 1024 * 1024
MESH = pl.DeviceIdType.MESH
F32, BF16 = jnp.float32, jnp.bfloat16
FIRST_AXES = "xyz"
CHIPS = DEVICES // 2
ROWS_CORE, ROWS_1, ROWS_2 = 256, 64, 16


def dot(a, b):
    return jnp.dot(a, b, preferred_element_type=F32)


def dot_rows(a, b):
    return lax.dot_general(a, b, (((0,), (0,)), ((), ())), preferred_element_type=F32)


def dot_cols(a, b):
    return lax.dot_general(a, b, (((1,), (1,)), ((), ())), preferred_element_type=F32)


def iota(shape, dim):
    return lax.broadcasted_iota(jnp.int32, shape, dim)


def one_hot(condition):
    return condition.astype(F32).astype(BF16)


def turned(a):
    return a.astype(F32).T.astype(BF16)


def await_bytes(ref, sem):
    pltpu.make_async_copy(ref, ref, sem).wait()


def send_to(src, dst, send_sem, recv_sem, place):
    pltpu.make_async_remote_copy(
        src_ref=src,
        dst_ref=dst,
        send_sem=send_sem,
        recv_sem=recv_sem,
        device_id=place,
        device_id_type=MESH,
    ).start()


def tile_rows(index, rows):
    return pl.ds(pl.multiple_of(index * rows, rows), rows)


def block_rows(c):
    return pl.ds(c * BLOCK, BLOCK)


def beside(lat, lon):
    for sign in (-1, 1):
        yield sign, (lat, (lon + sign + LON) % LON)


def above(lat, lon):
    for sign in (-1, 1):
        yield sign, ((lat + sign + LAT) % LAT, lon)


def cell(lat_step, lon_step):
    return (lat_step + 1) * 3 + lon_step + 1


def place_on(axis, lat, lon):
    return {"x": (lon // 8) * 2 + lat // 4, "y": lat % 4, "z": (lon // 2) % 4}[axis]


def moved_to(axis, index, lat, lon):
    if axis == "x":
        return (index % 2) * 4 + lat % 4, (index // 2) * 8 + lon % 8
    if axis == "y":
        return (lat // 4) * 4 + index, lon
    return lat, (lon // 8) * 8 + index * 2 + lon % 2


def diagonal(full):
    return jnp.concatenate(
        [
            full[h * HEAD_SIZE:(h + 1) * HEAD_SIZE, h * BLOCK:(h + 1) * BLOCK]
            for h in range(GROUP_HEADS)
        ],
        axis=0,
    )


def spread_heads(row):
    return jnp.concatenate(
        [
            jnp.broadcast_to(row[:, h * BLOCK:(h + 1) * BLOCK], (HEAD_SIZE, BLOCK))
            for h in range(GROUP_HEADS)
        ],
        axis=0,
    )


def sublayer_kernel(
    owner_ref, node_ref, listed_ref, gain_ref, grid_hbm, embed_hbm, w_qkv_hbm, w_out_hbm, cot_hbm,
    mixed_out, reduced_out, returned_ref, flat_out,
    mixed_ref, reduced_ref, flat_ref, grid_ref, embed_ref, w_qkv_ref, w_out_ref, cot_ref,
    send, recv, ids_send, ids_recv,
    halo, halo_t, latent_ref, spread_ref, keys, values, q_blocks, d_blocks,
    scores, tops, weights, inverses, deltas, d_keyvals, attended_t, d_query_t,
    grads, from_core, held_0, from_1, held_1, from_plane, from_chips, parts, from_around,
    load_sem, store_sem, send_sem, recv_sem, ids_send_sem, ids_recv_sem, halo_send_sem, halo_recv_sem,
    sum_send_sem, sum_recv_sem, parts_send_sem, parts_recv_sem, back_send_sem, back_recv_sem,
):
    lat, lon = lax.axis_index("lat"), lax.axis_index("lon")
    me = lat * LON + lon
    barrier = pltpu.get_barrier_semaphore()

    def greet(step, carry):
        other = (me + step) % DEVICES
        pl.semaphore_signal(
            barrier, inc=1, device_id=(other // LON, other % LON), device_id_type=MESH
        )
        return carry

    lax.fori_loop(1, DEVICES, greet, 0)
    loads = [
        pltpu.make_async_copy(src, dst, load_sem.at[i])
        for i, (src, dst) in enumerate(
            ((grid_hbm, grid_ref), (embed_hbm, embed_ref), (w_qkv_hbm, w_qkv_ref), (w_out_hbm, w_out_ref), (cot_hbm, cot_ref))
        )
    ]
    for load in loads:
        load.start()

    count, width = grid_ref.shape
    nodes = embed_ref.shape[0]
    half = width // 2
    slots = DEVICES * CAP

    owner = owner_ref[...]
    picked = (iota((DEVICES, count), 0) == owner).astype(F32)
    earlier = one_hot(iota((count, count), 0) < iota((count, count), 1))
    slot = jnp.sum(picked * dot(picked.astype(BF16), earlier), axis=0, keepdims=True).astype(jnp.int32)
    flat = owner * CAP + slot
    named = (picked * (node_ref[...] + 1).astype(F32)).astype(BF16)
    ids_send[:, 0, :] = dot_cols(named, one_hot(iota((LANES, count), 0) == slot))
    loads[0].wait()
    grid = grid_ref[...]

    for k in range(LAT):
        chosen = one_hot(iota((LON * CAP, count), 0) + k * (LON * CAP) == flat)
        block = dot(chosen, grid).reshape(LON, CAP, width)
        block = jnp.concatenate([block[:, :, :half], block[:, :, half:]], axis=1)
        send[pl.ds(k * 2 * CAP * LON, 2 * CAP * LON), :] = block.reshape(2 * CAP * LON, half).astype(BF16)
    pl.semaphore_wait(barrier, DEVICES - 1)

    def push(step, carry):
        other = (me + 53 * step) % DEVICES
        place = (other // LON, other % LON)
        send_to(ids_send.at[other], ids_recv.at[me], ids_send_sem, ids_recv_sem, place)
        send_to(
            send.at[tile_rows(other, 2 * CAP)], recv.at[tile_rows(me, 2 * CAP)], send_sem, recv_sem, place
        )
        return carry

    lax.fori_loop(1, DEVICES, push, 0)
    pltpu.make_async_copy(ids_send.at[me], ids_recv.at[me], ids_recv_sem).start()
    pltpu.make_async_copy(
        send.at[tile_rows(me, 2 * CAP)], recv.at[tile_rows(me, 2 * CAP)], recv_sem
    ).start()

    for load in loads[1:]:
        load.wait()
    cot = cot_ref[...]
    d_t = turned(dot_cols(cot, w_out_ref[...]).astype(BF16))
    q_blocks[...] = jnp.zeros_like(q_blocks)
    d_blocks[...] = jnp.zeros_like(d_blocks)

    def blocks_of(target, full_t):
        for g in range(GROUPS):
            for h in range(GROUP_HEADS):
                at = g * LANES + h * HEAD_SIZE
                target[g, h * HEAD_SIZE:(h + 1) * HEAD_SIZE, h * BLOCK:(h + 1) * BLOCK] = full_t[
                    at:at + HEAD_SIZE, :
                ]

    blocks_of(d_blocks, d_t)
    flat_ref[...] = jnp.broadcast_to(flat.astype(F32), (LANES, count)).T.astype(jnp.int32)
    listed = listed_ref[...]
    lat_step = listed // LON - lat
    lon_step = (listed % LON - lon + LON + 1) % LON - 1
    at_place = (lat_step + 1) * 3 + lon_step + 1 == iota((16, listed.shape[1]), 0)
    times = jnp.sum(at_place.astype(F32), axis=1, keepdims=True)
    bias = jnp.where(times > 0, jnp.log(jnp.maximum(times, 1.0)) * TO_LOG2, -1e30)

    await_bytes(ids_recv, ids_recv_sem)
    ids = ids_recv[:, 0, :]
    lanes = 2 * slots
    codes = dot(turned(ids)[:CAP, :], one_hot(iota((DEVICES, lanes), 0) == (iota((DEVICES, lanes), 1) >> 4)))
    mine = (iota((CAP, lanes), 1) & 7) == iota((CAP, lanes), 0)
    code = jnp.sum(jnp.where(mine, codes, 0.0), axis=0, keepdims=True).astype(jnp.int32)
    code = jnp.where(code > 0, code - 1 + nodes * ((iota((1, lanes), 1) >> 3) & 1), -1)
    members = (iota((2 * nodes, lanes), 0) == code).astype(F32)
    divisor = jnp.maximum(jnp.sum(members[:nodes, :], axis=1, keepdims=True), 1.0)
    members = members.astype(BF16)
    await_bytes(recv, recv_sem)
    sums = dot(members, recv[...])
    totals = jnp.concatenate([sums[:nodes, :], sums[nodes:, :]], axis=1)
    latent = embed_ref[...].astype(F32) + totals / divisor
    latent_ref[...] = latent
    centered = latent - jnp.mean(latent, axis=1, keepdims=True)
    inverse_std = lax.rsqrt(jnp.mean(centered * centered, axis=1, keepdims=True) + EPS)
    halo[block_rows(OWN), :] = (centered * inverse_std * gain_ref[...]).astype(BF16)
    mine = halo.at[block_rows(OWN)]
    for n, (sign, place) in enumerate(above(lat, lon)):
        send_to(
            mine, halo.at[block_rows(cell(-sign, 0))], halo_send_sem.at[n], halo_recv_sem.at[n], place
        )
    for sign, place in beside(lat, lon):
        send_to(mine, halo.at[block_rows(cell(0, -sign))], halo_send_sem.at[2], halo_recv_sem.at[2], place)

    own = halo[block_rows(OWN), :]
    own_t = turned(own)
    blocks_of(q_blocks, turned(dot(own, w_qkv_ref[:, :width]).astype(BF16)))

    def take(c):
        rows = block_rows(c)
        block = halo[rows, :]
        keys[rows, :] = dot(block, w_qkv_ref[:, width:2 * width]).astype(BF16)
        values[rows, :] = dot(block, w_qkv_ref[:, 2 * width:]).astype(BF16)
        halo_t[:, rows] = turned(block)
        for g in range(GROUPS):
            s = dot(keys[rows, g * LANES:(g + 1) * LANES], q_blocks[g])
            scores[g, rows, :] = s
            tops[g, c:c + 1, :] = jnp.max(s, axis=0, keepdims=True) * (SCALE * TO_LOG2) + bias[c:c + 1, :]

    take(OWN)
    for n, (step, _) in enumerate(above(lat, lon)):
        block = halo.at[block_rows(cell(-step, 0))]
        await_bytes(block, halo_recv_sem.at[n])
        for sign, place in beside(lat, lon):
            send_to(
                block, halo.at[block_rows(cell(-step, -sign))],
                halo_send_sem.at[3], halo_recv_sem.at[3], place,
            )
    await_bytes(halo.at[pl.ds(0, 2 * BLOCK)], halo_recv_sem.at[2])
    for c in (1, 3, 5, 7):
        take(c)
    codes = dot(one_hot(iota((lanes, DEVICES), 1) == (iota((lanes, DEVICES), 0) >> 4)), ids.astype(BF16))
    mine = (iota((lanes, LANES), 0) & 7) == iota((lanes, LANES), 1)
    code = jnp.sum(jnp.where(mine, codes, 0.0), axis=1, keepdims=True).astype(jnp.int32)
    code = jnp.where(code > 0, code - 1 + nodes * ((iota((lanes, 1), 0) >> 3) & 1), -1)
    spread_ref[...] = one_hot(iota((lanes, 2 * nodes), 1) == code)

    await_bytes(halo.at[pl.ds(0, 4 * BLOCK)], halo_recv_sem.at[3])
    for c in (0, 2, 6, 8):
        take(c)

    def forward(g, carry):
        cols = slice(g * LANES, (g + 1) * LANES)
        highest = jnp.max(tops[g, 0:9, :], axis=0, keepdims=True)
        total = jnp.zeros((1, COLUMNS), F32)
        for c in range(9):
            part = slice(c * BLOCK, (c + 1) * BLOCK)
            w = jnp.exp2(scores[g, part, :] * (SCALE * TO_LOG2) - (highest - bias[c:c + 1, :]))
            total = total + jnp.sum(w, axis=0, keepdims=True)
            weights[g, part, :] = w.astype(BF16)
        inverse = 1.0 / total
        out_group = diagonal(dot_rows(values[:, cols], weights[g])) * spread_heads(inverse)
        attended_t[cols, :] = out_group.astype(BF16)
        product = out_group * diagonal(d_blocks[g].astype(F32))
        delta = jnp.concatenate(
            [
                jnp.sum(product[h * HEAD_SIZE:(h + 1) * HEAD_SIZE, :], axis=0, keepdims=True)
                for h in range(GROUP_HEADS)
            ],
            axis=1,
        )
        inverses[g] = jnp.broadcast_to(inverse, (8, COLUMNS))
        deltas[g] = jnp.broadcast_to(delta, (8, COLUMNS))
        return carry

    for g in range(GROUPS):
        forward(g, 0)
    grad_w_out = dot(attended_t[...], cot).astype(BF16)
    for g in range(GROUPS):
        grads[4 * g + 3] = grad_w_out[:, g * LANES:(g + 1) * LANES]

    core = lon % 2
    twin = (lat, lon - core + (1 - core))
    core_rows = tile_rows(core, ROWS_CORE)
    places = {axis: place_on(axis, lat, lon) for axis in "xyz"}

    def group_units(g):
        return pl.ds(4 * g, 4)

    def others(axis):
        for k in range(1, 4):
            t = (places[axis] + k) % 4
            yield k - 1, t, moved_to(axis, t, lat, lon)

    def sum_core(g):
        send_to(
            grads.at[group_units(g), tile_rows(1 - core, ROWS_CORE)], from_core.at[group_units(g)],
            sum_send_sem.at[g, 0], sum_recv_sem.at[g, 0], twin,
        )

    def add_core(g):
        units = group_units(g)
        await_bytes(from_core.at[units], sum_recv_sem.at[g, 0])
        held_0[units] = (grads[units, core_rows, :].astype(F32) + from_core[units].astype(F32)).astype(BF16)

    def sum_1(g):
        add_core(g)
        units = group_units(g)
        for k, t, place in others(FIRST_AXES[g]):
            send_to(
                held_0.at[units, tile_rows(t, ROWS_1)], from_1.at[units, pl.ds(k * ROWS_1, ROWS_1)],
                sum_send_sem.at[g, 1], sum_recv_sem.at[g, 1], place,
            )

    def plane_index(g):
        b, c = (axis for axis in "xyz" if axis != FIRST_AXES[g])
        return places[b] * 4 + places[c]

    def plane_place(g, j):
        b, c = (axis for axis in "xyz" if axis != FIRST_AXES[g])
        return moved_to(c, j % 4, *moved_to(b, j // 4, lat, lon))

    def sum_plane(g):
        units = group_units(g)
        await_bytes(from_1.at[units], sum_recv_sem.at[g, 1])
        total = held_0[units, tile_rows(places[FIRST_AXES[g]], ROWS_1), :].astype(F32)
        for k in range(3):
            total = total + from_1[units, pl.ds(k * ROWS_1, ROWS_1), :].astype(F32)
        held_1[units] = total.astype(BF16)
        mine = plane_index(g)

        def push_piece(k, carry):
            j = (mine + k) % 16
            send_to(
                held_1.at[4 * g + j // 4, tile_rows(j % 4, ROWS_2)], from_plane.at[g, mine],
                sum_send_sem.at[g, 2], sum_recv_sem.at[g, 2], plane_place(g, j),
            )
            return carry

        lax.fori_loop(1, 16, push_piece, 0)
        from_plane[g, mine] = held_1[4 * g + mine // 4, tile_rows(mine % 4, ROWS_2), :]

    def back_plane(g):
        await_bytes(from_plane.at[g, pl.ds(0, 15)], sum_recv_sem.at[g, 2])
        mine = plane_index(g)
        row = core * ROWS_CORE + places[FIRST_AXES[g]] * ROWS_1 + (mine % 4) * ROWS_2
        piece = reduced_ref.at[4 * g + mine // 4, pl.ds(pl.multiple_of(row, ROWS_2), ROWS_2)]
        piece[...] = jnp.sum(from_plane[g].astype(F32), axis=0).astype(BF16)

        def push_sum(k, carry):
            send_to(
                piece, piece, sum_send_sem.at[g, 3], sum_recv_sem.at[g, 3],
                plane_place(g, (mine + k) % 16),
            )
            return carry

        lax.fori_loop(1, 16, push_sum, 0)

    def back_1(g):
        await_bytes(from_plane.at[g, pl.ds(0, 15)], sum_recv_sem.at[g, 3])
        row = core * ROWS_CORE + places[FIRST_AXES[g]] * ROWS_1
        piece = reduced_ref.at[group_units(g), pl.ds(pl.multiple_of(row, ROWS_1), ROWS_1)]
        for k, t, place in others(FIRST_AXES[g]):
            send_to(piece, piece, sum_send_sem.at[g, 4], sum_recv_sem.at[g, 4], place)

    def back_core(g):
        await_bytes(from_1.at[group_units(g)], sum_recv_sem.at[g, 4])
        piece = reduced_ref.at[group_units(g), core_rows]
        send_to(piece, piece, sum_send_sem.at[g, 5], sum_recv_sem.at[g, 5], twin)

    chip = places["x"] * 16 + places["y"] * 4 + places["z"]

    def place_of(i):
        x, y, z = i // 16, (i // 4) % 4, i % 4
        return (x % 2) * 4 + y, (x // 2) * 8 + z * 2 + core

    def piece_of(i):
        return i // 16, tile_rows(i % 16, ROWS_2)

    def scatter(g):
        add_core(g)

        def push_piece(k, carry):
            i = (chip + k) % CHIPS
            unit, rows = piece_of(i)
            send_to(
                held_0.at[4 * g + unit, rows], from_chips.at[chip],
                sum_send_sem.at[g, 1], sum_recv_sem.at[g, 1], place_of(i),
            )
            return carry

        lax.fori_loop(1, CHIPS, push_piece, 0)
        unit, rows = piece_of(chip)
        from_chips[chip] = held_0[4 * g + unit, rows, :]

    def gather(g):
        await_bytes(from_chips.at[pl.ds(0, CHIPS - 1)], sum_recv_sem.at[g, 1])
        total = jnp.sum(from_chips[...].astype(F32), axis=0)
        unit, rows = piece_of(chip)
        row = core * ROWS_CORE + (chip % 16) * ROWS_2
        piece = reduced_ref.at[4 * g + unit, pl.ds(pl.multiple_of(row, ROWS_2), ROWS_2)]
        piece[...] = total.astype(BF16)

        def push_sum(k, carry):
            send_to(
                piece, piece, sum_send_sem.at[g, 2], sum_recv_sem.at[g, 2], place_of((chip + k) % CHIPS)
            )
            return carry

        lax.fori_loop(1, CHIPS, push_sum, 0)

    def gather_core(g):
        await_bytes(from_chips.at[pl.ds(0, CHIPS - 1)], sum_recv_sem.at[g, 2])
        piece = reduced_ref.at[group_units(g), core_rows]
        send_to(piece, piece, sum_send_sem.at[g, 5], sum_recv_sem.at[g, 5], twin)

    def sum_end(g):
        units = group_units(g)
        await_bytes(from_core.at[units], sum_recv_sem.at[g, 5])
        await_bytes(from_core.at[units], sum_send_sem.at[g, 0])
        await_bytes(from_core.at[units], sum_send_sem.at[g, 5])
        if g < len(FIRST_AXES):
            await_bytes(from_1.at[units], sum_send_sem.at[g, 1])
            await_bytes(from_plane.at[g, pl.ds(0, 15)], sum_send_sem.at[g, 2])
            await_bytes(from_plane.at[g, pl.ds(0, 15)], sum_send_sem.at[g, 3])
            await_bytes(from_1.at[units], sum_send_sem.at[g, 4])
        else:
            for level in (1, 2):
                await_bytes(from_chips.at[pl.ds(0, CHIPS - 1)], sum_send_sem.at[g, level])

    def weight_grads(g):
        cols = slice(g * LANES, (g + 1) * LANES)
        v_cols = slice(width + g * LANES, width + (g + 1) * LANES)
        grads[4 * g] = dot_cols(own_t, d_query_t[cols, :]).astype(BF16)
        both = jnp.concatenate([d_keyvals[:, cols], d_keyvals[:, v_cols]], axis=1)
        both = dot(halo_t[...], both).astype(BF16)
        grads[4 * g + 1] = both[:, :LANES]
        grads[4 * g + 2] = both[:, LANES:]

    for g in range(GROUPS):
        cols = slice(g * LANES, (g + 1) * LANES)
        q_block, d_block = q_blocks[g].astype(F32), d_blocks[g]
        inverse, delta = inverses[g, 0:1, :], deltas[g, 0:1, :]
        d_scaled = (d_block.astype(F32) * inverse).astype(BF16)
        d_values = dot_cols(weights[g], d_scaled).astype(BF16)
        d_keyvals[:, width + g * LANES:width + (g + 1) * LANES] = d_values
        if g > 0:
            sum_1(g - 1)
        for c in range(9):
            part = slice(c * BLOCK, (c + 1) * BLOCK)
            d = dot(values[part, cols], d_block)
            weights[g, part, :] = (weights[g, part, :].astype(F32) * (d - delta)).astype(BF16)
        back = inverse * SCALE
        d_keys = dot_cols(weights[g], (q_block * back).astype(BF16)).astype(BF16)
        d_keyvals[:, cols] = d_keys
        d_query = (diagonal(dot_rows(keys[:, cols], weights[g])) * spread_heads(back)).astype(BF16)
        d_query_t[cols, :] = d_query
        if g < GROUPS - 1:
            weight_grads(g)
            sum_core(g)

    def node_part(c):
        return dot_cols(d_keyvals[block_rows(c), :], w_qkv_ref[:, width:])

    for lat_step in (-1, 1, 0):
        for n, (sign, place) in enumerate(beside(lat, lon)):
            slot_rows = pl.ds((2 * (lat_step % 3) + n) * BLOCK, BLOCK)
            parts[slot_rows, :] = node_part(cell(lat_step, sign)).astype(BF16)
            send_to(
                parts.at[slot_rows], from_around.at[slot_rows],
                parts_send_sem.at[lat_step % 3], parts_recv_sem.at[lat_step % 3], place,
            )
    weight_grads(3)
    sum_core(3)
    sum_plane(0)
    sum_plane(1)
    scatter(3)
    d_normed = node_part(OWN) + dot_cols(turned(d_query_t[...]), w_qkv_ref[:, :width])
    mixed_ref[...] = (latent_ref[...] + dot_rows(attended_t[...], w_out_ref[...])).astype(BF16)
    latent = latent_ref[...]
    centered = latent - jnp.mean(latent, axis=1, keepdims=True)
    inverse_std = lax.rsqrt(jnp.mean(centered * centered, axis=1, keepdims=True) + EPS)
    normalized = centered * inverse_std
    sum_plane(2)
    for n, (sign, place) in enumerate(above(lat, lon)):
        at = sign % 3
        part = node_part(cell(sign, 0))
        arrived = from_around.at[pl.ds(2 * at * BLOCK, 2 * BLOCK)]
        await_bytes(arrived, parts_recv_sem.at[at])
        part = part + arrived[:BLOCK, :].astype(F32) + arrived[BLOCK:, :].astype(F32)
        slot_rows = pl.ds((6 + n) * BLOCK, BLOCK)
        parts[slot_rows, :] = part.astype(BF16)
        send_to(
            parts.at[slot_rows], from_around.at[slot_rows], parts_send_sem.at[3], parts_recv_sem.at[3], place
        )
    for g in range(3):
        back_plane(g)
    gather(3)
    await_bytes(from_around.at[pl.ds(0, 2 * BLOCK)], parts_recv_sem.at[0])
    await_bytes(from_around.at[pl.ds(6 * BLOCK, 2 * BLOCK)], parts_recv_sem.at[3])
    for n in (0, 1, 6, 7):
        d_normed = d_normed + from_around[block_rows(n), :].astype(F32)
    scaled = d_normed * gain_ref[...]
    d_latent = cot.astype(F32) + inverse_std * (
        scaled
        - jnp.mean(scaled, axis=1, keepdims=True)
        - normalized * jnp.mean(scaled * normalized, axis=1, keepdims=True)
    )
    node_grad = (d_latent / divisor).astype(BF16)
    stacked = jnp.concatenate([node_grad[:, :half], node_grad[:, half:]], axis=0)

    await_bytes(send.at[pl.ds(0, (DEVICES - 1) * 2 * CAP)], send_sem)
    for turn, step in enumerate((0, 1, 7, 2, 6, 3, 5, 4)):
        if turn == 2:
            for g in range(3):
                back_1(g)
        to_lat = (lat + step) % LAT
        rows = tile_rows(to_lat, 2 * CAP * LON)
        send[rows, :] = dot(spread_ref[rows, :], stacked).astype(BF16)

        def push_back(j, carry, to_lat=to_lat):
            to_lon = (lon + j) % LON
            other = to_lat * LON + to_lon
            send_to(
                send.at[tile_rows(other, 2 * CAP)], returned_ref.at[tile_rows(me, 2 * CAP)],
                back_send_sem, back_recv_sem, (to_lat, to_lon),
            )
            return carry

        lax.fori_loop(1 if step == 0 else 0, LON, push_back, 0)
    pltpu.make_async_copy(
        send.at[tile_rows(me, 2 * CAP)], returned_ref.at[tile_rows(me, 2 * CAP)], back_recv_sem
    ).start()
    gather_core(3)
    for g in range(3):
        back_core(g)
    stores = [
        pltpu.make_async_copy(mixed_ref, mixed_out, store_sem.at[0]),
        pltpu.make_async_copy(flat_ref, flat_out, store_sem.at[1]),
    ]
    for g in range(GROUPS):
        sum_end(g)
        units = group_units(g)
        stores.append(
            pltpu.make_async_copy(reduced_ref.at[units], reduced_out.at[units], store_sem.at[2 + g])
        )
    for store in stores:
        store.start()
    await_bytes(ids_send.at[pl.ds(0, DEVICES - 1)], ids_send_sem)
    for n, blocks in enumerate((1, 1, 2, 4)):
        await_bytes(halo.at[pl.ds(0, blocks * BLOCK)], halo_send_sem.at[n])
    for n in range(4):
        await_bytes(parts.at[pl.ds(0, 2 * BLOCK)], parts_send_sem.at[n])
    await_bytes(send.at[pl.ds(0, (DEVICES - 1) * 2 * CAP)], back_send_sem)
    for store in stores:
        store.wait()
    await_bytes(returned_ref, back_recv_sem)


def sublayer(grid_rows, owner, node, embed, listed, gain, w_qkv, w_out, cotangent):
    count, width = grid_rows.shape
    nodes = embed.shape[0]
    lanes = 2 * DEVICES * CAP
    pool = 9 * nodes
    units, early = 4 * GROUPS, 4 * len(FIRST_AXES)
    vmem, dma = pltpu.VMEM, pltpu.SemaphoreType.DMA
    return pl.pallas_call(
        sublayer_kernel,
        name="sublayer",
        out_shape=(
            jax.ShapeDtypeStruct((nodes, width), BF16),
            jax.ShapeDtypeStruct((units, width, LANES), BF16),
            jax.ShapeDtypeStruct((lanes, width // 2), BF16),
            jax.ShapeDtypeStruct((count, LANES), jnp.int32),
        ),
        in_specs=[pl.BlockSpec(memory_space=vmem)] * 4 + [pl.BlockSpec(memory_space=pl.ANY)] * 5,
        out_specs=[pl.BlockSpec(memory_space=vmem if i == 2 else pl.ANY) for i in range(4)],
        scratch_shapes=[
            vmem((nodes, width), BF16),
            vmem((units, width, LANES), BF16),
            vmem((count, LANES), jnp.int32),
            vmem((count, width), BF16),
            vmem((nodes, width), BF16),
            vmem(w_qkv.shape, BF16),
            vmem(w_out.shape, BF16),
            vmem((nodes, width), BF16),
            vmem((lanes, width // 2), BF16),
            vmem((lanes, width // 2), BF16),
            vmem((DEVICES, 1, LANES), F32),
            vmem((DEVICES, 1, LANES), F32),
            vmem((pool, width), BF16),
            vmem((width, pool), BF16),
            vmem((nodes, width), F32),
            vmem((lanes, 2 * nodes), BF16),
            vmem((pool, width), BF16),
            vmem((pool, width), BF16),
            vmem((GROUPS, LANES, COLUMNS), BF16),
            vmem((GROUPS, LANES, COLUMNS), BF16),
            vmem((GROUPS, pool, COLUMNS), F32),
            vmem((GROUPS, 16, COLUMNS), F32),
            vmem((GROUPS, pool, COLUMNS), BF16),
            vmem((GROUPS, 8, COLUMNS), F32),
            vmem((GROUPS, 8, COLUMNS), F32),
            vmem((pool, 2 * width), BF16),
            vmem((width, BLOCK), BF16),
            vmem((width, BLOCK), BF16),
            vmem((units, width, LANES), BF16),
            vmem((units, ROWS_CORE, LANES), BF16),
            vmem((units, ROWS_CORE, LANES), BF16),
            vmem((early, 3 * ROWS_1, LANES), BF16),
            vmem((early, ROWS_1, LANES), BF16),
            vmem((len(FIRST_AXES), 16, ROWS_2, LANES), BF16),
            vmem((CHIPS, ROWS_2, LANES), BF16),
            vmem((8 * nodes, width), BF16),
            vmem((8 * nodes, width), BF16),
            dma((5,)),
            dma((2 + GROUPS,)),
        ] + [dma] * 4 + [dma((4,))] * 2 + [dma((GROUPS, 6))] * 2 + [dma((4,))] * 2 + [dma] * 2,
        compiler_params=pltpu.CompilerParams(
            collective_id=0, has_side_effects=True, vmem_limit_bytes=VMEM_LIMIT
        ),
    )(
        owner.reshape(1, count), node.reshape(1, count), listed, gain.reshape(1, width),
        grid_rows, embed, w_qkv, w_out, cotangent,
    )


def finish_kernel(
    reduced_ref, returned_ref, flat_ref, w_qkv_ref, gain_ref, mixed_in_ref,
    mixed_ref, grad_grid_ref, grad_w_qkv_ref, grad_w_out_ref, grad_gain_ref,
):
    count, width = grad_grid_ref.shape
    half = width // 2
    slots = DEVICES * CAP
    mixed_ref[...] = mixed_in_ref[...]
    product = jnp.zeros((width, LANES), F32)
    for g in range(GROUPS):
        for m in range(3):
            cols = slice(m * width + g * LANES, m * width + (g + 1) * LANES)
            grad = reduced_ref[4 * g + m].astype(F32)
            grad_w_qkv_ref[:, cols] = grad
            product = product + grad * w_qkv_ref[:, cols].astype(F32)
        grad_w_out_ref[:, g * LANES:(g + 1) * LANES] = reduced_ref[4 * g + 3].astype(F32)
    grad_gain_ref[...] = jnp.sum(product.T, axis=0, keepdims=True) / gain_ref[...]
    back = returned_ref[...].astype(F32).reshape(DEVICES, 2 * CAP, half)
    back = jnp.concatenate([back[:, :CAP, :], back[:, CAP:, :]], axis=2)
    back = back.reshape(slots, width).astype(BF16)
    chosen = one_hot(iota((count, slots), 1) == flat_ref[:, 0:1])
    grad_grid_ref[...] = dot(chosen, back).astype(BF16)


def finish(reduced, returned, flat, w_qkv, gain, mixed):
    width = w_qkv.shape[0]
    count = flat.shape[0]
    return pl.pallas_call(
        finish_kernel,
        name="finish",
        out_shape=(
            jax.ShapeDtypeStruct(mixed.shape, BF16),
            jax.ShapeDtypeStruct((count, width), BF16),
            jax.ShapeDtypeStruct((width, 3 * width), F32),
            jax.ShapeDtypeStruct((width, width), F32),
            jax.ShapeDtypeStruct((1, width), F32),
        ),
        in_specs=[pl.BlockSpec(memory_space=pltpu.VMEM)] * 6,
        out_specs=[pl.BlockSpec(memory_space=pltpu.VMEM)] * 5,
        compiler_params=pltpu.CompilerParams(vmem_limit_bytes=VMEM_LIMIT),
    )(reduced, returned, flat, w_qkv, gain.reshape(1, width), mixed)


def local(
    grid_rows, dest_owner, dest_node, node_embed, neighbours, norm_gain, w_qkv, w_out, cotangent
):
    mixed, reduced, returned, flat = sublayer(
        grid_rows, dest_owner, dest_node, node_embed, neighbours, norm_gain, w_qkv, w_out, cotangent
    )
    mixed, grad_grid, grad_w_qkv, grad_w_out, grad_gain = finish(
        reduced, returned, flat, w_qkv, norm_gain, mixed
    )
    return (mixed, grad_grid, grad_w_qkv, grad_w_out, grad_gain.reshape(norm_gain.shape))


def solution(mesh):
    split = P(("lat", "lon"), None)
    in_specs = (split, split, P(("lat", "lon")), split, split, P(), P(), P(), split)
    out_specs = (split, split, P(), P(), P())
    return jax.shard_map(local, mesh=mesh, in_specs=in_specs, out_specs=out_specs, check_vma=False)
```

```python
import math

import jax
import jax.numpy as jnp
from jax import lax
from jax.experimental import pallas as pl
from jax.experimental.pallas import tpu as pltpu
from jax.sharding import PartitionSpec as P

HEADS = 16
HEAD_SIZE = 32
BLOCK = 128
LANES = 128
LAT = 8
LON = 16
DEVICES = LAT * LON
OWN = 4
CAP = 8
GROUPS = 4
GROUP_HEADS = LANES // HEAD_SIZE
COLUMNS = GROUP_HEADS * BLOCK
SCALE = HEAD_SIZE ** (-0.5)
TO_LOG2 = math.log2(math.e)
EPS = 1e-05
VMEM_LIMIT = 56 * 1024 * 1024
MESH = pl.DeviceIdType.MESH
F32, BF16 = jnp.float32, jnp.bfloat16
FIRST_AXES = "xyz"
CHIPS = DEVICES // 2
ROWS_CORE, ROWS_1, ROWS_2 = 256, 64, 16


def dot(a, b):
    return jnp.dot(a, b, preferred_element_type=F32)


def dot_rows(a, b):
    return lax.dot_general(a, b, (((0,), (0,)), ((), ())), preferred_element_type=F32)


def dot_cols(a, b):
    return lax.dot_general(a, b, (((1,), (1,)), ((), ())), preferred_element_type=F32)


def iota(shape, dim):
    return lax.broadcasted_iota(jnp.int32, shape, dim)


def one_hot(condition):
    return condition.astype(F32).astype(BF16)


def turned(a):
    return a.astype(F32).T.astype(BF16)


def await_bytes(ref, sem):
    pltpu.make_async_copy(ref, ref, sem).wait()


def send_to(src, dst, send_sem, recv_sem, place):
    pltpu.make_async_remote_copy(
        src_ref=src,
        dst_ref=dst,
        send_sem=send_sem,
        recv_sem=recv_sem,
        device_id=place,
        device_id_type=MESH,
    ).start()


def tile_rows(index, rows):
    return pl.ds(pl.multiple_of(index * rows, rows), rows)


def block_rows(c):
    return pl.ds(c * BLOCK, BLOCK)


def beside(lat, lon):
    for sign in (-1, 1):
        yield sign, (lat, (lon + sign + LON) % LON)


def above(lat, lon):
    for sign in (-1, 1):
        yield sign, ((lat + sign + LAT) % LAT, lon)


def cell(lat_step, lon_step):
    return (lat_step + 1) * 3 + lon_step + 1


def place_on(axis, lat, lon):
    return {"x": (lon // 8) * 2 + lat // 4, "y": lat % 4, "z": (lon // 2) % 4}[axis]


def moved_to(axis, index, lat, lon):
    if axis == "x":
        return (index % 2) * 4 + lat % 4, (index // 2) * 8 + lon % 8
    if axis == "y":
        return (lat // 4) * 4 + index, lon
    return lat, (lon // 8) * 8 + index * 2 + lon % 2


def diagonal(full):
    return jnp.concatenate(
        [
            full[h * HEAD_SIZE:(h + 1) * HEAD_SIZE, h * BLOCK:(h + 1) * BLOCK]
            for h in range(GROUP_HEADS)
        ],
        axis=0,
    )


def spread_heads(row):
    return jnp.concatenate(
        [
            jnp.broadcast_to(row[:, h * BLOCK:(h + 1) * BLOCK], (HEAD_SIZE, BLOCK))
            for h in range(GROUP_HEADS)
        ],
        axis=0,
    )


def sublayer_kernel(
    owner_ref, node_ref, listed_ref, gain_ref, grid_hbm, embed_hbm, w_qkv_hbm, w_out_hbm, cot_hbm,
    mixed_out, reduced_out, returned_ref, flat_out,
    mixed_ref, reduced_ref, flat_ref, grid_ref, embed_ref, w_qkv_ref, w_out_ref, cot_ref,
    send, recv, ids_send, ids_recv,
    halo, halo_t, latent_ref, spread_ref, keys, values, q_blocks, d_blocks,
    scores, tops, weights, inverses, deltas, d_keyvals, attended_t, d_query_t,
    grads, from_core, held_0, from_1, held_1, from_plane, from_chips, parts, from_around,
    load_sem, store_sem, send_sem, recv_sem, ids_send_sem, ids_recv_sem, halo_send_sem, halo_recv_sem,
    sum_send_sem, sum_recv_sem, parts_send_sem, parts_recv_sem, back_send_sem, back_recv_sem,
):
    lat, lon = lax.axis_index("lat"), lax.axis_index("lon")
    me = lat * LON + lon
    barrier = pltpu.get_barrier_semaphore()

    def greet(step, carry):
        other = (me + step) % DEVICES
        pl.semaphore_signal(
            barrier, inc=1, device_id=(other // LON, other % LON), device_id_type=MESH
        )
        return carry

    lax.fori_loop(1, DEVICES, greet, 0)
    loads = [
        pltpu.make_async_copy(src, dst, load_sem.at[i])
        for i, (src, dst) in enumerate(
            ((grid_hbm, grid_ref), (embed_hbm, embed_ref), (w_qkv_hbm, w_qkv_ref), (w_out_hbm, w_out_ref), (cot_hbm, cot_ref))
        )
    ]
    for load in loads:
        load.start()

    count, width = grid_ref.shape
    nodes = embed_ref.shape[0]
    half = width // 2
    slots = DEVICES * CAP

    owner = owner_ref[...]
    picked = (iota((DEVICES, count), 0) == owner).astype(F32)
    earlier = one_hot(iota((count, count), 0) < iota((count, count), 1))
    slot = jnp.sum(picked * dot(picked.astype(BF16), earlier), axis=0, keepdims=True).astype(jnp.int32)
    flat = owner * CAP + slot
    named = (picked * (node_ref[...] + 1).astype(F32)).astype(BF16)
    ids_send[:, 0, :] = dot_cols(named, one_hot(iota((LANES, count), 0) == slot))
    loads[0].wait()
    grid = grid_ref[...]

    for k in range(LAT):
        chosen = one_hot(iota((LON * CAP, count), 0) + k * (LON * CAP) == flat)
        block = dot(chosen, grid).reshape(LON, CAP, width)
        block = jnp.concatenate([block[:, :, :half], block[:, :, half:]], axis=1)
        send[pl.ds(k * 2 * CAP * LON, 2 * CAP * LON), :] = block.reshape(2 * CAP * LON, half).astype(BF16)
    pl.semaphore_wait(barrier, DEVICES - 1)

    def push(step, carry):
        other = (me + 53 * step) % DEVICES
        place = (other // LON, other % LON)
        send_to(ids_send.at[other], ids_recv.at[me], ids_send_sem, ids_recv_sem, place)
        send_to(
            send.at[tile_rows(other, 2 * CAP)], recv.at[tile_rows(me, 2 * CAP)], send_sem, recv_sem, place
        )
        return carry

    lax.fori_loop(1, DEVICES, push, 0)
    pltpu.make_async_copy(ids_send.at[me], ids_recv.at[me], ids_recv_sem).start()
    pltpu.make_async_copy(
        send.at[tile_rows(me, 2 * CAP)], recv.at[tile_rows(me, 2 * CAP)], recv_sem
    ).start()

    for load in loads[1:]:
        load.wait()
    cot = cot_ref[...]
    d_t = turned(dot_cols(cot, w_out_ref[...]).astype(BF16))
    q_blocks[...] = jnp.zeros_like(q_blocks)
    d_blocks[...] = jnp.zeros_like(d_blocks)

    def blocks_of(target, full_t):
        for g in range(GROUPS):
            for h in range(GROUP_HEADS):
                at = g * LANES + h * HEAD_SIZE
                target[g, h * HEAD_SIZE:(h + 1) * HEAD_SIZE, h * BLOCK:(h + 1) * BLOCK] = full_t[
                    at:at + HEAD_SIZE, :
                ]

    blocks_of(d_blocks, d_t)
    flat_ref[...] = jnp.broadcast_to(flat.astype(F32), (LANES, count)).T.astype(jnp.int32)
    listed = listed_ref[...]
    lat_step = listed // LON - lat
    lon_step = (listed % LON - lon + LON + 1) % LON - 1
    at_place = (lat_step + 1) * 3 + lon_step + 1 == iota((16, listed.shape[1]), 0)
    times = jnp.sum(at_place.astype(F32), axis=1, keepdims=True)
    bias = jnp.where(times > 0, jnp.log(jnp.maximum(times, 1.0)) * TO_LOG2, -1e30)

    await_bytes(ids_recv, ids_recv_sem)
    ids = ids_recv[:, 0, :]
    lanes = 2 * slots
    codes = dot(turned(ids)[:CAP, :], one_hot(iota((DEVICES, lanes), 0) == (iota((DEVICES, lanes), 1) >> 4)))
    mine = (iota((CAP, lanes), 1) & 7) == iota((CAP, lanes), 0)
    code = jnp.sum(jnp.where(mine, codes, 0.0), axis=0, keepdims=True).astype(jnp.int32)
    code = jnp.where(code > 0, code - 1 + nodes * ((iota((1, lanes), 1) >> 3) & 1), -1)
    members = (iota((2 * nodes, lanes), 0) == code).astype(F32)
    divisor = jnp.maximum(jnp.sum(members[:nodes, :], axis=1, keepdims=True), 1.0)
    members = members.astype(BF16)
    await_bytes(recv, recv_sem)
    sums = dot(members, recv[...])
    totals = jnp.concatenate([sums[:nodes, :], sums[nodes:, :]], axis=1)
    latent = embed_ref[...].astype(F32) + totals / divisor
    latent_ref[...] = latent
    centered = latent - jnp.mean(latent, axis=1, keepdims=True)
    inverse_std = lax.rsqrt(jnp.mean(centered * centered, axis=1, keepdims=True) + EPS)
    halo[block_rows(OWN), :] = (centered * inverse_std * gain_ref[...]).astype(BF16)
    mine = halo.at[block_rows(OWN)]
    for n, (sign, place) in enumerate(above(lat, lon)):
        send_to(
            mine, halo.at[block_rows(cell(-sign, 0))], halo_send_sem.at[n], halo_recv_sem.at[n], place
        )
    for sign, place in beside(lat, lon):
        send_to(mine, halo.at[block_rows(cell(0, -sign))], halo_send_sem.at[2], halo_recv_sem.at[2], place)

    own = halo[block_rows(OWN), :]
    own_t = turned(own)
    blocks_of(q_blocks, turned(dot(own, w_qkv_ref[:, :width]).astype(BF16)))

    def take(c):
        rows = block_rows(c)
        block = halo[rows, :]
        keys[rows, :] = dot(block, w_qkv_ref[:, width:2 * width]).astype(BF16)
        values[rows, :] = dot(block, w_qkv_ref[:, 2 * width:]).astype(BF16)
        halo_t[:, rows] = turned(block)
        for g in range(GROUPS):
            s = dot(keys[rows, g * LANES:(g + 1) * LANES], q_blocks[g])
            scores[g, rows, :] = s
            tops[g, c:c + 1, :] = jnp.max(s, axis=0, keepdims=True) * (SCALE * TO_LOG2) + bias[c:c + 1, :]

    take(OWN)
    for n, (step, _) in enumerate(above(lat, lon)):
        block = halo.at[block_rows(cell(-step, 0))]
        await_bytes(block, halo_recv_sem.at[n])
        for sign, place in beside(lat, lon):
            send_to(
                block, halo.at[block_rows(cell(-step, -sign))],
                halo_send_sem.at[3], halo_recv_sem.at[3], place,
            )
    await_bytes(halo.at[pl.ds(0, 2 * BLOCK)], halo_recv_sem.at[2])
    for c in (1, 3, 5, 7):
        take(c)
    codes = dot(one_hot(iota((lanes, DEVICES), 1) == (iota((lanes, DEVICES), 0) >> 4)), ids.astype(BF16))
    mine = (iota((lanes, LANES), 0) & 7) == iota((lanes, LANES), 1)
    code = jnp.sum(jnp.where(mine, codes, 0.0), axis=1, keepdims=True).astype(jnp.int32)
    code = jnp.where(code > 0, code - 1 + nodes * ((iota((lanes, 1), 0) >> 3) & 1), -1)
    spread_ref[...] = one_hot(iota((lanes, 2 * nodes), 1) == code)

    await_bytes(halo.at[pl.ds(0, 4 * BLOCK)], halo_recv_sem.at[3])
    for c in (0, 2, 6, 8):
        take(c)

    def forward(g, carry):
        cols = slice(g * LANES, (g + 1) * LANES)
        highest = jnp.max(tops[g, 0:9, :], axis=0, keepdims=True)
        total = jnp.zeros((1, COLUMNS), F32)
        for c in range(9):
            part = slice(c * BLOCK, (c + 1) * BLOCK)
            w = jnp.exp2(scores[g, part, :] * (SCALE * TO_LOG2) - (highest - bias[c:c + 1, :]))
            total = total + jnp.sum(w, axis=0, keepdims=True)
            weights[g, part, :] = w.astype(BF16)
        inverse = 1.0 / total
        out_group = diagonal(dot_rows(values[:, cols], weights[g])) * spread_heads(inverse)
        attended_t[cols, :] = out_group.astype(BF16)
        product = out_group * diagonal(d_blocks[g].astype(F32))
        delta = jnp.concatenate(
            [
                jnp.sum(product[h * HEAD_SIZE:(h + 1) * HEAD_SIZE, :], axis=0, keepdims=True)
                for h in range(GROUP_HEADS)
            ],
            axis=1,
        )
        inverses[g] = jnp.broadcast_to(inverse, (8, COLUMNS))
        deltas[g] = jnp.broadcast_to(delta, (8, COLUMNS))
        return carry

    for g in range(GROUPS):
        forward(g, 0)
    grad_w_out = dot(attended_t[...], cot).astype(BF16)
    for g in range(GROUPS):
        grads[4 * g + 3] = grad_w_out[:, g * LANES:(g + 1) * LANES]

    core = lon % 2
    twin = (lat, lon - core + (1 - core))
    core_rows = tile_rows(core, ROWS_CORE)
    places = {axis: place_on(axis, lat, lon) for axis in "xyz"}

    def group_units(g):
        return pl.ds(4 * g, 4)

    def others(axis):
        for k in range(1, 4):
            t = (places[axis] + k) % 4
            yield k - 1, t, moved_to(axis, t, lat, lon)

    def sum_core(g):
        send_to(
            grads.at[group_units(g), tile_rows(1 - core, ROWS_CORE)], from_core.at[group_units(g)],
            sum_send_sem.at[g, 0], sum_recv_sem.at[g, 0], twin,
        )

    def add_core(g):
        units = group_units(g)
        await_bytes(from_core.at[units], sum_recv_sem.at[g, 0])
        held_0[units] = (grads[units, core_rows, :].astype(F32) + from_core[units].astype(F32)).astype(BF16)

    def sum_1(g):
        add_core(g)
        units = group_units(g)
        for k, t, place in others(FIRST_AXES[g]):
            send_to(
                held_0.at[units, tile_rows(t, ROWS_1)], from_1.at[units, pl.ds(k * ROWS_1, ROWS_1)],
                sum_send_sem.at[g, 1], sum_recv_sem.at[g, 1], place,
            )

    def plane_index(g):
        b, c = (axis for axis in "xyz" if axis != FIRST_AXES[g])
        return places[b] * 4 + places[c]

    def plane_place(g, j):
        b, c = (axis for axis in "xyz" if axis != FIRST_AXES[g])
        return moved_to(c, j % 4, *moved_to(b, j // 4, lat, lon))

    def sum_plane(g):
        units = group_units(g)
        await_bytes(from_1.at[units], sum_recv_sem.at[g, 1])
        total = held_0[units, tile_rows(places[FIRST_AXES[g]], ROWS_1), :].astype(F32)
        for k in range(3):
            total = total + from_1[units, pl.ds(k * ROWS_1, ROWS_1), :].astype(F32)
        held_1[units] = total.astype(BF16)
        mine = plane_index(g)

        def push_piece(k, carry):
            j = (mine + k) % 16
            send_to(
                held_1.at[4 * g + j // 4, tile_rows(j % 4, ROWS_2)], from_plane.at[g, mine],
                sum_send_sem.at[g, 2], sum_recv_sem.at[g, 2], plane_place(g, j),
            )
            return carry

        lax.fori_loop(1, 16, push_piece, 0)
        from_plane[g, mine] = held_1[4 * g + mine // 4, tile_rows(mine % 4, ROWS_2), :]

    def back_plane(g):
        await_bytes(from_plane.at[g, pl.ds(0, 15)], sum_recv_sem.at[g, 2])
        mine = plane_index(g)
        row = core * ROWS_CORE + places[FIRST_AXES[g]] * ROWS_1 + (mine % 4) * ROWS_2
        piece = reduced_ref.at[4 * g + mine // 4, pl.ds(pl.multiple_of(row, ROWS_2), ROWS_2)]
        piece[...] = jnp.sum(from_plane[g].astype(F32), axis=0).astype(BF16)

        def push_sum(k, carry):
            send_to(
                piece, piece, sum_send_sem.at[g, 3], sum_recv_sem.at[g, 3],
                plane_place(g, (mine + k) % 16),
            )
            return carry

        lax.fori_loop(1, 16, push_sum, 0)

    def back_1(g):
        await_bytes(from_plane.at[g, pl.ds(0, 15)], sum_recv_sem.at[g, 3])
        row = core * ROWS_CORE + places[FIRST_AXES[g]] * ROWS_1
        piece = reduced_ref.at[group_units(g), pl.ds(pl.multiple_of(row, ROWS_1), ROWS_1)]
        for k, t, place in others(FIRST_AXES[g]):
            send_to(piece, piece, sum_send_sem.at[g, 4], sum_recv_sem.at[g, 4], place)

    def back_core(g):
        await_bytes(from_1.at[group_units(g)], sum_recv_sem.at[g, 4])
        piece = reduced_ref.at[group_units(g), core_rows]
        send_to(piece, piece, sum_send_sem.at[g, 5], sum_recv_sem.at[g, 5], twin)

    chip = places["x"] * 16 + places["y"] * 4 + places["z"]

    def place_of(i):
        x, y, z = i // 16, (i // 4) % 4, i % 4
        return (x % 2) * 4 + y, (x // 2) * 8 + z * 2 + core

    def piece_of(i):
        return i // 16, tile_rows(i % 16, ROWS_2)

    def scatter(g):
        add_core(g)

        def push_piece(k, carry):
            i = (chip + k) % CHIPS
            unit, rows = piece_of(i)
            send_to(
                held_0.at[4 * g + unit, rows], from_chips.at[chip],
                sum_send_sem.at[g, 1], sum_recv_sem.at[g, 1], place_of(i),
            )
            return carry

        lax.fori_loop(1, CHIPS, push_piece, 0)
        unit, rows = piece_of(chip)
        from_chips[chip] = held_0[4 * g + unit, rows, :]

    def gather(g):
        await_bytes(from_chips.at[pl.ds(0, CHIPS - 1)], sum_recv_sem.at[g, 1])
        total = jnp.sum(from_chips[...].astype(F32), axis=0)
        unit, rows = piece_of(chip)
        row = core * ROWS_CORE + (chip % 16) * ROWS_2
        piece = reduced_ref.at[4 * g + unit, pl.ds(pl.multiple_of(row, ROWS_2), ROWS_2)]
        piece[...] = total.astype(BF16)

        def push_sum(k, carry):
            send_to(
                piece, piece, sum_send_sem.at[g, 2], sum_recv_sem.at[g, 2], place_of((chip + k) % CHIPS)
            )
            return carry

        lax.fori_loop(1, CHIPS, push_sum, 0)

    def gather_core(g):
        await_bytes(from_chips.at[pl.ds(0, CHIPS - 1)], sum_recv_sem.at[g, 2])
        piece = reduced_ref.at[group_units(g), core_rows]
        send_to(piece, piece, sum_send_sem.at[g, 5], sum_recv_sem.at[g, 5], twin)

    def sum_end(g):
        units = group_units(g)
        await_bytes(from_core.at[units], sum_recv_sem.at[g, 5])
        await_bytes(from_core.at[units], sum_send_sem.at[g, 0])
        await_bytes(from_core.at[units], sum_send_sem.at[g, 5])
        if g < len(FIRST_AXES):
            await_bytes(from_1.at[units], sum_send_sem.at[g, 1])
            await_bytes(from_plane.at[g, pl.ds(0, 15)], sum_send_sem.at[g, 2])
            await_bytes(from_plane.at[g, pl.ds(0, 15)], sum_send_sem.at[g, 3])
            await_bytes(from_1.at[units], sum_send_sem.at[g, 4])
        else:
            for level in (1, 2):
                await_bytes(from_chips.at[pl.ds(0, CHIPS - 1)], sum_send_sem.at[g, level])

    def weight_grads(g):
        cols = slice(g * LANES, (g + 1) * LANES)
        v_cols = slice(width + g * LANES, width + (g + 1) * LANES)
        grads[4 * g] = dot_cols(own_t, d_query_t[cols, :]).astype(BF16)
        both = jnp.concatenate([d_keyvals[:, cols], d_keyvals[:, v_cols]], axis=1)
        both = dot(halo_t[...], both).astype(BF16)
        grads[4 * g + 1] = both[:, :LANES]
        grads[4 * g + 2] = both[:, LANES:]

    for g in range(GROUPS):
        cols = slice(g * LANES, (g + 1) * LANES)
        q_block, d_block = q_blocks[g].astype(F32), d_blocks[g]
        inverse, delta = inverses[g, 0:1, :], deltas[g, 0:1, :]
        d_scaled = (d_block.astype(F32) * inverse).astype(BF16)
        d_values = dot_cols(weights[g], d_scaled).astype(BF16)
        d_keyvals[:, width + g * LANES:width + (g + 1) * LANES] = d_values
        if g > 0:
            sum_1(g - 1)
        for c in range(9):
            part = slice(c * BLOCK, (c + 1) * BLOCK)
            d = dot(values[part, cols], d_block)
            weights[g, part, :] = (weights[g, part, :].astype(F32) * (d - delta)).astype(BF16)
        back = inverse * SCALE
        d_keys = dot_cols(weights[g], (q_block * back).astype(BF16)).astype(BF16)
        d_keyvals[:, cols] = d_keys
        d_query = (diagonal(dot_rows(keys[:, cols], weights[g])) * spread_heads(back)).astype(BF16)
        d_query_t[cols, :] = d_query
        if g < GROUPS - 1:
            weight_grads(g)
            sum_core(g)

    def node_part(c):
        return dot_cols(d_keyvals[block_rows(c), :], w_qkv_ref[:, width:])

    for lat_step in (-1, 1, 0):
        for n, (sign, place) in enumerate(beside(lat, lon)):
            slot_rows = pl.ds((2 * (lat_step % 3) + n) * BLOCK, BLOCK)
            parts[slot_rows, :] = node_part(cell(lat_step, sign)).astype(BF16)
            send_to(
                parts.at[slot_rows], from_around.at[slot_rows],
                parts_send_sem.at[lat_step % 3], parts_recv_sem.at[lat_step % 3], place,
            )
    weight_grads(3)
    sum_core(3)
    sum_plane(0)
    sum_plane(1)
    scatter(3)
    d_normed = node_part(OWN) + dot_cols(turned(d_query_t[...]), w_qkv_ref[:, :width])
    mixed_ref[...] = (latent_ref[...] + dot_rows(attended_t[...], w_out_ref[...])).astype(BF16)
    latent = latent_ref[...]
    centered = latent - jnp.mean(latent, axis=1, keepdims=True)
    inverse_std = lax.rsqrt(jnp.mean(centered * centered, axis=1, keepdims=True) + EPS)
    normalized = centered * inverse_std
    sum_plane(2)
    for n, (sign, place) in enumerate(above(lat, lon)):
        at = sign % 3
        part = node_part(cell(sign, 0))
        arrived = from_around.at[pl.ds(2 * at * BLOCK, 2 * BLOCK)]
        await_bytes(arrived, parts_recv_sem.at[at])
        part = part + arrived[:BLOCK, :].astype(F32) + arrived[BLOCK:, :].astype(F32)
        slot_rows = pl.ds((6 + n) * BLOCK, BLOCK)
        parts[slot_rows, :] = part.astype(BF16)
        send_to(
            parts.at[slot_rows], from_around.at[slot_rows], parts_send_sem.at[3], parts_recv_sem.at[3], place
        )
    for g in range(3):
        back_plane(g)
    gather(3)
    await_bytes(from_around.at[pl.ds(0, 2 * BLOCK)], parts_recv_sem.at[0])
    await_bytes(from_around.at[pl.ds(6 * BLOCK, 2 * BLOCK)], parts_recv_sem.at[3])
    for n in (0, 1, 6, 7):
        d_normed = d_normed + from_around[block_rows(n), :].astype(F32)
    scaled = d_normed * gain_ref[...]
    d_latent = cot.astype(F32) + inverse_std * (
        scaled
        - jnp.mean(scaled, axis=1, keepdims=True)
        - normalized * jnp.mean(scaled * normalized, axis=1, keepdims=True)
    )
    node_grad = (d_latent / divisor).astype(BF16)
    stacked = jnp.concatenate([node_grad[:, :half], node_grad[:, half:]], axis=0)

    await_bytes(send.at[pl.ds(0, (DEVICES - 1) * 2 * CAP)], send_sem)
    send[...] = dot(spread_ref[...], stacked).astype(BF16)

    def push_back(step, carry):
        other = (me + 53 * step) % DEVICES
        send_to(
            send.at[tile_rows(other, 2 * CAP)], returned_ref.at[tile_rows(me, 2 * CAP)],
            back_send_sem, back_recv_sem, (other // LON, other % LON),
        )
        return carry

    lax.fori_loop(1, 64, push_back, 0)
    for g in range(3):
        back_1(g)
    lax.fori_loop(64, DEVICES, push_back, 0)
    pltpu.make_async_copy(
        send.at[tile_rows(me, 2 * CAP)], returned_ref.at[tile_rows(me, 2 * CAP)], back_recv_sem
    ).start()
    gather_core(3)
    for g in range(3):
        back_core(g)
    stores = [
        pltpu.make_async_copy(mixed_ref, mixed_out, store_sem.at[0]),
        pltpu.make_async_copy(flat_ref, flat_out, store_sem.at[1]),
    ]
    for g in range(GROUPS):
        sum_end(g)
        units = group_units(g)
        stores.append(
            pltpu.make_async_copy(reduced_ref.at[units], reduced_out.at[units], store_sem.at[2 + g])
        )
    for store in stores:
        store.start()
    await_bytes(ids_send.at[pl.ds(0, DEVICES - 1)], ids_send_sem)
    for n, blocks in enumerate((1, 1, 2, 4)):
        await_bytes(halo.at[pl.ds(0, blocks * BLOCK)], halo_send_sem.at[n])
    for n in range(4):
        await_bytes(parts.at[pl.ds(0, 2 * BLOCK)], parts_send_sem.at[n])
    await_bytes(send.at[pl.ds(0, (DEVICES - 1) * 2 * CAP)], back_send_sem)
    for store in stores:
        store.wait()
    await_bytes(returned_ref, back_recv_sem)


def sublayer(grid_rows, owner, node, embed, listed, gain, w_qkv, w_out, cotangent):
    count, width = grid_rows.shape
    nodes = embed.shape[0]
    lanes = 2 * DEVICES * CAP
    pool = 9 * nodes
    units, early = 4 * GROUPS, 4 * len(FIRST_AXES)
    vmem, dma = pltpu.VMEM, pltpu.SemaphoreType.DMA
    return pl.pallas_call(
        sublayer_kernel,
        name="sublayer",
        out_shape=(
            jax.ShapeDtypeStruct((nodes, width), BF16),
            jax.ShapeDtypeStruct((units, width, LANES), BF16),
            jax.ShapeDtypeStruct((lanes, width // 2), BF16),
            jax.ShapeDtypeStruct((count, LANES), jnp.int32),
        ),
        in_specs=[pl.BlockSpec(memory_space=vmem)] * 4 + [pl.BlockSpec(memory_space=pl.ANY)] * 5,
        out_specs=[pl.BlockSpec(memory_space=vmem if i == 2 else pl.ANY) for i in range(4)],
        scratch_shapes=[
            vmem((nodes, width), BF16),
            vmem((units, width, LANES), BF16),
            vmem((count, LANES), jnp.int32),
            vmem((count, width), BF16),
            vmem((nodes, width), BF16),
            vmem(w_qkv.shape, BF16),
            vmem(w_out.shape, BF16),
            vmem((nodes, width), BF16),
            vmem((lanes, width // 2), BF16),
            vmem((lanes, width // 2), BF16),
            vmem((DEVICES, 1, LANES), F32),
            vmem((DEVICES, 1, LANES), F32),
            vmem((pool, width), BF16),
            vmem((width, pool), BF16),
            vmem((nodes, width), F32),
            vmem((lanes, 2 * nodes), BF16),
            vmem((pool, width), BF16),
            vmem((pool, width), BF16),
            vmem((GROUPS, LANES, COLUMNS), BF16),
            vmem((GROUPS, LANES, COLUMNS), BF16),
            vmem((GROUPS, pool, COLUMNS), F32),
            vmem((GROUPS, 16, COLUMNS), F32),
            vmem((GROUPS, pool, COLUMNS), BF16),
            vmem((GROUPS, 8, COLUMNS), F32),
            vmem((GROUPS, 8, COLUMNS), F32),
            vmem((pool, 2 * width), BF16),
            vmem((width, BLOCK), BF16),
            vmem((width, BLOCK), BF16),
            vmem((units, width, LANES), BF16),
            vmem((units, ROWS_CORE, LANES), BF16),
            vmem((units, ROWS_CORE, LANES), BF16),
            vmem((early, 3 * ROWS_1, LANES), BF16),
            vmem((early, ROWS_1, LANES), BF16),
            vmem((len(FIRST_AXES), 16, ROWS_2, LANES), BF16),
            vmem((CHIPS, ROWS_2, LANES), BF16),
            vmem((8 * nodes, width), BF16),
            vmem((8 * nodes, width), BF16),
            dma((5,)),
            dma((2 + GROUPS,)),
        ] + [dma] * 4 + [dma((4,))] * 2 + [dma((GROUPS, 6))] * 2 + [dma((4,))] * 2 + [dma] * 2,
        compiler_params=pltpu.CompilerParams(
            collective_id=0, has_side_effects=True, vmem_limit_bytes=VMEM_LIMIT
        ),
    )(
        owner.reshape(1, count), node.reshape(1, count), listed, gain.reshape(1, width),
        grid_rows, embed, w_qkv, w_out, cotangent,
    )


def finish_kernel(
    reduced_ref, returned_ref, flat_ref, w_qkv_ref, gain_ref, mixed_in_ref,
    mixed_ref, grad_grid_ref, grad_w_qkv_ref, grad_w_out_ref, grad_gain_ref,
):
    count, width = grad_grid_ref.shape
    half = width // 2
    slots = DEVICES * CAP
    mixed_ref[...] = mixed_in_ref[...]
    product = jnp.zeros((width, LANES), F32)
    for g in range(GROUPS):
        for m in range(3):
            cols = slice(m * width + g * LANES, m * width + (g + 1) * LANES)
            grad = reduced_ref[4 * g + m].astype(F32)
            grad_w_qkv_ref[:, cols] = grad
            product = product + grad * w_qkv_ref[:, cols].astype(F32)
        grad_w_out_ref[:, g * LANES:(g + 1) * LANES] = reduced_ref[4 * g + 3].astype(F32)
    grad_gain_ref[...] = jnp.sum(product.T, axis=0, keepdims=True) / gain_ref[...]
    back = returned_ref[...].astype(F32).reshape(DEVICES, 2 * CAP, half)
    back = jnp.concatenate([back[:, :CAP, :], back[:, CAP:, :]], axis=2)
    back = back.reshape(slots, width).astype(BF16)
    chosen = one_hot(iota((count, slots), 1) == flat_ref[:, 0:1])
    grad_grid_ref[...] = dot(chosen, back).astype(BF16)


def finish(reduced, returned, flat, w_qkv, gain, mixed):
    width = w_qkv.shape[0]
    count = flat.shape[0]
    return pl.pallas_call(
        finish_kernel,
        name="finish",
        out_shape=(
            jax.ShapeDtypeStruct(mixed.shape, BF16),
            jax.ShapeDtypeStruct((count, width), BF16),
            jax.ShapeDtypeStruct((width, 3 * width), F32),
            jax.ShapeDtypeStruct((width, width), F32),
            jax.ShapeDtypeStruct((1, width), F32),
        ),
        in_specs=[pl.BlockSpec(memory_space=pltpu.VMEM)] * 6,
        out_specs=[pl.BlockSpec(memory_space=pltpu.VMEM)] * 5,
        compiler_params=pltpu.CompilerParams(vmem_limit_bytes=VMEM_LIMIT),
    )(reduced, returned, flat, w_qkv, gain.reshape(1, width), mixed)


def local(
    grid_rows, dest_owner, dest_node, node_embed, neighbours, norm_gain, w_qkv, w_out, cotangent
):
    mixed, reduced, returned, flat = sublayer(
        grid_rows, dest_owner, dest_node, node_embed, neighbours, norm_gain, w_qkv, w_out, cotangent
    )
    mixed, grad_grid, grad_w_qkv, grad_w_out, grad_gain = finish(
        reduced, returned, flat, w_qkv, norm_gain, mixed
    )
    return (mixed, grad_grid, grad_w_qkv, grad_w_out, grad_gain.reshape(norm_gain.shape))


def solution(mesh):
    split = P(("lat", "lon"), None)
    in_specs = (split, split, P(("lat", "lon")), split, split, P(), P(), P(), split)
    out_specs = (split, split, P(), P(), P())
    return jax.shard_map(local, mesh=mesh, in_specs=in_specs, out_specs=out_specs, check_vma=False)
```

```python
import math

import jax
import jax.numpy as jnp
from jax import lax
from jax.experimental import pallas as pl
from jax.experimental.pallas import tpu as pltpu
from jax.sharding import PartitionSpec as P

HEADS = 16
HEAD_SIZE = 32
BLOCK = 128
LANES = 128
LAT = 8
LON = 16
DEVICES = LAT * LON
OWN = 4
CAP = 8
GROUPS = 4
GROUP_HEADS = LANES // HEAD_SIZE
COLUMNS = GROUP_HEADS * BLOCK
SCALE = HEAD_SIZE ** (-0.5)
TO_LOG2 = math.log2(math.e)
EPS = 1e-05
VMEM_LIMIT = 56 * 1024 * 1024
MESH = pl.DeviceIdType.MESH
F32, BF16 = jnp.float32, jnp.bfloat16
FIRST_AXES = "xyz"
CHIPS = DEVICES // 2
ROWS_CORE, ROWS_1, ROWS_2 = 256, 64, 16


def dot(a, b):
    return jnp.dot(a, b, preferred_element_type=F32)


def dot_rows(a, b):
    return lax.dot_general(a, b, (((0,), (0,)), ((), ())), preferred_element_type=F32)


def dot_cols(a, b):
    return lax.dot_general(a, b, (((1,), (1,)), ((), ())), preferred_element_type=F32)


def iota(shape, dim):
    return lax.broadcasted_iota(jnp.int32, shape, dim)


def one_hot(condition):
    return condition.astype(F32).astype(BF16)


def turned(a):
    return a.astype(F32).T.astype(BF16)


def await_bytes(ref, sem):
    pltpu.make_async_copy(ref, ref, sem).wait()


def send_to(src, dst, send_sem, recv_sem, place):
    pltpu.make_async_remote_copy(
        src_ref=src,
        dst_ref=dst,
        send_sem=send_sem,
        recv_sem=recv_sem,
        device_id=place,
        device_id_type=MESH,
    ).start()


def tile_rows(index, rows):
    return pl.ds(pl.multiple_of(index * rows, rows), rows)


def block_rows(c):
    return pl.ds(c * BLOCK, BLOCK)


def beside(lat, lon):
    for sign in (-1, 1):
        yield sign, (lat, (lon + sign + LON) % LON)


def above(lat, lon):
    for sign in (-1, 1):
        yield sign, ((lat + sign + LAT) % LAT, lon)


def cell(lat_step, lon_step):
    return (lat_step + 1) * 3 + lon_step + 1


def place_on(axis, lat, lon):
    return {"x": (lon // 8) * 2 + lat // 4, "y": lat % 4, "z": (lon // 2) % 4}[axis]


def moved_to(axis, index, lat, lon):
    if axis == "x":
        return (index % 2) * 4 + lat % 4, (index // 2) * 8 + lon % 8
    if axis == "y":
        return (lat // 4) * 4 + index, lon
    return lat, (lon // 8) * 8 + index * 2 + lon % 2


def diagonal(full):
    return jnp.concatenate(
        [
            full[h * HEAD_SIZE:(h + 1) * HEAD_SIZE, h * BLOCK:(h + 1) * BLOCK]
            for h in range(GROUP_HEADS)
        ],
        axis=0,
    )


def spread_heads(row):
    return jnp.concatenate(
        [
            jnp.broadcast_to(row[:, h * BLOCK:(h + 1) * BLOCK], (HEAD_SIZE, BLOCK))
            for h in range(GROUP_HEADS)
        ],
        axis=0,
    )


def sublayer_kernel(
    owner_ref, node_ref, listed_ref, gain_ref, grid_hbm, embed_hbm, w_qkv_hbm, w_out_hbm, cot_hbm,
    mixed_out, reduced_out, returned_ref, flat_out,
    mixed_ref, reduced_ref, flat_ref, grid_ref, embed_ref, w_qkv_ref, w_out_ref, cot_ref,
    send, recv, ids_send, ids_recv,
    w_t, halo, halo_t, latent_ref, spread_ref, keys, values, q_blocks, d_blocks,
    scores, tops, weights, inverses, deltas, d_keyvals, attended_t, d_query_t,
    grads, from_core, held_0, from_1, held_1, from_plane, from_chips, parts, from_around,
    load_sem, store_sem, send_sem, recv_sem, ids_send_sem, ids_recv_sem, halo_send_sem, halo_recv_sem,
    sum_send_sem, sum_recv_sem, parts_send_sem, parts_recv_sem, back_send_sem, back_recv_sem,
):
    lat, lon = lax.axis_index("lat"), lax.axis_index("lon")
    me = lat * LON + lon
    barrier = pltpu.get_barrier_semaphore()

    def greet(step, carry):
        other = (me + step) % DEVICES
        pl.semaphore_signal(
            barrier, inc=1, device_id=(other // LON, other % LON), device_id_type=MESH
        )
        return carry

    lax.fori_loop(1, DEVICES, greet, 0)
    loads = [
        pltpu.make_async_copy(src, dst, load_sem.at[i])
        for i, (src, dst) in enumerate(
            ((grid_hbm, grid_ref), (embed_hbm, embed_ref), (w_qkv_hbm, w_qkv_ref), (w_out_hbm, w_out_ref), (cot_hbm, cot_ref))
        )
    ]
    for load in loads:
        load.start()

    count, width = grid_ref.shape
    nodes = embed_ref.shape[0]
    half = width // 2
    slots = DEVICES * CAP

    owner = owner_ref[...]
    picked = (iota((DEVICES, count), 0) == owner).astype(F32)
    earlier = one_hot(iota((count, count), 0) < iota((count, count), 1))
    slot = jnp.sum(picked * dot(picked.astype(BF16), earlier), axis=0, keepdims=True).astype(jnp.int32)
    flat = owner * CAP + slot
    named = (picked * (node_ref[...] + 1).astype(F32)).astype(BF16)
    ids_send[:, 0, :] = dot_cols(named, one_hot(iota((LANES, count), 0) == slot))
    loads[0].wait()
    grid = grid_ref[...]

    for k in range(LAT):
        chosen = one_hot(iota((LON * CAP, count), 0) + k * (LON * CAP) == flat)
        block = dot(chosen, grid).reshape(LON, CAP, width)
        block = jnp.concatenate([block[:, :, :half], block[:, :, half:]], axis=1)
        send[pl.ds(k * 2 * CAP * LON, 2 * CAP * LON), :] = block.reshape(2 * CAP * LON, half).astype(BF16)
    pl.semaphore_wait(barrier, DEVICES - 1)

    def push(step, carry):
        other = (me + 53 * step) % DEVICES
        place = (other // LON, other % LON)
        send_to(ids_send.at[other], ids_recv.at[me], ids_send_sem, ids_recv_sem, place)
        send_to(
            send.at[tile_rows(other, 2 * CAP)], recv.at[tile_rows(me, 2 * CAP)], send_sem, recv_sem, place
        )
        return carry

    lax.fori_loop(1, DEVICES, push, 0)
    pltpu.make_async_copy(ids_send.at[me], ids_recv.at[me], ids_recv_sem).start()
    pltpu.make_async_copy(
        send.at[tile_rows(me, 2 * CAP)], recv.at[tile_rows(me, 2 * CAP)], recv_sem
    ).start()

    for load in loads[1:]:
        load.wait()
    cot = cot_ref[...]
    d_t = turned(dot_cols(cot, w_out_ref[...]).astype(BF16))
    q_blocks[...] = jnp.zeros_like(q_blocks)
    d_blocks[...] = jnp.zeros_like(d_blocks)

    def blocks_of(target, full_t):
        for g in range(GROUPS):
            for h in range(GROUP_HEADS):
                at = g * LANES + h * HEAD_SIZE
                target[g, h * HEAD_SIZE:(h + 1) * HEAD_SIZE, h * BLOCK:(h + 1) * BLOCK] = full_t[
                    at:at + HEAD_SIZE, :
                ]

    blocks_of(d_blocks, d_t)
    for third in (1, 2):
        w_t[(third - 1) * width:third * width, :] = turned(w_qkv_ref[:, third * width:(third + 1) * width])
    flat_ref[...] = jnp.broadcast_to(flat.astype(F32), (LANES, count)).T.astype(jnp.int32)
    listed = listed_ref[...]
    lat_step = listed // LON - lat
    lon_step = (listed % LON - lon + LON + 1) % LON - 1
    at_place = (lat_step + 1) * 3 + lon_step + 1 == iota((16, listed.shape[1]), 0)
    times = jnp.sum(at_place.astype(F32), axis=1, keepdims=True)
    bias = jnp.where(times > 0, jnp.log(jnp.maximum(times, 1.0)) * TO_LOG2, -1e30)

    await_bytes(ids_recv, ids_recv_sem)
    ids = ids_recv[:, 0, :]
    lanes = 2 * slots
    codes = dot(turned(ids)[:CAP, :], one_hot(iota((DEVICES, lanes), 0) == (iota((DEVICES, lanes), 1) >> 4)))
    mine = (iota((CAP, lanes), 1) & 7) == iota((CAP, lanes), 0)
    code = jnp.sum(jnp.where(mine, codes, 0.0), axis=0, keepdims=True).astype(jnp.int32)
    code = jnp.where(code > 0, code - 1 + nodes * ((iota((1, lanes), 1) >> 3) & 1), -1)
    members = (iota((2 * nodes, lanes), 0) == code).astype(F32)
    divisor = jnp.maximum(jnp.sum(members[:nodes, :], axis=1, keepdims=True), 1.0)
    members = members.astype(BF16)
    await_bytes(recv, recv_sem)
    sums = dot(members, recv[...])
    totals = jnp.concatenate([sums[:nodes, :], sums[nodes:, :]], axis=1)
    latent = embed_ref[...].astype(F32) + totals / divisor
    latent_ref[...] = latent
    centered = latent - jnp.mean(latent, axis=1, keepdims=True)
    inverse_std = lax.rsqrt(jnp.mean(centered * centered, axis=1, keepdims=True) + EPS)
    halo[block_rows(OWN), :] = (centered * inverse_std * gain_ref[...]).astype(BF16)
    mine = halo.at[block_rows(OWN)]
    for n, (sign, place) in enumerate(above(lat, lon)):
        send_to(
            mine, halo.at[block_rows(cell(-sign, 0))], halo_send_sem.at[n], halo_recv_sem.at[n], place
        )
    for sign, place in beside(lat, lon):
        send_to(mine, halo.at[block_rows(cell(0, -sign))], halo_send_sem.at[2], halo_recv_sem.at[2], place)

    own = halo[block_rows(OWN), :]
    own_t = turned(own)
    blocks_of(q_blocks, turned(dot(own, w_qkv_ref[:, :width]).astype(BF16)))

    def take(c):
        rows = block_rows(c)
        block = halo[rows, :]
        keys[rows, :] = dot(block, w_qkv_ref[:, width:2 * width]).astype(BF16)
        values[rows, :] = dot(block, w_qkv_ref[:, 2 * width:]).astype(BF16)
        halo_t[:, rows] = turned(block)
        for g in range(GROUPS):
            s = dot(keys[rows, g * LANES:(g + 1) * LANES], q_blocks[g])
            scores[g, rows, :] = s
            tops[g, c:c + 1, :] = jnp.max(s, axis=0, keepdims=True) * (SCALE * TO_LOG2) + bias[c:c + 1, :]

    take(OWN)
    for n, (step, _) in enumerate(above(lat, lon)):
        block = halo.at[block_rows(cell(-step, 0))]
        await_bytes(block, halo_recv_sem.at[n])
        for sign, place in beside(lat, lon):
            send_to(
                block, halo.at[block_rows(cell(-step, -sign))],
                halo_send_sem.at[3], halo_recv_sem.at[3], place,
            )
    await_bytes(halo.at[pl.ds(0, 2 * BLOCK)], halo_recv_sem.at[2])
    for c in (1, 3, 5, 7):
        take(c)
    codes = dot(one_hot(iota((lanes, DEVICES), 1) == (iota((lanes, DEVICES), 0) >> 4)), ids.astype(BF16))
    mine = (iota((lanes, LANES), 0) & 7) == iota((lanes, LANES), 1)
    code = jnp.sum(jnp.where(mine, codes, 0.0), axis=1, keepdims=True).astype(jnp.int32)
    code = jnp.where(code > 0, code - 1 + nodes * ((iota((lanes, 1), 0) >> 3) & 1), -1)
    spread_ref[...] = one_hot(iota((lanes, 2 * nodes), 1) == code)

    await_bytes(halo.at[pl.ds(0, 4 * BLOCK)], halo_recv_sem.at[3])
    for c in (0, 2, 6, 8):
        take(c)

    def forward(g, carry):
        cols = slice(g * LANES, (g + 1) * LANES)
        highest = jnp.max(tops[g, 0:9, :], axis=0, keepdims=True)
        total = jnp.zeros((1, COLUMNS), F32)
        for c in range(9):
            part = slice(c * BLOCK, (c + 1) * BLOCK)
            w = jnp.exp2(scores[g, part, :] * (SCALE * TO_LOG2) - (highest - bias[c:c + 1, :]))
            total = total + jnp.sum(w, axis=0, keepdims=True)
            weights[g, part, :] = w.astype(BF16)
        inverse = 1.0 / total
        out_group = diagonal(dot_rows(values[:, cols], weights[g])) * spread_heads(inverse)
        attended_t[cols, :] = out_group.astype(BF16)
        product = out_group * diagonal(d_blocks[g].astype(F32))
        delta = jnp.concatenate(
            [
                jnp.sum(product[h * HEAD_SIZE:(h + 1) * HEAD_SIZE, :], axis=0, keepdims=True)
                for h in range(GROUP_HEADS)
            ],
            axis=1,
        )
        inverses[g] = jnp.broadcast_to(inverse, (8, COLUMNS))
        deltas[g] = jnp.broadcast_to(delta, (8, COLUMNS))
        return carry

    for g in range(GROUPS):
        forward(g, 0)
    grad_w_out = dot(attended_t[...], cot).astype(BF16)
    for g in range(GROUPS):
        grads[4 * g + 3] = grad_w_out[:, g * LANES:(g + 1) * LANES]

    core = lon % 2
    twin = (lat, lon - core + (1 - core))
    core_rows = tile_rows(core, ROWS_CORE)
    places = {axis: place_on(axis, lat, lon) for axis in "xyz"}

    def group_units(g):
        return pl.ds(4 * g, 4)

    def others(axis):
        for k in range(1, 4):
            t = (places[axis] + k) % 4
            yield k - 1, t, moved_to(axis, t, lat, lon)

    def sum_core(g):
        send_to(
            grads.at[group_units(g), tile_rows(1 - core, ROWS_CORE)], from_core.at[group_units(g)],
            sum_send_sem.at[g, 0], sum_recv_sem.at[g, 0], twin,
        )

    def add_core(g):
        units = group_units(g)
        await_bytes(from_core.at[units], sum_recv_sem.at[g, 0])
        held_0[units] = (grads[units, core_rows, :].astype(F32) + from_core[units].astype(F32)).astype(BF16)

    def sum_1(g):
        add_core(g)
        units = group_units(g)
        for k, t, place in others(FIRST_AXES[g]):
            send_to(
                held_0.at[units, tile_rows(t, ROWS_1)], from_1.at[units, pl.ds(k * ROWS_1, ROWS_1)],
                sum_send_sem.at[g, 1], sum_recv_sem.at[g, 1], place,
            )

    def plane_index(g):
        b, c = (axis for axis in "xyz" if axis != FIRST_AXES[g])
        return places[b] * 4 + places[c]

    def plane_place(g, j):
        b, c = (axis for axis in "xyz" if axis != FIRST_AXES[g])
        return moved_to(c, j % 4, *moved_to(b, j // 4, lat, lon))

    def sum_plane(g):
        units = group_units(g)
        await_bytes(from_1.at[units], sum_recv_sem.at[g, 1])
        total = held_0[units, tile_rows(places[FIRST_AXES[g]], ROWS_1), :].astype(F32)
        for k in range(3):
            total = total + from_1[units, pl.ds(k * ROWS_1, ROWS_1), :].astype(F32)
        held_1[units] = total.astype(BF16)
        mine = plane_index(g)

        def push_piece(k, carry):
            j = (mine + k) % 16
            send_to(
                held_1.at[4 * g + j // 4, tile_rows(j % 4, ROWS_2)], from_plane.at[g, mine],
                sum_send_sem.at[g, 2], sum_recv_sem.at[g, 2], plane_place(g, j),
            )
            return carry

        lax.fori_loop(1, 16, push_piece, 0)
        from_plane[g, mine] = held_1[4 * g + mine // 4, tile_rows(mine % 4, ROWS_2), :]

    def back_plane(g):
        await_bytes(from_plane.at[g, pl.ds(0, 15)], sum_recv_sem.at[g, 2])
        mine = plane_index(g)
        row = core * ROWS_CORE + places[FIRST_AXES[g]] * ROWS_1 + (mine % 4) * ROWS_2
        piece = reduced_ref.at[4 * g + mine // 4, pl.ds(pl.multiple_of(row, ROWS_2), ROWS_2)]
        piece[...] = jnp.sum(from_plane[g].astype(F32), axis=0).astype(BF16)

        def push_sum(k, carry):
            send_to(
                piece, piece, sum_send_sem.at[g, 3], sum_recv_sem.at[g, 3],
                plane_place(g, (mine + k) % 16),
            )
            return carry

        lax.fori_loop(1, 16, push_sum, 0)

    def back_1(g):
        await_bytes(from_plane.at[g, pl.ds(0, 15)], sum_recv_sem.at[g, 3])
        row = core * ROWS_CORE + places[FIRST_AXES[g]] * ROWS_1
        piece = reduced_ref.at[group_units(g), pl.ds(pl.multiple_of(row, ROWS_1), ROWS_1)]
        for k, t, place in others(FIRST_AXES[g]):
            send_to(piece, piece, sum_send_sem.at[g, 4], sum_recv_sem.at[g, 4], place)

    def back_core(g):
        await_bytes(from_1.at[group_units(g)], sum_recv_sem.at[g, 4])
        piece = reduced_ref.at[group_units(g), core_rows]
        send_to(piece, piece, sum_send_sem.at[g, 5], sum_recv_sem.at[g, 5], twin)

    chip = places["x"] * 16 + places["y"] * 4 + places["z"]

    def place_of(i):
        x, y, z = i // 16, (i // 4) % 4, i % 4
        return (x % 2) * 4 + y, (x // 2) * 8 + z * 2 + core

    def piece_of(i):
        return i // 16, tile_rows(i % 16, ROWS_2)

    def scatter(g):
        add_core(g)

        def push_piece(k, carry):
            i = (chip + k) % CHIPS
            unit, rows = piece_of(i)
            send_to(
                held_0.at[4 * g + unit, rows], from_chips.at[chip],
                sum_send_sem.at[g, 1], sum_recv_sem.at[g, 1], place_of(i),
            )
            return carry

        lax.fori_loop(1, CHIPS, push_piece, 0)
        unit, rows = piece_of(chip)
        from_chips[chip] = held_0[4 * g + unit, rows, :]

    def gather(g):
        await_bytes(from_chips.at[pl.ds(0, CHIPS - 1)], sum_recv_sem.at[g, 1])
        total = jnp.sum(from_chips[...].astype(F32), axis=0)
        unit, rows = piece_of(chip)
        row = core * ROWS_CORE + (chip % 16) * ROWS_2
        piece = reduced_ref.at[4 * g + unit, pl.ds(pl.multiple_of(row, ROWS_2), ROWS_2)]
        piece[...] = total.astype(BF16)

        def push_sum(k, carry):
            send_to(
                piece, piece, sum_send_sem.at[g, 2], sum_recv_sem.at[g, 2], place_of((chip + k) % CHIPS)
            )
            return carry

        lax.fori_loop(1, CHIPS, push_sum, 0)

    def gather_core(g):
        await_bytes(from_chips.at[pl.ds(0, CHIPS - 1)], sum_recv_sem.at[g, 2])
        piece = reduced_ref.at[group_units(g), core_rows]
        send_to(piece, piece, sum_send_sem.at[g, 5], sum_recv_sem.at[g, 5], twin)

    def sum_end(g):
        units = group_units(g)
        await_bytes(from_core.at[units], sum_recv_sem.at[g, 5])
        await_bytes(from_core.at[units], sum_send_sem.at[g, 0])
        await_bytes(from_core.at[units], sum_send_sem.at[g, 5])
        if g < len(FIRST_AXES):
            await_bytes(from_1.at[units], sum_send_sem.at[g, 1])
            await_bytes(from_plane.at[g, pl.ds(0, 15)], sum_send_sem.at[g, 2])
            await_bytes(from_plane.at[g, pl.ds(0, 15)], sum_send_sem.at[g, 3])
            await_bytes(from_1.at[units], sum_send_sem.at[g, 4])
        else:
            for level in (1, 2):
                await_bytes(from_chips.at[pl.ds(0, CHIPS - 1)], sum_send_sem.at[g, level])

    def weight_grads(g):
        cols = slice(g * LANES, (g + 1) * LANES)
        v_cols = slice(width + g * LANES, width + (g + 1) * LANES)
        grads[4 * g] = dot_cols(own_t, d_query_t[cols, :]).astype(BF16)
        both = jnp.concatenate([d_keyvals[:, cols], d_keyvals[:, v_cols]], axis=1)
        both = dot(halo_t[...], both).astype(BF16)
        grads[4 * g + 1] = both[:, :LANES]
        grads[4 * g + 2] = both[:, LANES:]

    for g in range(GROUPS):
        cols = slice(g * LANES, (g + 1) * LANES)
        q_block, d_block = q_blocks[g].astype(F32), d_blocks[g]
        inverse, delta = inverses[g, 0:1, :], deltas[g, 0:1, :]
        d_scaled = (d_block.astype(F32) * inverse).astype(BF16)
        d_values = dot_cols(weights[g], d_scaled).astype(BF16)
        d_keyvals[:, width + g * LANES:width + (g + 1) * LANES] = d_values
        if g > 0:
            sum_1(g - 1)
        for c in range(9):
            part = slice(c * BLOCK, (c + 1) * BLOCK)
            d = dot(values[part, cols], d_block)
            weights[g, part, :] = (weights[g, part, :].astype(F32) * (d - delta)).astype(BF16)
        back = inverse * SCALE
        d_keys = dot_cols(weights[g], (q_block * back).astype(BF16)).astype(BF16)
        d_keyvals[:, cols] = d_keys
        d_query = (diagonal(dot_rows(keys[:, cols], weights[g])) * spread_heads(back)).astype(BF16)
        d_query_t[cols, :] = d_query
        if g < GROUPS - 1:
            weight_grads(g)
            sum_core(g)

    def node_part(c):
        return dot(d_keyvals[block_rows(c), :], w_t[...])

    for lat_step in (-1, 1, 0):
        for n, (sign, place) in enumerate(beside(lat, lon)):
            slot_rows = pl.ds((2 * (lat_step % 3) + n) * BLOCK, BLOCK)
            parts[slot_rows, :] = node_part(cell(lat_step, sign)).astype(BF16)
            send_to(
                parts.at[slot_rows], from_around.at[slot_rows],
                parts_send_sem.at[lat_step % 3], parts_recv_sem.at[lat_step % 3], place,
            )
    weight_grads(3)
    sum_core(3)
    sum_plane(0)
    sum_plane(1)
    scatter(3)
    d_normed = node_part(OWN) + dot_cols(turned(d_query_t[...]), w_qkv_ref[:, :width])
    mixed_ref[...] = (latent_ref[...] + dot_rows(attended_t[...], w_out_ref[...])).astype(BF16)
    latent = latent_ref[...]
    centered = latent - jnp.mean(latent, axis=1, keepdims=True)
    inverse_std = lax.rsqrt(jnp.mean(centered * centered, axis=1, keepdims=True) + EPS)
    normalized = centered * inverse_std
    sum_plane(2)
    for n, (sign, place) in enumerate(above(lat, lon)):
        at = sign % 3
        part = node_part(cell(sign, 0))
        arrived = from_around.at[pl.ds(2 * at * BLOCK, 2 * BLOCK)]
        await_bytes(arrived, parts_recv_sem.at[at])
        part = part + arrived[:BLOCK, :].astype(F32) + arrived[BLOCK:, :].astype(F32)
        slot_rows = pl.ds((6 + n) * BLOCK, BLOCK)
        parts[slot_rows, :] = part.astype(BF16)
        send_to(
            parts.at[slot_rows], from_around.at[slot_rows], parts_send_sem.at[3], parts_recv_sem.at[3], place
        )
    for g in range(3):
        back_plane(g)
    gather(3)
    await_bytes(from_around.at[pl.ds(0, 2 * BLOCK)], parts_recv_sem.at[0])
    await_bytes(from_around.at[pl.ds(6 * BLOCK, 2 * BLOCK)], parts_recv_sem.at[3])
    for n in (0, 1, 6, 7):
        d_normed = d_normed + from_around[block_rows(n), :].astype(F32)
    scaled = d_normed * gain_ref[...]
    d_latent = cot.astype(F32) + inverse_std * (
        scaled
        - jnp.mean(scaled, axis=1, keepdims=True)
        - normalized * jnp.mean(scaled * normalized, axis=1, keepdims=True)
    )
    node_grad = (d_latent / divisor).astype(BF16)
    stacked = jnp.concatenate([node_grad[:, :half], node_grad[:, half:]], axis=0)

    await_bytes(send.at[pl.ds(0, (DEVICES - 1) * 2 * CAP)], send_sem)
    send[...] = dot(spread_ref[...], stacked).astype(BF16)

    def push_back(step, carry):
        other = (me + 53 * step) % DEVICES
        send_to(
            send.at[tile_rows(other, 2 * CAP)], returned_ref.at[tile_rows(me, 2 * CAP)],
            back_send_sem, back_recv_sem, (other // LON, other % LON),
        )
        return carry

    lax.fori_loop(1, 64, push_back, 0)
    for g in range(3):
        back_1(g)
    lax.fori_loop(64, DEVICES, push_back, 0)
    pltpu.make_async_copy(
        send.at[tile_rows(me, 2 * CAP)], returned_ref.at[tile_rows(me, 2 * CAP)], back_recv_sem
    ).start()
    gather_core(3)
    for g in range(3):
        back_core(g)
    stores = [
        pltpu.make_async_copy(mixed_ref, mixed_out, store_sem.at[0]),
        pltpu.make_async_copy(flat_ref, flat_out, store_sem.at[1]),
    ]
    for g in range(GROUPS):
        sum_end(g)
        units = group_units(g)
        stores.append(
            pltpu.make_async_copy(reduced_ref.at[units], reduced_out.at[units], store_sem.at[2 + g])
        )
    for store in stores:
        store.start()
    await_bytes(ids_send.at[pl.ds(0, DEVICES - 1)], ids_send_sem)
    for n, blocks in enumerate((1, 1, 2, 4)):
        await_bytes(halo.at[pl.ds(0, blocks * BLOCK)], halo_send_sem.at[n])
    for n in range(4):
        await_bytes(parts.at[pl.ds(0, 2 * BLOCK)], parts_send_sem.at[n])
    await_bytes(send.at[pl.ds(0, (DEVICES - 1) * 2 * CAP)], back_send_sem)
    for store in stores:
        store.wait()
    await_bytes(returned_ref, back_recv_sem)


def sublayer(grid_rows, owner, node, embed, listed, gain, w_qkv, w_out, cotangent):
    count, width = grid_rows.shape
    nodes = embed.shape[0]
    lanes = 2 * DEVICES * CAP
    pool = 9 * nodes
    units, early = 4 * GROUPS, 4 * len(FIRST_AXES)
    vmem, dma = pltpu.VMEM, pltpu.SemaphoreType.DMA
    return pl.pallas_call(
        sublayer_kernel,
        name="sublayer",
        out_shape=(
            jax.ShapeDtypeStruct((nodes, width), BF16),
            jax.ShapeDtypeStruct((units, width, LANES), BF16),
            jax.ShapeDtypeStruct((lanes, width // 2), BF16),
            jax.ShapeDtypeStruct((count, LANES), jnp.int32),
        ),
        in_specs=[pl.BlockSpec(memory_space=vmem)] * 4 + [pl.BlockSpec(memory_space=pl.ANY)] * 5,
        out_specs=[pl.BlockSpec(memory_space=vmem if i == 2 else pl.ANY) for i in range(4)],
        scratch_shapes=[
            vmem((nodes, width), BF16),
            vmem((units, width, LANES), BF16),
            vmem((count, LANES), jnp.int32),
            vmem((count, width), BF16),
            vmem((nodes, width), BF16),
            vmem(w_qkv.shape, BF16),
            vmem(w_out.shape, BF16),
            vmem((nodes, width), BF16),
            vmem((lanes, width // 2), BF16),
            vmem((lanes, width // 2), BF16),
            vmem((DEVICES, 1, LANES), F32),
            vmem((DEVICES, 1, LANES), F32),
            vmem((2 * width, width), BF16),
            vmem((pool, width), BF16),
            vmem((width, pool), BF16),
            vmem((nodes, width), F32),
            vmem((lanes, 2 * nodes), BF16),
            vmem((pool, width), BF16),
            vmem((pool, width), BF16),
            vmem((GROUPS, LANES, COLUMNS), BF16),
            vmem((GROUPS, LANES, COLUMNS), BF16),
            vmem((GROUPS, pool, COLUMNS), F32),
            vmem((GROUPS, 16, COLUMNS), F32),
            vmem((GROUPS, pool, COLUMNS), BF16),
            vmem((GROUPS, 8, COLUMNS), F32),
            vmem((GROUPS, 8, COLUMNS), F32),
            vmem((pool, 2 * width), BF16),
            vmem((width, BLOCK), BF16),
            vmem((width, BLOCK), BF16),
            vmem((units, width, LANES), BF16),
            vmem((units, ROWS_CORE, LANES), BF16),
            vmem((units, ROWS_CORE, LANES), BF16),
            vmem((early, 3 * ROWS_1, LANES), BF16),
            vmem((early, ROWS_1, LANES), BF16),
            vmem((len(FIRST_AXES), 16, ROWS_2, LANES), BF16),
            vmem((CHIPS, ROWS_2, LANES), BF16),
            vmem((8 * nodes, width), BF16),
            vmem((8 * nodes, width), BF16),
            dma((5,)),
            dma((2 + GROUPS,)),
        ] + [dma] * 4 + [dma((4,))] * 2 + [dma((GROUPS, 6))] * 2 + [dma((4,))] * 2 + [dma] * 2,
        compiler_params=pltpu.CompilerParams(
            collective_id=0, has_side_effects=True, vmem_limit_bytes=VMEM_LIMIT
        ),
    )(
        owner.reshape(1, count), node.reshape(1, count), listed, gain.reshape(1, width),
        grid_rows, embed, w_qkv, w_out, cotangent,
    )


def finish_kernel(
    reduced_ref, returned_ref, flat_ref, w_qkv_ref, gain_ref, mixed_in_ref,
    mixed_ref, grad_grid_ref, grad_w_qkv_ref, grad_w_out_ref, grad_gain_ref,
):
    count, width = grad_grid_ref.shape
    half = width // 2
    slots = DEVICES * CAP
    mixed_ref[...] = mixed_in_ref[...]
    product = jnp.zeros((width, LANES), F32)
    for g in range(GROUPS):
        for m in range(3):
            cols = slice(m * width + g * LANES, m * width + (g + 1) * LANES)
            grad = reduced_ref[4 * g + m].astype(F32)
            grad_w_qkv_ref[:, cols] = grad
            product = product + grad * w_qkv_ref[:, cols].astype(F32)
        grad_w_out_ref[:, g * LANES:(g + 1) * LANES] = reduced_ref[4 * g + 3].astype(F32)
    grad_gain_ref[...] = jnp.sum(product.T, axis=0, keepdims=True) / gain_ref[...]
    back = returned_ref[...].astype(F32).reshape(DEVICES, 2 * CAP, half)
    back = jnp.concatenate([back[:, :CAP, :], back[:, CAP:, :]], axis=2)
    back = back.reshape(slots, width).astype(BF16)
    chosen = one_hot(iota((count, slots), 1) == flat_ref[:, 0:1])
    grad_grid_ref[...] = dot(chosen, back).astype(BF16)


def finish(reduced, returned, flat, w_qkv, gain, mixed):
    width = w_qkv.shape[0]
    count = flat.shape[0]
    return pl.pallas_call(
        finish_kernel,
        name="finish",
        out_shape=(
            jax.ShapeDtypeStruct(mixed.shape, BF16),
            jax.ShapeDtypeStruct((count, width), BF16),
            jax.ShapeDtypeStruct((width, 3 * width), F32),
            jax.ShapeDtypeStruct((width, width), F32),
            jax.ShapeDtypeStruct((1, width), F32),
        ),
        in_specs=[pl.BlockSpec(memory_space=pltpu.VMEM)] * 6,
        out_specs=[pl.BlockSpec(memory_space=pltpu.VMEM)] * 5,
        compiler_params=pltpu.CompilerParams(vmem_limit_bytes=VMEM_LIMIT),
    )(reduced, returned, flat, w_qkv, gain.reshape(1, width), mixed)


def local(
    grid_rows, dest_owner, dest_node, node_embed, neighbours, norm_gain, w_qkv, w_out, cotangent
):
    mixed, reduced, returned, flat = sublayer(
        grid_rows, dest_owner, dest_node, node_embed, neighbours, norm_gain, w_qkv, w_out, cotangent
    )
    mixed, grad_grid, grad_w_qkv, grad_w_out, grad_gain = finish(
        reduced, returned, flat, w_qkv, norm_gain, mixed
    )
    return (mixed, grad_grid, grad_w_qkv, grad_w_out, grad_gain.reshape(norm_gain.shape))


def solution(mesh):
    split = P(("lat", "lon"), None)
    in_specs = (split, split, P(("lat", "lon")), split, split, P(), P(), P(), split)
    out_specs = (split, split, P(), P(), P())
    return jax.shard_map(local, mesh=mesh, in_specs=in_specs, out_specs=out_specs, check_vma=False)
```
